256 devices in a mesh: tm: 4 (over y), rows: 64 (over z, x, core).
Axes of the slice: x: 4, y: 4, z: 8, core: 2. Of those that a mesh axis runs over, the one named last changes fastest.
Arguments:
- latents: bfloat16 [8, 512, 48, 384], P('tm', 'rows'), may hold values from -27 to 27
- gain_first: float32 [384], replicated, may hold values from 0.1 to 1.9
- kernel_first: bfloat16 [3, 3, 3, 384, 192], replicated, may hold values from -0.0625 to 0.0625
- gain_second: float32 [192], replicated, may hold values from 0.1 to 1.9
- kernel_second: bfloat16 [3, 3, 3, 192, 192], replicated, may hold values from -0.078125 to 0.078125
- shortcut: bfloat16 [384, 192], replicated, may hold values from -0.3125 to 0.3125
- gain_third: float32 [192], replicated, may hold values from 0.1 to 1.9
- kernel_third: bfloat16 [3, 3, 3, 192, 192], replicated, may hold values from -0.078125 to 0.078125
Outputs:
- block_out: bfloat16 [8, 512, 48, 192], P('tm', 'rows')
- decoded: bfloat16 [8, 1024, 96, 192], P('tm', 'rows')
The draws below stay inside these ranges and needn't reach their ends.
All inputs are finite; a program needn't handle non-finite values.
Results may differ from the reference program's by a relative error of at most 0.015.
Values may be sent and summed in bfloat16 or wider, within the bound.
No kernel may reach another device: no remote copies, remote signals or barrier semaphores. Data moves between devices by JAX's collectives and lax.ppermute only.
A program may use at most 128 MiB of HBM per device.

```python
import math
import jax
import jax.numpy as jnp
from jax import lax

C_IN = 384
C_OUT = 192
WIDTH = 48
FRAMES = 8
HEIGHT = 512


def draw_latents(key, part):
    key = jax.random.fold_in(key, 11)
    keys = jax.random.split(key, 3)
    shape = (FRAMES, HEIGHT, WIDTH, C_IN)
    base = jax.random.truncated_normal(keys[0], -3.0, 3.0, shape, jnp.float32)
    lowest = 0.3
    pixel = jnp.exp(jax.random.uniform(keys[1], (FRAMES, HEIGHT, WIDTH, 1), jnp.float32, math.log(lowest), math.log(3.0)))
    channel = jnp.exp(jax.random.uniform(keys[2], (1, 1, 1, C_IN), jnp.float32, math.log(0.3), math.log(3.0)))
    return (base * pixel * channel).astype(jnp.bfloat16)


def gaussian(stream_key, dims, deviation, bound, held_as=jnp.bfloat16):
    return jnp.clip(deviation * jax.random.normal(stream_key, dims, jnp.float32), -bound, bound).astype(held_as)


def setup_inputs(seed: int = 0) -> dict:
    key_of = jax.random.split(jax.random.key(seed), 9)
    latents = draw_latents(jax.random.fold_in(key_of[8], 71), 0)
    gain_first = jnp.clip(1.0 + 0.18 * jax.random.normal(key_of[1], (C_IN,), jnp.float32), 0.1, 1.9)
    kernel_first = gaussian(key_of[2], (3, 3, 3, C_IN, C_OUT), (27 * C_IN) ** -0.5, 0.0625)
    gain_second = jnp.clip(1.0 + 0.18 * jax.random.normal(key_of[3], (C_OUT,), jnp.float32), 0.1, 1.9)
    kernel_second = gaussian(key_of[4], (3, 3, 3, C_OUT, C_OUT), (27 * C_OUT) ** -0.5, 0.078125)
    shortcut = gaussian(key_of[5], (C_IN, C_OUT), C_IN ** -0.5, 0.3125)
    gain_third = jnp.clip(1.0 + 0.18 * jax.random.normal(key_of[6], (C_OUT,), jnp.float32), 0.1, 1.9)
    kernel_third = gaussian(key_of[7], (3, 3, 3, C_OUT, C_OUT), (27 * C_OUT) ** -0.5, 0.078125)
    return {"latents": latents, "gain_first": gain_first, "kernel_first": kernel_first, "gain_second": gain_second, "kernel_second": kernel_second, "shortcut": shortcut, "gain_third": gain_third, "kernel_third": kernel_third}


def activate(values, scales):
    wide_values = values.astype(jnp.float32)
    mean_square = lax.optimization_barrier(jnp.mean(wide_values * wide_values, axis=-1, keepdims=True))
    return jax.nn.silu(wide_values * lax.rsqrt(mean_square + 1e-06) * scales).astype(jnp.bfloat16)

def causal_convolve(active, kernel):
    frames = active.shape[0]
    height = active.shape[1]
    breadth = active.shape[2]
    padded = jnp.pad(active.astype(jnp.float32), ((2, 0), (1, 1), (1, 1), (0, 0)))
    weights = kernel.astype(jnp.float32)
    outputs = []
    for instant in range(frames):
        summed = jnp.zeros((height, breadth, kernel.shape[4]), jnp.float32)
        for offset_time in range(3):
            for offset_row in range(3):
                for offset_col in range(3):
                    window = padded[instant + offset_time, offset_row:offset_row + height, offset_col:offset_col + breadth]
                    summed = summed + jnp.einsum('hwc,co->hwo', window, weights[offset_time, offset_row, offset_col], precision=lax.Precision.HIGHEST)
        outputs.append(summed)
    return jnp.stack(outputs)

def reference(latents, gain_first, kernel_first, gain_second, kernel_second, shortcut, gain_third, kernel_third):
    normed_in = activate(latents, gain_first)
    first_out = causal_convolve(normed_in, kernel_first).astype(jnp.bfloat16)
    second_in = activate(first_out, gain_second)
    second_out = causal_convolve(second_in, kernel_second)
    skipped = jnp.einsum('fhwc,co->fhwo', latents.astype(jnp.float32), shortcut.astype(jnp.float32), precision=lax.Precision.HIGHEST)
    block_out = (skipped + second_out).astype(jnp.bfloat16)
    third_in = activate(block_out, gain_third)
    widened = jnp.repeat(jnp.repeat(third_in, 2, axis=1), 2, axis=2)
    decoded = causal_convolve(widened, kernel_third).astype(jnp.bfloat16)
    return (block_out, decoded)
```

```python
import jax
import jax.numpy as jnp
from jax import lax
from jax.experimental import pallas as pl
from jax.experimental.pallas import tpu as pltpu
from jax.sharding import PartitionSpec as P

F32 = jnp.float32
BF16 = jnp.bfloat16
HALO = 3


def dot(a, b):
    return jnp.dot(a, b, preferred_element_type=F32)


def normed(v, gain):
    mean_square = jnp.mean(v * v, axis=-1, keepdims=True)
    u = v * lax.rsqrt(mean_square + 1e-06) * gain
    return u * (0.5 + 0.5 * jnp.tanh(0.5 * u))


def beside(v):
    width = v.shape[0]
    column = lax.broadcasted_iota(jnp.int32, v.shape, 0)
    left = jnp.where(column == 0, 0.0, pltpu.roll(v, 1, 0))
    right = jnp.where(column == width - 1, 0.0, pltpu.roll(v, width - 1, 0))
    return left, right


def call(kernel, out_shape, scratch, flops, nbytes, limit, *args):
    smem = pl.BlockSpec(memory_space=pltpu.SMEM)
    vmem = pl.BlockSpec(memory_space=pltpu.VMEM)
    return pl.pallas_call(
        kernel,
        out_shape=out_shape,
        in_specs=[smem] + [vmem] * (len(args) - 1),
        out_specs=jax.tree.map(lambda _: vmem, out_shape),
        scratch_shapes=scratch,
        compiler_params=pltpu.CompilerParams(vmem_limit_bytes=limit << 20),
        cost_estimate=pl.CostEstimate(flops=flops, bytes_accessed=nbytes, transcendentals=0),
    )(*args)


def pack_rows(ref, value):
    half = value.shape[1] // 2
    ref[:, :, :, 0:192] = value[:, :half].astype(BF16)
    ref[:, :, :, 192:384] = value[:, half:].astype(BF16)


def first_kernel(place, latents, near, far, gain, kernel, partial, cols, acc):
    frames, rows, width, channels = latents.shape
    tall = rows + 2 * HALO
    odd = place[1] % 2
    inner = jnp.logical_and(place[1] > 0, place[1] < place[3] - 1)

    def put(frame, row, values):
        v = normed(values.astype(F32), gain[...])
        left, right = beside(v)
        cols[frame, row, :, 0:channels] = left.astype(BF16)
        cols[frame, row, :, channels : 2 * channels] = v.astype(BF16)
        cols[frame, row, :, 2 * channels : 3 * channels] = right.astype(BF16)

    for frame in range(frames):
        @pl.loop(0, rows)
        def _(row):
            put(frame, row + HALO, latents[frame, row])

        @pl.loop(0, HALO)
        def _(row):
            put(frame, jnp.where(odd == 1, 0, tall - HALO) + row, near[frame, row])
            values = far[frame, row]
            put(
                frame,
                jnp.where(odd == 1, tall - HALO, 0) + row,
                jnp.where(inner, values, jnp.zeros_like(values)),
            )

    wide = tall - 2
    pixels = wide * width

    @pl.loop(0, 3)
    def _(b):
        window = cols[:, pl.ds(b, wide)].reshape(2 * pixels, 3 * channels)
        first = dot(window, kernel[0, b])
        second = dot(window[pixels:], kernel[1, b])

        @pl.when(b == 0)
        def _():
            acc[0] = first[:pixels] + second
            acc[1] = first[pixels:]

        @pl.when(b > 0)
        def _():
            acc[0] += first[:pixels] + second
            acc[1] += first[pixels:]

    pack_rows(partial, acc[...].reshape(2, wide, width, 192))


def first_own_kernel(place, cols, kernel, own):
    wide = cols.shape[1] - 2
    width = cols.shape[2]
    pixels = wide * width

    @pl.loop(0, 3)
    def _(b):
        window = cols[:, pl.ds(b, wide)].reshape(2 * pixels, cols.shape[3])
        last = dot(window, kernel[2, b])
        middle = dot(window[:pixels], kernel[1, b])

        @pl.when(b == 0)
        def _():
            own[0] = last[:pixels]
            own[1] = last[pixels:] + middle

        @pl.when(b > 0)
        def _():
            own[0] += last[:pixels]
            own[1] += last[pixels:] + middle


def three(window, kernel, a, b):
    total = dot(window[0], kernel[a, b, 0])
    total += dot(window[1], kernel[a, b, 1])
    return total + dot(window[2], kernel[a, b, 2])


def second_kernel(place, own, before, gain, kernel, partial, cols, acc):
    frames = own.shape[0]
    half, width = before.shape[1], before.shape[2]
    tall = 2 * half
    beyond = (tall - 8) // 2
    start = place[1] * 8 - beyond
    follows = place[0] > 0

    for frame in range(frames):
        @pl.loop(0, half)
        def _(row):
            pair = before[frame, row].astype(F32)
            for side in range(2):
                at = row + side * half
                earlier = jnp.where(follows, pair[:, 192 * side : 192 * side + 192], 0.0)
                first_out = (own[frame, pl.ds(at * width, width)] + earlier).astype(BF16)
                inside = jnp.logical_and(start + at >= 0, start + at < place[3] * 8)
                v = jnp.where(inside, normed(first_out.astype(F32), gain[...]), 0.0)
                left, right = beside(v)
                cols[0, frame, at] = left.astype(BF16)
                cols[1, frame, at] = v.astype(BF16)
                cols[2, frame, at] = right.astype(BF16)

    wide = tall - 2
    pixels = wide * width

    @pl.loop(0, 3)
    def _(b):
        window = [cols[e, :, pl.ds(b, wide)].reshape(2 * pixels, 192) for e in range(3)]
        first = three(window, kernel, 0, b)
        second = three([w[pixels:] for w in window], kernel, 1, b)

        @pl.when(b == 0)
        def _():
            acc[0] = first[:pixels] + second
            acc[1] = first[pixels:]

        @pl.when(b > 0)
        def _():
            acc[0] += first[:pixels] + second
            acc[1] += first[pixels:]

    pack_rows(partial, acc[...].reshape(2, wide, width, 192))


def second_own_kernel(place, cols, kernel, latents, near, far, shortcut, own):
    wide = cols.shape[2] - 2
    width = cols.shape[3]
    pixels = wide * width
    rows, channels = latents.shape[1], latents.shape[3]
    odd = place[1] % 2
    inner = wide - 1

    @pl.loop(0, 3)
    def _(b):
        window = [cols[e, :, pl.ds(b, wide)].reshape(2 * pixels, 192) for e in range(3)]
        last = three(window, kernel, 2, b)
        middle = three([w[:pixels] for w in window], kernel, 1, b)

        @pl.when(b == 0)
        def _():
            own[0] = last[:pixels]
            own[1] = last[pixels:] + middle

        @pl.when(b > 0)
        def _():
            own[0] += last[:pixels]
            own[1] += last[pixels:] + middle

    for frame in range(2):
        body = latents[frame].reshape(rows * width, channels)
        own[frame, width : pixels - width] += dot(body, shortcut[...])
        other = dot(near[frame, jnp.where(odd == 1, HALO - 1, 0)], shortcut[...])
        own[frame, pl.ds(jnp.where(odd == 1, 0, inner * width), width)] += other
        other = dot(far[frame, jnp.where(odd == 1, 0, HALO - 1)], shortcut[...])
        own[frame, pl.ds(jnp.where(odd == 1, inner * width, 0), width)] += other


def third_kernel(place, own, before, gain, block_out, packed, active):
    half, width = before.shape[1], before.shape[2]
    tall = 2 * half
    start = place[1] * 8 - 1
    follows = place[0] > 0
    for frame in range(2):
        for row in range(half):
            pair = before[frame, row].astype(F32)
            for side in range(2):
                at = row + side * half
                earlier = jnp.where(follows, pair[:, 192 * side : 192 * side + 192], 0.0)
                total = (own[frame, at * width : (at + 1) * width] + earlier).astype(BF16)
                if 0 < at < tall - 1:
                    block_out[frame, at - 1] = total
                v = normed(total.astype(F32), gain[...])
                if at in (0, tall - 1):
                    inside = jnp.logical_and(start + at >= 0, start + at < place[3] * 8)
                    v = jnp.where(inside, v, 0.0)
                v = v.astype(BF16)
                active[frame, at] = v
                packed[frame, row, :, 192 * side : 192 * side + 192] = v


def weights_kernel(place, kernel, out):
    for a in range(3):
        by_row = []
        for b in range(3):
            k = [kernel[a, b, e].astype(F32) for e in range(3)]
            by_row.append((-k[0], k[0] + k[1] + k[2], k[2]))
        for q in range(3):
            out[a, 0, q] = (-by_row[0][q]).astype(BF16)
            out[a, 1, q] = (by_row[0][q] + by_row[1][q] + by_row[2][q]).astype(BF16)
            out[a, 2, q] = by_row[2][q].astype(BF16)


def differences(get, level, steps, frame, tall):
    last = None
    for at in range(tall):
        v = get(at).astype(F32)
        left, right = beside(v)
        now = (v - left, v, right - v)
        for q in range(3):
            if 0 < at < tall - 1:
                level[q, frame, at - 1] = now[q].astype(BF16)
            if at > 0:
                steps[q, frame, at - 1] = (now[q] - last[q]).astype(BF16)
        last = now


def products(level, steps, kernel, taps, rows, width, p, q):
    total = None
    for frame, a in taps:
        if p == 1:
            window = level[q, frame]
        else:
            window = steps[q, frame, 0:rows] if p == 0 else steps[q, frame, 1 : rows + 1]
        term = dot(window.reshape(rows * width, 192), kernel[a, p, q])
        total = term if total is None else total + term
    return total


def phases(level, steps, kernel, taps, rows, width):
    by = []
    for q in range(3):
        m = [products(level, steps, kernel, taps, rows, width, p, q) for p in range(3)]
        by.append((m[1] + m[0], m[1] + m[2]))
    return [[by[1][i] + by[0][i], by[1][i] + by[2][i]] for i in range(2)]


def third_own_kernel(place, active, kernel, own, level, steps):
    rows, width = active.shape[1] - 2, active.shape[2]
    for frame in range(2):
        differences(lambda at: active[frame, at], level, steps, frame, rows + 2)
    for out, taps in ((0, ((0, 2),)), (1, ((0, 1), (1, 2)))):
        result = phases(level, steps, kernel, taps, rows, width)
        for i in range(2):
            for j in range(2):
                own[out, 2 * i + j] = result[i][j]


def last_kernel(place, packed, kernel, own, decoded, level, steps, woven):
    half, width = packed.shape[1], packed.shape[2]
    tall = 2 * half
    rows = tall - 2
    follows = place[0] > 0

    for frame in range(2):
        def get(at):
            side, row = divmod(at, half)
            v = packed[frame, row, :, 192 * side : 192 * side + 192]
            return jnp.where(follows, v, jnp.zeros_like(v))

        differences(get, level, steps, frame, tall)
    for out, taps in ((0, ((0, 0), (1, 1))), (1, ((1, 0),))):
        result = phases(level, steps, kernel, taps, rows, width)
        for i in range(2):
            for j in range(2):
                own[out, 2 * i + j] += result[i][j]

        @pl.loop(0, rows)
        def _(row):
            for i in range(2):
                for j in range(2):
                    value = own[out, 2 * i + j, pl.ds(row * width, width)]
                    woven[i, 0, pl.ds(j, width, stride=2)] = value[:, 0:128]
                    woven[i, 1, pl.ds(j, width, stride=2), 0:64] = value[:, 128:192]
                decoded[out, 2 * row + i, :, 0:128] = woven[i, 0].astype(BF16)
                decoded[out, 2 * row + i, :, 128:192] = woven[i, 1, :, 0:64].astype(BF16)


def onward(value):
    count = lax.axis_size("tm")
    return lax.ppermute(value, "tm", [(i, (i + 1) % count) for i in range(count)])


def swap(value, offset):
    count = lax.axis_size("rows")
    pairs = [((2 * i + offset) % count, (2 * i + 1 + offset) % count) for i in range(count // 2)]
    return lax.ppermute(value, "rows", pairs + [(b, a) for a, b in pairs])


def body(
    latents,
    gain_first,
    kernel_first,
    gain_second,
    kernel_second,
    shortcut,
    gain_third,
    kernel_third,
):
    frames, rows, width, channels = latents.shape
    group, slab = lax.axis_index("tm"), lax.axis_index("rows")
    place = jnp.stack(
        [group, slab, jnp.int32(lax.axis_size("tm")), jnp.int32(lax.axis_size("rows"))]
    ).astype(jnp.int32)
    odd = slab % 2
    near = swap(lax.dynamic_slice_in_dim(latents, (rows - HALO) * (1 - odd), HALO, 1), 0)
    far = swap(lax.dynamic_slice_in_dim(latents, (rows - HALO) * odd, HALO, 1), 1)

    shape = jax.ShapeDtypeStruct
    wide1, wide2 = rows + 4, rows + 2
    pixels1, pixels2 = wide1 * width, wide2 * width
    folded = kernel_first.reshape(3, 3, 3 * channels, 192)
    partial, cols = call(
        first_kernel,
        (shape((2, wide1 // 2, width, 384), BF16), shape((2, wide1 + 2, width, 3 * channels), BF16)),
        [pltpu.VMEM((2, pixels1, 192), F32)],
        6 * 9 * pixels1 * channels * 192,
        8 << 20,
        40,
        place, latents, near, far, gain_first.reshape(1, -1), folded,
    )
    before = onward(partial)
    own = call(
        first_own_kernel,
        shape((2, pixels1, 192), F32),
        [],
        6 * 9 * pixels1 * channels * 192,
        8 << 20,
        40,
        place, cols, folded,
    )
    mixed = call(
        weights_kernel, shape((3, 3, 3, 192, 192), BF16), [], 1 << 24, 4 << 20, 40, place, kernel_third
    )
    partial, cols = call(
        second_kernel,
        (shape((2, wide2 // 2, width, 384), BF16), shape((3, 2, wide1, width, 192), BF16)),
        [pltpu.VMEM((2, pixels2, 192), F32)],
        6 * 9 * pixels2 * 192 * 192,
        8 << 20,
        40,
        place, own, before, gain_second.reshape(1, -1), kernel_second,
    )
    before = onward(partial)
    own = call(
        second_own_kernel,
        shape((2, pixels2, 192), F32),
        [],
        6 * 9 * pixels2 * 192 * 192,
        8 << 20,
        40,
        place, cols, kernel_second, latents, near, far, shortcut,
    )
    block_out, packed, active = call(
        third_kernel,
        (
            shape((2, rows, width, 192), BF16),
            shape((2, wide2 // 2, width, 384), BF16),
            shape((2, wide2, width, 192), BF16),
        ),
        [],
        1 << 24,
        4 << 20,
        40,
        place, own, before, gain_third.reshape(1, -1),
    )
    before = onward(packed)
    scratch = [
        pltpu.VMEM((3, 2, rows, width, 192), BF16),
        pltpu.VMEM((3, 2, rows + 1, width, 192), BF16),
    ]
    own = call(
        third_own_kernel,
        shape((2, 4, rows * width, 192), F32),
        scratch,
        6 * 9 * rows * width * 192 * 192,
        8 << 20,
        40,
        place, active, mixed,
    )
    decoded = call(
        last_kernel,
        shape((2, 2 * rows, 2 * width, 192), BF16),
        scratch + [pltpu.VMEM((2, 2, 2 * width, 128), F32)],
        6 * 9 * rows * width * 192 * 192,
        8 << 20,
        40,
        place, before, mixed, own,
    )
    return (block_out, decoded)


def solution(mesh):
    return jax.shard_map(
        body,
        mesh=mesh,
        in_specs=(P("tm", "rows", None, None), P(), P(), P(), P(), P(), P(), P()),
        out_specs=(P("tm", "rows", None, None), P("tm", "rows", None, None)),
        check_vma=False,
    )
```

```python
import jax
import jax.numpy as jnp
from jax import lax
from jax.experimental import pallas as pl
from jax.experimental.pallas import tpu as pltpu
from jax.sharding import PartitionSpec as P

F32 = jnp.float32
BF16 = jnp.bfloat16
HALO = 3
LIMIT = 24


def dot(a, b):
    return jnp.dot(a, b, preferred_element_type=F32)


def dot_t(a, b):
    return lax.dot_general(a, b, (((1,), (1,)), ((), ())), preferred_element_type=F32)


def spans(channels):
    return [(at, min(128, channels - at)) for at in range(0, channels, 128)]


def scales(squares, channels):
    total = dot(squares, jnp.ones((channels, 128), BF16))
    return lax.rsqrt(total * (1.0 / channels) + 1e-06)


def activated(v, scale, gain):
    u = v * scale * gain
    return u * (0.5 + 0.5 * jnp.tanh(0.5 * u))


def column_masks(width, channels):
    column = lax.broadcasted_iota(jnp.int32, (width, channels), 0)
    return column == 0, column == width - 1


def beside(v, masks):
    width = v.shape[0]
    left = jnp.where(masks[0], 0.0, pltpu.roll(v, 1, 0))
    right = jnp.where(masks[1], 0.0, pltpu.roll(v, width - 1, 0))
    return left, right


def call(kernel, out_shape, scratch, flops, args, hbm=(), out_hbm=(), aliases=None):
    smem = pl.BlockSpec(memory_space=pltpu.SMEM)
    vmem = pl.BlockSpec(memory_space=pltpu.VMEM)
    far = pl.BlockSpec(memory_space=pltpu.HBM)
    in_specs = [smem] + [far if i in hbm else vmem for i in range(1, len(args))]
    args = [pltpu.with_memory_space_constraint(x, pltpu.HBM) if i in hbm else x for i, x in enumerate(args)]
    return pl.pallas_call(
        kernel,
        out_shape=out_shape,
        in_specs=in_specs,
        out_specs=tuple(far if i in out_hbm else vmem for i in range(len(out_shape))),
        scratch_shapes=scratch,
        input_output_aliases=aliases or {},
        compiler_params=pltpu.CompilerParams(vmem_limit_bytes=LIMIT << 20),
        cost_estimate=pl.CostEstimate(flops=flops, bytes_accessed=4 << 20, transcendentals=0),
    )(*args)


def pack_rows(ref, rows, get):
    half = rows // 2
    for row in range(half):
        upper, lower = get(row), get(row + half)
        ref[row] = upper[:, 0:128].astype(BF16)
        ref[row + half] = lower[:, 0:128].astype(BF16)
        ref[rows + row] = jnp.concatenate([upper[:, 128:192], lower[:, 128:192]], axis=1).astype(BF16)


def unpack_row(ref, row):
    half = ref.shape[0] // 3
    side, at = divmod(row, half)
    rest = ref[2 * half + at].astype(F32)
    return jnp.concatenate([ref[row].astype(F32), rest[:, 64 * side : 64 * side + 64]], axis=1)


def convolve(acc, product, kernel, terms, rows, width):
    masks = column_masks(width, 192)
    fields = [window(b) for window, a in terms for b in range(3)]
    if product is dot_t:
        fields = [jnp.concatenate(fields, axis=1)]
    for e in range(3):
        taps = [kernel[a, b, e] for window, a in terms for b in range(3)]
        if product is dot_t:
            taps = [jnp.concatenate(taps, axis=1)]
        total = None
        for field, tap in zip(fields, taps):
            term = product(field, tap)
            total = term if total is None else total + term
        for row in range(rows):
            part = slice(row * width, (row + 1) * width)
            moved = total[part]
            if e == 0:
                acc[part] = jnp.where(masks[0], 0.0, pltpu.roll(moved, 1, 0))
            elif e == 1:
                acc[part] += moved
            else:
                acc[part] += jnp.where(masks[1], 0.0, pltpu.roll(moved, width - 1, 0))


def windows(ref, rows):
    return lambda b: ref[b : b + rows].reshape(rows * ref.shape[1], ref.shape[2])


OWN = (((0, 2),), ((0, 1), (1, 2)))


def activate_rows(ref, gain, squares, scale, out):
    rows, width, channels = ref.shape
    pixels = rows * width
    v = ref[...].astype(F32)
    squares[0:pixels] = (v * v).astype(BF16).reshape(pixels, channels)
    scale[0:pixels] = scales(squares[0:pixels], channels)
    for row in range(rows):
        part = slice(row * width, (row + 1) * width)
        for at, lanes in spans(channels):
            out[row, :, at : at + lanes] = activated(
                ref[row, :, at : at + lanes].astype(F32), scale[part], gain[at : at + lanes].reshape(1, lanes)
            ).astype(BF16)


def inner_kernel(place, latents, gain, kernel, held, weights, active, sums, held_gain, squares, scale, sems):
    frames, rows, width, channels = held.shape
    copies = [
        pltpu.make_async_copy(latents.at[1], held.at[1], sems.at[0]),
        pltpu.make_async_copy(latents.at[0], held.at[0], sems.at[1]),
        pltpu.make_async_copy(kernel, weights, sems.at[2]),
        pltpu.make_async_copy(gain, held_gain, sems.at[3]),
    ]
    for copy in (copies[0], copies[3], copies[1], copies[2]):
        copy.start()
    copies[3].wait()
    for frame, copy in ((1, copies[0]), (0, copies[1])):
        copy.wait()
        activate_rows(held.at[frame], held_gain, squares, scale, active.at[frame])
    copies[2].wait()
    count = rows - 2
    convolve(sums.at[1], dot_t, weights, [(windows(active.at[1], count), 0)], count, width)
    convolve(
        sums.at[0],
        dot_t,
        weights,
        [(windows(active.at[0], count), 0), (windows(active.at[1], count), 1)],
        count,
        width,
    )


def fill_edges(place, near, far, frame, gain, active, edges, raw, squares, scale):
    odd = place[1] % 2 == 1
    inner = jnp.logical_and(place[1] > 0, place[1] < place[3] - 1)
    rows = active.shape[1]
    for row in range(HALO):
        chip = near[frame, row]
        next_chip = jnp.where(inner, far[frame, row], jnp.zeros_like(chip))
        raw[row] = jnp.where(odd, chip, next_chip)
        raw[HALO + row] = jnp.where(odd, next_chip, chip)
    activate_rows(raw.at[0:HALO], gain, squares, scale, edges.at[0, 0:HALO])
    activate_rows(raw.at[HALO : 2 * HALO], gain, squares, scale, edges.at[1, 2 : 2 + HALO])
    edges[0, HALO : HALO + 2] = active[frame, 0:2]
    edges[1, 0:2] = active[frame, rows - 2 : rows]


def edge_windows(edges):
    width, channels = edges.shape[2], edges.shape[3]
    return lambda b: edges[:, b : b + HALO].reshape(2 * HALO * width, channels)


def pack_joined(partial, sums, acc, wide, width):
    def get(row):
        if HALO <= row < wide - HALO:
            return sums[(row - HALO) * width : (row - HALO + 1) * width]
        at = row if row < HALO else row - (wide - 2 * HALO)
        return acc[at * width : (at + 1) * width]

    pack_rows(partial, wide, get)


def late_edge_kernel(
    place, near, far, gain, active, weights, sums, partial, edges, acc, raw, squares, scale
):
    fill_edges(place, near, far, 1, gain, active, edges, raw, squares, scale)
    width = active.shape[2]
    convolve(acc, dot_t, weights, [(edge_windows(edges), 0)], 2 * HALO, width)
    pack_joined(partial, sums.at[1], acc, active.shape[1] + 4, width)


def early_edge_kernel(
    place, near, far, gain, active, weights, sums, late, partial, tall, edges, acc, raw, squares, scale
):
    fill_edges(place, near, far, 0, gain, active, edges, raw, squares, scale)
    rows, width = active.shape[1], active.shape[2]
    convolve(acc, dot_t, weights, [(edge_windows(edges), 0), (edge_windows(late), 1)], 2 * HALO, width)
    pack_joined(partial, sums.at[0], acc, rows + 4, width)
    for frame, ends in ((0, edges), (1, late)):
        tall[frame, 0:HALO] = ends[0, 0:HALO]
        tall[frame, HALO : HALO + rows] = active[frame]
        tall[frame, HALO + rows :] = ends[1, 2:]


def first_own_kernel(place, active, kernel, own):
    wide, width = active.shape[1] - 2, active.shape[2]
    for out in (1, 0):
        terms = [(windows(active.at[frame], wide), a) for frame, a in OWN[out]]
        convolve(own.at[out], dot_t, kernel, terms, wide, width)


def finish(place, own, before, gain, raw, squares, scale, keep, out):
    tall, width = before.shape[0] * 2 // 3, before.shape[1]
    start = place[1] * 8 - (tall - 8) // 2
    follows = place[0] > 0
    for row in range(tall):
        part = slice(row * width, (row + 1) * width)
        earlier = jnp.where(follows, unpack_row(before, row), 0.0)
        total = (own[part] + earlier).astype(BF16)
        raw[part] = total
        keep(row, total)
        total = total.astype(F32)
        squares[part] = (total * total).astype(BF16)
    scale[...] = scales(squares[...], 192)

    def get(row):
        part = slice(row * width, (row + 1) * width)
        inside = jnp.logical_and(start + row >= 0, start + row < place[3] * 8)
        lanes = []
        for at, count in spans(192):
            v = activated(
                raw[part, at : at + count].astype(F32), scale[part, 0:count], gain[at : at + count].reshape(1, count)
            )
            if not (tall - 8) // 2 <= row < (tall + 8) // 2:
                v = jnp.where(inside, v, 0.0)
            lanes.append(v)
        v = jnp.concatenate(lanes, axis=1)
        out[row] = v.astype(BF16)
        return v

    return get


def late_second_kernel(
    place, own, before, gain, kernel, partial, active, raw, squares, scale, acc
):
    tall, width = active.shape[0], active.shape[1]
    get = finish(place, own.at[1], before, gain, raw, squares, scale, lambda row, total: None, active)
    for row in range(tall):
        get(row)
    wide = tall - 2
    convolve(acc, dot, kernel, [(windows(active, wide), 0)], wide, width)
    pack_rows(partial, wide, lambda row: acc[row * width : (row + 1) * width])


def early_second_kernel(
    place, own, before, gain, kernel, late, partial, active, raw, squares, scale, acc
):
    tall, width = active.shape[0], active.shape[1]
    get = finish(place, own.at[0], before, gain, raw, squares, scale, lambda row, total: None, active)
    for row in range(tall):
        get(row)
    wide = tall - 2
    convolve(acc, dot, kernel, [(windows(active, wide), 0), (windows(late, wide), 1)], wide, width)
    pack_rows(partial, wide, lambda row: acc[row * width : (row + 1) * width])


def second_own_kernel(place, early, late, kernel, latents, near, far, shortcut, own):
    wide, width = early.shape[0] - 2, early.shape[1]
    pixels = wide * width
    rows, channels = latents.shape[1], latents.shape[3]
    odd = place[1] % 2
    inner = wide - 1
    active = (early, late)
    for out in (1, 0):
        terms = [(windows(active[frame], wide), a) for frame, a in OWN[out]]
        convolve(own.at[out], dot, kernel, terms, wide, width)
        body = latents[out].reshape(rows * width, channels)
        own[out, width : pixels - width] += dot_t(body, shortcut[...])
        other = dot_t(near[out, jnp.where(odd == 1, HALO - 1, 0)], shortcut[...])
        own[out, pl.ds(jnp.where(odd == 1, 0, inner * width), width)] += other
        other = dot_t(far[out, jnp.where(odd == 1, 0, HALO - 1)], shortcut[...])
        own[out, pl.ds(jnp.where(odd == 1, inner * width, 0), width)] += other


def late_third_kernel(place, own, before, gain, block_out, packed, active, raw, squares, scale):
    tall = active.shape[0]

    def keep(row, total):
        if 0 < row < tall - 1:
            block_out[row - 1] = total

    pack_rows(packed, tall, finish(place, own.at[1], before, gain, raw, squares, scale, keep, active))


def early_third_kernel(place, own, before, gain, late_out, block_out, packed, active, raw, squares, scale):
    tall = active.shape[0]

    def keep(row, total):
        if 0 < row < tall - 1:
            block_out[0, row - 1] = total

    block_out[1] = late_out[...]
    pack_rows(packed, tall, finish(place, own.at[0], before, gain, raw, squares, scale, keep, active))


def weights_kernel(place, kernel, out):
    for a in range(3):
        by_row = []
        for b in range(3):
            k = [kernel[a, b, e].astype(F32) for e in range(3)]
            by_row.append((-k[0], k[0] + k[1] + k[2], k[2]))
        for q in range(3):
            out[a, 0, q] = (-by_row[0][q]).astype(BF16)
            out[a, 1, q] = (by_row[0][q] + by_row[1][q] + by_row[2][q]).astype(BF16)
            out[a, 2, q] = by_row[2][q].astype(BF16)


def differences(get, level, steps, tall, width):
    masks = column_masks(width, 192)
    last = None
    for at in range(tall):
        v = get(at).astype(F32)
        left, right = beside(v, masks)
        now = (v - left, v, right - v)
        for q in range(3):
            if 0 < at < tall - 1:
                level[q, at - 1] = now[q].astype(BF16)
            if at > 0:
                steps[q, at - 1] = (now[q] - last[q]).astype(BF16)
        last = now


def products(terms, kernel, rows, width, p, q):
    total = None
    for level, steps, a in terms:
        if p == 1:
            window = level[q]
        else:
            window = steps[q, 0:rows] if p == 0 else steps[q, 1 : rows + 1]
        term = dot(window.reshape(rows * width, 192), kernel[a, p, q])
        total = term if total is None else total + term
    return total


def phases(terms, kernel, rows, width):
    by = []
    for q in range(3):
        m = [products(terms, kernel, rows, width, p, q) for p in range(3)]
        by.append((m[1] + m[0], m[1] + m[2]))
    return [[by[1][i] + by[0][i], by[1][i] + by[2][i]] for i in range(2)]


def third_own_kernel(place, early, late, kernel, own, level, steps):
    rows, width = early.shape[0] - 2, early.shape[1]
    for frame, active in enumerate((early, late)):
        differences(lambda at: active[at], level.at[frame], steps.at[frame], rows + 2, width)
    for out, taps in enumerate(OWN):
        terms = [(level.at[frame], steps.at[frame], a) for frame, a in taps]
        result = phases(terms, kernel, rows, width)
        for i in range(2):
            for j in range(2):
                own[out, 2 * i + j] = result[i][j]


def weave(total, i, j, rows, width, woven):
    for row in range(rows):
        value = total[row * width : (row + 1) * width]
        woven[i, row, 0, pl.ds(j, width, stride=2)] = value[:, 0:128]
        woven[i, row, 1, pl.ds(j, width, stride=2), 0:64] = value[:, 128:192]


def weave_out(fine, i, rows, woven):
    for row in range(rows):
        fine[2 * row + i, :, 0:128] = woven[i, row, 0].astype(BF16)
        fine[2 * row + i, :, 128:192] = woven[i, row, 1, :, 0:64].astype(BF16)


def before_terms(place, packed, level, steps, a):
    tall, width = 2 * packed.shape[0] // 3, packed.shape[1]
    follows = place[0] > 0
    differences(lambda at: jnp.where(follows, unpack_row(packed, at), 0.0), level, steps, tall, width)
    return [(level, steps, a)]


def late_last_kernel(place, packed, kernel, own, decoded, rest, level, steps, woven, fine, sem):
    rows, width = 2 * packed.shape[0] // 3 - 2, packed.shape[1]
    terms = before_terms(place, packed, level, steps, 0)
    result = phases(terms, kernel, rows, width)
    for i in range(2):
        for j in range(2):
            weave(own[1, 2 * i + j] + result[i][j], i, j, rows, width, woven)
        weave_out(fine, i, rows, woven)
    copy = pltpu.make_async_copy(fine, decoded.at[1], sem)
    copy.start()
    result = phases([(level, steps, 1)], kernel, rows, width)
    for i in range(2):
        for j in range(2):
            rest[2 * i + j] = own[0, 2 * i + j] + result[i][j]
    copy.wait()


def early_last_kernel(place, packed, kernel, rest, half, decoded, level, steps, woven, fine, sem):
    rows, width = 2 * packed.shape[0] // 3 - 2, packed.shape[1]
    terms = before_terms(place, packed, level, steps, 0)
    result = phases(terms, kernel, rows, width)
    for i in range(2):
        for j in range(2):
            weave(rest[2 * i + j] + result[i][j], i, j, rows, width, woven)
        weave_out(fine, i, rows, woven)
    copy = pltpu.make_async_copy(fine, decoded.at[0], sem)
    copy.start()
    copy.wait()


def onward(value):
    count = lax.axis_size("tm")
    return lax.ppermute(value, "tm", [(i, (i + 1) % count) for i in range(count)])


def swap(value, offset):
    count = lax.axis_size("rows")
    pairs = [((2 * i + offset) % count, (2 * i + 1 + offset) % count) for i in range(count // 2)]
    return lax.ppermute(value, "rows", pairs + [(b, a) for a, b in pairs])


def body(
    latents,
    gain_first,
    kernel_first,
    gain_second,
    kernel_second,
    shortcut,
    gain_third,
    kernel_third,
):
    frames, rows, width, channels = latents.shape
    group, slab = lax.axis_index("tm"), lax.axis_index("rows")
    place = jnp.stack(
        [group, slab, jnp.int32(lax.axis_size("tm")), jnp.int32(lax.axis_size("rows"))]
    ).astype(jnp.int32)
    shape = jax.ShapeDtypeStruct
    odd = slab % 2
    near = lax.dynamic_slice_in_dim(latents, (rows - HALO) * (1 - odd), HALO, 1)
    far = lax.dynamic_slice_in_dim(latents, (rows - HALO) * odd, HALO, 1)
    near, far = swap(near, 0), swap(far, 1)

    wide1, wide2 = rows + 4, rows + 2
    pixels, pixels1, pixels2 = rows * width, wide1 * width, wide2 * width
    flops1, flops2, flops3 = (18 * n * 192 for n in (pixels1 * channels, pixels2 * 192, pixels * 192))
    dma = pltpu.SemaphoreType.DMA

    def work(tall, channels):
        return [pltpu.VMEM((tall * width, channels), BF16), pltpu.VMEM((tall * width, 128), F32)]

    held, weights, active, sums, gain_first = call(
        inner_kernel,
        (
            shape(latents.shape, BF16),
            shape((3, 3, 3, 192, channels), BF16),
            shape(latents.shape, BF16),
            shape((2, (rows - 2) * width, 192), F32),
            shape((channels,), F32),
        ),
        work(rows, channels) + [dma((4,))],
        2 * flops1,
        (place, latents, gain_first, jnp.swapaxes(kernel_first, 3, 4)),
        hbm=(1, 2, 3),
    )
    edge_work = [
        pltpu.VMEM((2 * HALO * width, 192), F32),
        pltpu.VMEM((2 * HALO, width, channels), BF16),
    ] + work(HALO, channels)
    ends = shape((2, HALO + 2, width, channels), BF16)
    packed1 = shape((wide1 * 3 // 2, width, 128), BF16)
    partial, late = call(
        late_edge_kernel,
        (packed1, ends),
        edge_work,
        flops1 // 2,
        (place, near, far, gain_first, active, weights, sums),
    )
    before_late = onward(partial)
    partial, tall = call(
        early_edge_kernel,
        (packed1, shape((2, wide1 + 2, width, channels), BF16)),
        [pltpu.VMEM(ends.shape, BF16)] + edge_work,
        flops1,
        (place, near, far, gain_first, active, weights, sums, late),
    )
    before_early = onward(partial)
    (own,) = call(
        first_own_kernel, (shape((2, pixels1, 192), F32),), [], 3 * flops1, (place, tall, weights)
    )
    (mixed,) = call(
        weights_kernel, (shape((3, 3, 3, 192, 192), BF16),), [], 1 << 24, (place, kernel_third)
    )
    second_work = (
        [pltpu.VMEM((pixels1, 192), BF16)] + work(wide1, 192) + [pltpu.VMEM((pixels2, 192), F32)]
    )
    packed2 = shape((wide2 * 3 // 2, width, 128), BF16)
    field = shape((wide1, width, 192), BF16)
    partial, late = call(
        late_second_kernel,
        (packed2, field),
        second_work,
        flops2,
        (place, own, before_late, gain_second, kernel_second),
    )
    before_late = onward(partial)
    partial, early = call(
        early_second_kernel,
        (packed2, field),
        second_work,
        2 * flops2,
        (place, own, before_early, gain_second, kernel_second, late),
    )
    before_early = onward(partial)
    (own,) = call(
        second_own_kernel,
        (shape((2, pixels2, 192), F32),),
        [],
        3 * flops2,
        (place, early, late, kernel_second, held, near, far, shortcut.T),
    )
    third_work = [pltpu.VMEM((pixels2, 192), BF16)] + work(wide2, 192)
    field = shape((wide2, width, 192), BF16)
    late_out, packed, late = call(
        late_third_kernel,
        (shape((rows, width, 192), BF16), packed2, field),
        third_work,
        1 << 24,
        (place, own, before_late, gain_third),
    )
    before_late = onward(packed)
    block_out, packed, early = call(
        early_third_kernel,
        (shape((2, rows, width, 192), BF16), packed2, field),
        third_work,
        1 << 24,
        (place, own, before_early, gain_third, late_out),
    )
    before_early = onward(packed)
    (own,) = call(
        third_own_kernel,
        (shape((2, 4, pixels, 192), F32),),
        [pltpu.VMEM((2, 3, rows, width, 192), BF16), pltpu.VMEM((2, 3, rows + 1, width, 192), BF16)],
        3 * flops3,
        (place, early, late, mixed),
    )
    last_work = [
        pltpu.VMEM((3, rows, width, 192), BF16),
        pltpu.VMEM((3, rows + 1, width, 192), BF16),
        pltpu.VMEM((2, rows, 2, 2 * width, 128), F32),
        pltpu.VMEM((2 * rows, 2 * width, 192), BF16),
        dma,
    ]
    fine = shape((2, 2 * rows, 2 * width, 192), BF16)
    decoded, rest = call(
        late_last_kernel,
        (fine, shape((4, pixels, 192), F32)),
        last_work,
        2 * flops3,
        (place, before_late, mixed, own),
        out_hbm=(0,),
    )
    (decoded,) = call(
        early_last_kernel,
        (fine,),
        last_work,
        flops3,
        (place, before_early, mixed, rest, decoded),
        hbm=(4,),
        out_hbm=(0,),
        aliases={4: 0},
    )
    return (block_out, decoded)


def solution(mesh):
    return jax.shard_map(
        body,
        mesh=mesh,
        in_specs=(P("tm", "rows", None, None), P(), P(), P(), P(), P(), P(), P()),
        out_specs=(P("tm", "rows", None, None), P("tm", "rows", None, None)),
        check_vma=False,
    )
```

```python
import jax
import jax.numpy as jnp
from jax import lax
from jax.experimental import pallas as pl
from jax.experimental.pallas import tpu as pltpu
from jax.sharding import PartitionSpec as P

F32 = jnp.float32
BF16 = jnp.bfloat16
HALO = 3
LIMIT = 24


def dot(a, b):
    return jnp.dot(a, b, preferred_element_type=F32)


def dot_t(a, b):
    return lax.dot_general(a, b, (((1,), (1,)), ((), ())), preferred_element_type=F32)


def spans(channels):
    return [(at, min(128, channels - at)) for at in range(0, channels, 128)]


def scales(squares, channels):
    total = dot(squares, jnp.ones((channels, 128), BF16))
    return lax.rsqrt(total * (1.0 / channels) + 1e-06)


def activated(v, scale, gain):
    u = v * scale * gain
    return u * (0.5 + 0.5 * jnp.tanh(0.5 * u))


def column_masks(width, channels):
    column = lax.broadcasted_iota(jnp.int32, (width, channels), 0)
    return column == 0, column == width - 1


def beside(v, masks):
    width = v.shape[0]
    left = jnp.where(masks[0], 0.0, pltpu.roll(v, 1, 0))
    right = jnp.where(masks[1], 0.0, pltpu.roll(v, width - 1, 0))
    return left, right


def call(kernel, out_shape, scratch, flops, args, hbm=(), out_hbm=(), aliases=None):
    vmem = pl.BlockSpec(memory_space=pltpu.VMEM)
    far = pl.BlockSpec(memory_space=pltpu.HBM)
    args = [pltpu.with_memory_space_constraint(x, pltpu.HBM) if i in hbm else x for i, x in enumerate(args)]

    def placed(*refs):
        kernel([f(axis) for f in (lax.axis_index, lax.axis_size) for axis in ("tm", "rows")], *refs)

    return pl.pallas_call(
        placed,
        out_shape=out_shape,
        in_specs=[far if i in hbm else vmem for i in range(len(args))],
        out_specs=tuple(far if i in out_hbm else vmem for i in range(len(out_shape))),
        scratch_shapes=scratch,
        input_output_aliases=aliases or {},
        compiler_params=pltpu.CompilerParams(vmem_limit_bytes=LIMIT << 20),
        cost_estimate=pl.CostEstimate(flops=flops, bytes_accessed=4 << 20, transcendentals=0),
    )(*args)


def pack_rows(ref, rows, get):
    for row in range(0, rows, 2):
        upper, lower = get(row), get(row + 1)
        ref[row] = upper[:, 0:128].astype(BF16)
        ref[row + 1] = lower[:, 0:128].astype(BF16)
        ref[rows + row // 2] = jnp.concatenate([upper[:, 128:192], lower[:, 128:192]], axis=1).astype(BF16)


def unpack_row(ref, row):
    rows = ref.shape[0] * 2 // 3
    rest = ref[rows + row // 2].astype(F32)
    side = 64 * (row % 2)
    return jnp.concatenate([ref[row].astype(F32), rest[:, side : side + 64]], axis=1)


def fill_field(field, rows, first, rest):
    width = field.shape[2]
    masks = column_masks(width, 128)
    for row in range(rows):
        for at, part in ((0, first(row)), (128, rest(row))):
            left, right = beside(part, masks)
            for shift, value in enumerate((left, part, right)):
                field[shift, row, :, at : at + 128] = value.astype(BF16)


def packed_parts(ref, follows=None):
    rows = ref.shape[0] * 2 // 3

    def guard(value):
        value = value.astype(F32)
        return value if follows is None else jnp.where(follows, value, 0.0)

    def first(row):
        return guard(ref[row])

    def rest(row):
        at = rows + row // 2
        if row % 2 == 0:
            return guard(ref[at])
        upper = ref[at].astype(F32)[:, 64:128]
        lower = jnp.zeros_like(upper) if row == rows - 1 else ref[at + 1].astype(F32)[:, 0:64]
        return guard(jnp.concatenate([upper, lower], axis=1))

    return rows, first, rest


def row_parts(rows, get):
    made = {}

    def row_of(row):
        if row not in made:
            made[row] = get(row)
        return made[row]

    def rest(row):
        upper = row_of(row)[:, 128:192]
        lower = row_of(row + 1)[:, 128:192] if row < rows - 1 else jnp.zeros_like(upper)
        return jnp.concatenate([upper, lower], axis=1)

    return rows, lambda row: row_of(row)[:, 0:128], rest


def two_rows(field, shift, row, rows):
    pixels = rows * field.shape[2]
    return [
        field[shift, row : row + rows].reshape(pixels, 256),
        field[shift, row + 1 : row + 1 + rows, :, 0:128].reshape(pixels, 128),
    ]


def two_rows_weights(upper, lower):
    return [upper, lower[128:192], lower[0:128]]


def convolve_field(kernel, terms, rows):
    lanes, weights = [], []
    for field, a in terms:
        for e in range(3):
            lanes += two_rows(field, e, 0, rows)
            weights += two_rows_weights(kernel[a, 0, e], kernel[a, 1, e])
            lanes.append(field[e, 2 : 2 + rows].reshape(rows * field.shape[2], 256))
            weights += [kernel[a, 2, e], jnp.zeros((64, 192), BF16)]
    return dot(jnp.concatenate(lanes, axis=1), jnp.concatenate(weights, axis=0))


def convolve(acc, product, kernel, terms, rows, width):
    masks = column_masks(width, 192)
    fields = [window(b) for window, a in terms for b in range(3)]
    if product is dot_t:
        fields = [jnp.concatenate(fields, axis=1)]
    for e in range(3):
        taps = [kernel[a, b, e] for window, a in terms for b in range(3)]
        if product is dot_t:
            taps = [jnp.concatenate(taps, axis=1)]
        total = None
        for field, tap in zip(fields, taps):
            term = product(field, tap)
            total = term if total is None else total + term
        for row in range(rows):
            part = slice(row * width, (row + 1) * width)
            moved = total[part]
            if e == 0:
                acc[part] = jnp.where(masks[0], 0.0, pltpu.roll(moved, 1, 0))
            elif e == 1:
                acc[part] += moved
            else:
                acc[part] += jnp.where(masks[1], 0.0, pltpu.roll(moved, width - 1, 0))


def windows(ref, rows):
    return lambda b: ref[b : b + rows].reshape(rows * ref.shape[1], ref.shape[2])


OWN = (((0, 2),), ((0, 1), (1, 2)))


def activate_rows(ref, gain, squares, scale, out):
    rows, width, channels = ref.shape
    pixels = rows * width
    v = ref[...].astype(F32)
    squares[0:pixels] = (v * v).astype(BF16).reshape(pixels, channels)
    scale[0:pixels] = scales(squares[0:pixels], channels)
    for row in range(rows):
        part = slice(row * width, (row + 1) * width)
        for at, lanes in spans(channels):
            out[row, :, at : at + lanes] = activated(
                ref[row, :, at : at + lanes].astype(F32), scale[part], gain[at : at + lanes].reshape(1, lanes)
            ).astype(BF16)


def inner_kernel(place, latents, gain, kernel, held, weights, active, sums, held_gain, squares, scale, sems):
    frames, rows, width, channels = held.shape
    copies = [
        pltpu.make_async_copy(latents.at[1], held.at[1], sems.at[0]),
        pltpu.make_async_copy(latents.at[0], held.at[0], sems.at[1]),
        pltpu.make_async_copy(kernel, weights, sems.at[2]),
        pltpu.make_async_copy(gain, held_gain, sems.at[3]),
    ]
    for copy in (copies[0], copies[3], copies[1], copies[2]):
        copy.start()
    copies[3].wait()
    for frame, copy in ((1, copies[0]), (0, copies[1])):
        copy.wait()
        activate_rows(held.at[frame], held_gain, squares, scale, active.at[frame])
    copies[2].wait()
    count = rows - 2
    convolve(sums, dot_t, weights, [(windows(active.at[1], count), 0)], count, width)


def fill_edges(place, near, far, frame, gain, active, edges, raw, squares, scale):
    odd = place[1] % 2 == 1
    inner = jnp.logical_and(place[1] > 0, place[1] < place[3] - 1)
    rows = active.shape[1]
    for row in range(HALO):
        chip = near[frame, row]
        next_chip = jnp.where(inner, far[frame, row], jnp.zeros_like(chip))
        raw[row] = jnp.where(odd, chip, next_chip)
        raw[HALO + row] = jnp.where(odd, next_chip, chip)
    activate_rows(raw.at[0:HALO], gain, squares, scale, edges.at[0, 0:HALO])
    activate_rows(raw.at[HALO : 2 * HALO], gain, squares, scale, edges.at[1, 2 : 2 + HALO])
    edges[0, HALO : HALO + 2] = active[frame, 0:2]
    edges[1, 0:2] = active[frame, rows - 2 : rows]


def edge_windows(edges):
    width, channels = edges.shape[2], edges.shape[3]
    return lambda b: edges[:, b : b + HALO].reshape(2 * HALO * width, channels)


def pack_joined(partial, sums, acc, wide, width):
    def get(row):
        if HALO <= row < wide - HALO:
            return sums[(row - HALO) * width : (row - HALO + 1) * width]
        at = row if row < HALO else row - (wide - 2 * HALO)
        return acc[at * width : (at + 1) * width]

    pack_rows(partial, wide, get)


def late_edge_kernel(
    place, near, far, gain, active, weights, sums, partial, edges, acc, raw, squares, scale
):
    fill_edges(place, near, far, 1, gain, active, edges, raw, squares, scale)
    width = active.shape[2]
    convolve(acc, dot_t, weights, [(edge_windows(edges), 0)], 2 * HALO, width)
    pack_joined(partial, sums, acc, active.shape[1] + 4, width)


def early_edge_kernel(
    place, near, far, gain, active, weights, late, partial, tall, edges, acc, raw, squares, scale
):
    fill_edges(place, near, far, 0, gain, active, edges, raw, squares, scale)
    rows, width = active.shape[1], active.shape[2]
    for frame, ends in ((0, edges), (1, late)):
        tall[frame, 0:HALO] = ends[0, 0:HALO]
        tall[frame, HALO : HALO + rows] = active[frame]
        tall[frame, HALO + rows :] = ends[1, 2:]
    wide = rows + 4
    convolve(
        acc, dot_t, weights, [(windows(tall.at[0], wide), 0), (windows(tall.at[1], wide), 1)], wide, width
    )
    pack_rows(partial, wide, lambda row: acc[row * width : (row + 1) * width])


def first_own_kernel(place, active, kernel, third, own, mixed):
    wide, width = active.shape[1] - 2, active.shape[2]
    for out in (1, 0):
        terms = [(windows(active.at[frame], wide), a) for frame, a in OWN[out]]
        convolve(own.at[out], dot_t, kernel, terms, wide, width)
    mix_weights(third, mixed)


def finish(place, own, before, gain, raw, squares, scale, keep):
    tall, width = before.shape[0] * 2 // 3, before.shape[1]
    start = place[1] * 8 - (tall - 8) // 2
    follows = place[0] > 0
    for row in range(tall):
        part = slice(row * width, (row + 1) * width)
        earlier = jnp.where(follows, unpack_row(before, row), 0.0)
        total = (own[part] + earlier).astype(BF16)
        raw[part] = total
        keep(row, total)
        total = total.astype(F32)
        squares[part] = (total * total).astype(BF16)
    scale[...] = scales(squares[...], 192)

    def get(row):
        part = slice(row * width, (row + 1) * width)
        inside = jnp.logical_and(start + row >= 0, start + row < place[3] * 8)
        lanes = []
        for at, count in spans(192):
            v = activated(
                raw[part, at : at + count].astype(F32), scale[part, 0:count], gain[at : at + count].reshape(1, count)
            )
            if not (tall - 8) // 2 <= row < (tall + 8) // 2:
                v = jnp.where(inside, v, 0.0)
            lanes.append(v)
        return jnp.concatenate(lanes, axis=1)

    return get


def second(place, own, before, gain, kernel, terms, partial, field, raw, squares, scale):
    rows = field.shape[1]
    width, wide = field.shape[2], rows - 2
    get = finish(place, own, before, gain, raw, squares, scale, lambda row, total: None)
    fill_field(field, *row_parts(rows, get))
    total = convolve_field(kernel, terms, wide)
    pack_rows(partial, wide, lambda row: total[row * width : (row + 1) * width])


def late_second_kernel(place, own, before, gain, kernel, partial, field, raw, squares, scale):
    terms = [(field, 0)]
    second(place, own.at[1], before, gain, kernel, terms, partial, field, raw, squares, scale)


def early_second_kernel(place, own, before, gain, kernel, late, partial, field, raw, squares, scale):
    terms = [(field, 0), (late, 1)]
    second(place, own.at[0], before, gain, kernel, terms, partial, field, raw, squares, scale)


def second_own_kernel(place, early, late, kernel, latents, near, far, shortcut, own):
    wide, width = early.shape[1] - 2, early.shape[2]
    pixels = wide * width
    rows, channels = latents.shape[1], latents.shape[3]
    odd = place[1] % 2
    inner = wide - 1
    fields = (early, late)
    for out in (1, 0):
        own[out] = convolve_field(kernel, [(fields[frame], a) for frame, a in OWN[out]], wide)
        body = latents[out].reshape(rows * width, channels)
        own[out, width : pixels - width] += dot_t(body, shortcut[...])
        other = dot_t(near[out, jnp.where(odd == 1, HALO - 1, 0)], shortcut[...])
        own[out, pl.ds(jnp.where(odd == 1, 0, inner * width), width)] += other
        other = dot_t(far[out, jnp.where(odd == 1, 0, HALO - 1)], shortcut[...])
        own[out, pl.ds(jnp.where(odd == 1, inner * width, 0), width)] += other


def third(place, own, before, gain, block, packed, raw, squares, scale):
    tall = packed.shape[0] * 2 // 3

    def keep(row, total):
        if 0 < row < tall - 1:
            block[row - 1] = total

    pack_rows(packed, tall, finish(place, own, before, gain, raw, squares, scale, keep))


def late_third_kernel(place, own, before, gain, block, packed, raw, squares, scale):
    third(place, own.at[1], before, gain, block, packed, raw, squares, scale)


def early_third_kernel(place, own, before, gain, block, packed, raw, squares, scale):
    third(place, own.at[0], before, gain, block, packed, raw, squares, scale)


def mix_weights(kernel, out):
    def halves(taps, parity):
        if parity == 0:
            return taps[0], taps[1] + taps[2]
        return taps[0] + taps[1], taps[2]

    for a in range(3):
        for i in range(2):
            rows = [halves([kernel[a, b, e].astype(F32) for b in range(3)], i) for e in range(3)]
            for j in range(2):
                upper = halves([rows[e][0] for e in range(3)], j)
                lower = halves([rows[e][1] for e in range(3)], j)
                for column in range(2):
                    at = 384 * column
                    for part in two_rows_weights(upper[column].astype(BF16), lower[column].astype(BF16)):
                        out[a, 2 * i + j, at : at + part.shape[0]] = part
                        at += part.shape[0]


def phase(terms, kernel, i, j, rows):
    lanes, weights = [], []
    for field, a in terms:
        for shift in (j, j + 1):
            lanes += two_rows(field, shift, i, rows)
        weights.append(kernel[a, 2 * i + j])
    return dot(jnp.concatenate(lanes, axis=1), jnp.concatenate(weights, axis=0))


def third_own_kernel(place, early, late, kernel, early_out, late_out, own, block_out, fields, sems):
    copies = [
        pltpu.make_async_copy(block, block_out.at[frame], sems.at[frame])
        for frame, block in enumerate((early_out, late_out))
    ]
    for copy in copies:
        copy.start()
    for frame, packed in enumerate((early, late)):
        fill_field(fields.at[frame], *packed_parts(packed))
    rows = early_out.shape[0]
    for out in (1, 0):
        terms = [(fields.at[frame], a) for frame, a in OWN[out]]
        for i in range(2):
            for j in range(2):
                own[out, 2 * i + j] = phase(terms, kernel, i, j, rows)
    for copy in copies:
        copy.wait()


def weave(total, j, rows, width, woven):
    for row in range(rows):
        value = total[row * width : (row + 1) * width]
        woven[row, 0, pl.ds(j, width, stride=2)] = value[:, 0:128]
        woven[row, 1, pl.ds(j, width, stride=2), 0:64] = value[:, 128:192]


def write_out(own, field, kernel, a, rows, width, woven, fine, out, sems):
    copies = []
    for i in range(2):
        for j in range(2):
            total = own[2 * i + j] + phase([(field, a)], kernel, i, j, rows)
            weave(total, j, rows, width, woven.at[i])
        for row in range(rows):
            fine[i, row, :, 0:128] = woven[i, row, 0].astype(BF16)
            fine[i, row, :, 128:192] = woven[i, row, 1, :, 0:64].astype(BF16)
        copies.append(pltpu.make_async_copy(fine.at[i], out.at[:, i], sems.at[i]))
        copies[-1].start()
    return copies


def late_last_kernel(place, packed, kernel, own, decoded, rest, field, woven, fine, sems):
    rows, width = packed.shape[0] * 2 // 3 - 2, packed.shape[1]
    fill_field(field, *packed_parts(packed, place[0] > 0))
    copies = write_out(own.at[1], field, kernel, 0, rows, width, woven, fine, decoded.at[1], sems)
    for i in range(2):
        for j in range(2):
            rest[2 * i + j] = own[0, 2 * i + j] + phase([(field, 1)], kernel, i, j, rows)
    for copy in copies:
        copy.wait()


def early_last_kernel(place, packed, kernel, rest, late, decoded, field, woven, fine, sems):
    rows, width = packed.shape[0] * 2 // 3 - 2, packed.shape[1]
    fill_field(field, *packed_parts(packed, place[0] > 0))
    for copy in write_out(rest, field, kernel, 0, rows, width, woven, fine, decoded.at[0], sems):
        copy.wait()


def onward(value):
    count = lax.axis_size("tm")
    return lax.ppermute(value, "tm", [(i, (i + 1) % count) for i in range(count)])


def swap(value, offset):
    count = lax.axis_size("rows")
    pairs = [(i, i + 1) for i in range(offset, count - 1, 2)]
    alone = set(range(count)) - {i for pair in pairs for i in pair}
    return lax.ppermute(
        value, "rows", pairs + [(b, a) for a, b in pairs] + [(i, i) for i in sorted(alone)]
    )


def body(
    latents,
    gain_first,
    kernel_first,
    gain_second,
    kernel_second,
    shortcut,
    gain_third,
    kernel_third,
):
    frames, rows, width, channels = latents.shape
    shape = jax.ShapeDtypeStruct
    odd = lax.axis_index("rows") % 2
    near = lax.dynamic_slice_in_dim(latents, (rows - HALO) * (1 - odd), HALO, 1)
    far = lax.dynamic_slice_in_dim(latents, (rows - HALO) * odd, HALO, 1)
    near, far = swap(near, 0), swap(far, 1)

    wide1, wide2 = rows + 4, rows + 2
    pixels, pixels1, pixels2 = rows * width, wide1 * width, wide2 * width
    flops1, flops2, flops3 = (18 * n * 192 for n in (pixels1 * channels, pixels2 * 192, pixels * 192))
    dma = pltpu.SemaphoreType.DMA

    def work(tall, channels):
        return [pltpu.VMEM((tall * width, channels), BF16), pltpu.VMEM((tall * width, 128), F32)]

    held, weights, active, sums, gain_first = call(
        inner_kernel,
        (
            shape(latents.shape, BF16),
            shape((3, 3, 3, 192, channels), BF16),
            shape(latents.shape, BF16),
            shape(((rows - 2) * width, 192), F32),
            shape((channels,), F32),
        ),
        work(rows, channels) + [dma((4,))],
        2 * flops1,
        (latents, gain_first, jnp.swapaxes(kernel_first, 3, 4)),
        hbm=(0, 1, 2),
    )
    edge_work = [pltpu.VMEM((2 * HALO, width, channels), BF16)] + work(HALO, channels)
    ends = shape((2, HALO + 2, width, channels), BF16)
    packed1 = shape((wide1 * 3 // 2, width, 128), BF16)
    partial, late = call(
        late_edge_kernel,
        (packed1, ends),
        [pltpu.VMEM((2 * HALO * width, 192), F32)] + edge_work,
        flops1 // 2,
        (near, far, gain_first, active, weights, sums),
    )
    before_late = onward(partial)
    partial, tall = call(
        early_edge_kernel,
        (packed1, shape((2, wide1 + 2, width, channels), BF16)),
        [pltpu.VMEM(ends.shape, BF16), pltpu.VMEM((pixels1, 192), F32)] + edge_work,
        2 * flops1,
        (near, far, gain_first, active, weights, late),
    )
    before_early = onward(partial)
    own, mixed = call(
        first_own_kernel,
        (shape((2, pixels1, 192), F32), shape((3, 4, 768, 192), BF16)),
        [],
        3 * flops1,
        (tall, weights, kernel_third),
    )
    second_work = [pltpu.VMEM((pixels1, 192), BF16)] + work(wide1, 192)
    packed2 = shape((wide2 * 3 // 2, width, 128), BF16)
    field = shape((3, wide1, width, 256), BF16)
    partial, late = call(
        late_second_kernel,
        (packed2, field),
        second_work,
        flops2,
        (own, before_late, gain_second, kernel_second),
    )
    before_late = onward(partial)
    partial, early = call(
        early_second_kernel,
        (packed2, field),
        second_work,
        2 * flops2,
        (own, before_early, gain_second, kernel_second, late),
    )
    before_early = onward(partial)
    (own,) = call(
        second_own_kernel,
        (shape((2, pixels2, 192), F32),),
        [],
        3 * flops2,
        (early, late, kernel_second, held, near, far, shortcut.T),
    )
    third_work = [pltpu.VMEM((pixels2, 192), BF16)] + work(wide2, 192)
    block = shape((rows, width, 192), BF16)
    late_out, late = call(
        late_third_kernel,
        (block, packed2),
        third_work,
        1 << 24,
        (own, before_late, gain_third),
    )
    before_late = onward(late)
    early_out, early = call(
        early_third_kernel,
        (block, packed2),
        third_work,
        1 << 24,
        (own, before_early, gain_third),
    )
    before_early = onward(early)
    own, block_out = call(
        third_own_kernel,
        (shape((2, 4, pixels, 192), F32), shape((2, rows, width, 192), BF16)),
        [pltpu.VMEM((2, 3, wide2, width, 256), BF16), dma((2,))],
        3 * flops3,
        (early, late, mixed, early_out, late_out),
        out_hbm=(1,),
    )
    last_work = [
        pltpu.VMEM((3, wide2, width, 256), BF16),
        pltpu.VMEM((2, rows, 2, 2 * width, 128), F32),
        pltpu.VMEM((2, rows, 2 * width, 192), BF16),
        dma((2,)),
    ]
    fine = shape((2, rows, 2, 2 * width, 192), BF16)
    decoded, rest = call(
        late_last_kernel,
        (fine, shape((4, pixels, 192), F32)),
        last_work,
        2 * flops3,
        (before_late, mixed, own),
        out_hbm=(0,),
    )
    (decoded,) = call(
        early_last_kernel,
        (fine,),
        last_work,
        flops3,
        (before_early, mixed, rest, decoded),
        hbm=(3,),
        out_hbm=(0,),
        aliases={3: 0},
    )
    decoded = decoded.reshape(2, 2 * rows, 2 * width, 192)
    return (block_out, decoded)


def solution(mesh):
    return jax.shard_map(
        body,
        mesh=mesh,
        in_specs=(P("tm", "rows", None, None), P(), P(), P(), P(), P(), P(), P()),
        out_specs=(P("tm", "rows", None, None), P("tm", "rows", None, None)),
        check_vma=False,
    )
```

```python
import jax
import jax.numpy as jnp
from jax import lax
from jax.experimental import pallas as pl
from jax.experimental.pallas import tpu as pltpu
from jax.sharding import PartitionSpec as P

F32 = jnp.float32
BF16 = jnp.bfloat16
HALO = 3
LIMIT = 24


def dot(a, b):
    return jnp.dot(a, b, preferred_element_type=F32)


def dot_t(a, b):
    return lax.dot_general(a, b, (((1,), (1,)), ((), ())), preferred_element_type=F32)


def spans(channels):
    return [(at, min(128, channels - at)) for at in range(0, channels, 128)]


def scales(squares, channels):
    total = dot(squares, jnp.ones((channels, 128), BF16))
    return lax.rsqrt(total * (1.0 / channels) + 1e-06)


def activated(v, scale, gain):
    u = v * scale * gain
    return u * (0.5 + 0.5 * jnp.tanh(0.5 * u))


def column_masks(width, channels):
    column = lax.broadcasted_iota(jnp.int32, (width, channels), 0)
    return column == 0, column == width - 1


def beside(v, masks):
    width = v.shape[0]
    left = jnp.where(masks[0], 0.0, pltpu.roll(v, 1, 0))
    right = jnp.where(masks[1], 0.0, pltpu.roll(v, width - 1, 0))
    return left, right


def call(kernel, out_shape, scratch, flops, args, hbm=(), out_hbm=(), aliases=None, after=()):
    vmem = pl.BlockSpec(memory_space=pltpu.VMEM)
    far = pl.BlockSpec(memory_space=pltpu.HBM)
    args = [pltpu.with_memory_space_constraint(x, pltpu.HBM) if i in hbm else x for i, x in enumerate(args)]

    count = len(args)

    def placed(*refs):
        place = [f(axis) for f in (lax.axis_index, lax.axis_size) for axis in ("tm", "rows")]
        kernel(place, *refs[:count], *refs[count + len(after) :])

    return pl.pallas_call(
        placed,
        out_shape=out_shape,
        in_specs=[far if i in hbm else vmem for i in range(count)] + [pl.BlockSpec(memory_space=pl.ANY)] * len(after),
        out_specs=tuple(far if i in out_hbm else vmem for i in range(len(out_shape))),
        scratch_shapes=scratch,
        input_output_aliases=aliases or {},
        compiler_params=pltpu.CompilerParams(vmem_limit_bytes=LIMIT << 20),
        cost_estimate=pl.CostEstimate(flops=flops, bytes_accessed=4 << 20, transcendentals=0),
    )(*args, *after)


def pack_rows(ref, rows, get):
    for row in range(0, rows, 2):
        upper, lower = get(row), get(row + 1)
        ref[row] = upper[:, 0:128].astype(BF16)
        ref[row + 1] = lower[:, 0:128].astype(BF16)
        ref[rows + row // 2] = jnp.concatenate([upper[:, 128:192], lower[:, 128:192]], axis=1).astype(BF16)


def unpack_row(ref, row):
    rows = ref.shape[0] * 2 // 3
    rest = ref[rows + row // 2].astype(F32)
    side = 64 * (row % 2)
    return jnp.concatenate([ref[row].astype(F32), rest[:, side : side + 64]], axis=1)


def fill_field(field, rows, first, rest):
    width = field.shape[2]
    masks = column_masks(width, 128)
    for row in range(rows):
        for at, part in ((0, first(row)), (128, rest(row))):
            left, right = beside(part, masks)
            for shift, value in enumerate((left, part, right)):
                field[shift, row, :, at : at + 128] = value.astype(BF16)


def packed_parts(ref, follows=None):
    rows = ref.shape[0] * 2 // 3

    def guard(value):
        value = value.astype(F32)
        return value if follows is None else jnp.where(follows, value, 0.0)

    def first(row):
        return guard(ref[row])

    def rest(row):
        at = rows + row // 2
        if row % 2 == 0:
            return guard(ref[at])
        upper = ref[at].astype(F32)[:, 64:128]
        lower = jnp.zeros_like(upper) if row == rows - 1 else ref[at + 1].astype(F32)[:, 0:64]
        return guard(jnp.concatenate([upper, lower], axis=1))

    return rows, first, rest


def row_parts(rows, get):
    made = {}

    def row_of(row):
        if row not in made:
            made[row] = get(row)
        return made[row]

    def rest(row):
        upper = row_of(row)[:, 128:192]
        lower = row_of(row + 1)[:, 128:192] if row < rows - 1 else jnp.zeros_like(upper)
        return jnp.concatenate([upper, lower], axis=1)

    return rows, lambda row: row_of(row)[:, 0:128], rest


def two_rows(field, shift, row, rows):
    pixels = rows * field.shape[2]
    return [
        field[shift, row : row + rows].reshape(pixels, 256),
        field[shift, row + 1 : row + 1 + rows, :, 0:128].reshape(pixels, 128),
    ]


def two_rows_weights(upper, lower):
    return [upper, lower[128:192], lower[0:128]]


def convolve_field(kernel, terms, rows):
    lanes, weights = [], []
    for field, a in terms:
        for e in range(3):
            lanes += two_rows(field, e, 0, rows)
            weights += two_rows_weights(kernel[a, 0, e], kernel[a, 1, e])
            lanes.append(field[e, 2 : 2 + rows].reshape(rows * field.shape[2], 256))
            weights += [kernel[a, 2, e], jnp.zeros((64, 192), BF16)]
    return dot(jnp.concatenate(lanes, axis=1), jnp.concatenate(weights, axis=0))


def convolve(acc, product, kernel, terms, rows, width):
    masks = column_masks(width, 192)
    fields = [window(b) for window, a in terms for b in range(3)]
    if product is dot_t:
        fields = [jnp.concatenate(fields, axis=1)]
    for e in range(3):
        taps = [kernel[a, b, e] for window, a in terms for b in range(3)]
        if product is dot_t:
            taps = [jnp.concatenate(taps, axis=1)]
        total = None
        for field, tap in zip(fields, taps):
            term = product(field, tap)
            total = term if total is None else total + term
        for row in range(rows):
            part = slice(row * width, (row + 1) * width)
            moved = total[part]
            if e == 0:
                acc[part] = jnp.where(masks[0], 0.0, pltpu.roll(moved, 1, 0))
            elif e == 1:
                acc[part] += moved
            else:
                acc[part] += jnp.where(masks[1], 0.0, pltpu.roll(moved, width - 1, 0))


def windows(ref, rows):
    return lambda b: ref[b : b + rows].reshape(rows * ref.shape[1], ref.shape[2])


OWN = (((0, 2),), ((0, 1), (1, 2)))


def activate_rows(ref, gain, squares, scale, out):
    rows, width, channels = ref.shape
    pixels = rows * width
    v = ref[...].astype(F32)
    squares[0:pixels] = (v * v).astype(BF16).reshape(pixels, channels)
    scale[0:pixels] = scales(squares[0:pixels], channels)
    for row in range(rows):
        part = slice(row * width, (row + 1) * width)
        for at, lanes in spans(channels):
            out[row, :, at : at + lanes] = activated(
                ref[row, :, at : at + lanes].astype(F32), scale[part], gain[at : at + lanes].reshape(1, lanes)
            ).astype(BF16)


def rim_kernel(place, latents, gain, held, held_gain, near, far, sems):
    rows = held.shape[1]
    copies = [pltpu.make_async_copy(latents.at[frame], held.at[frame], sems.at[frame]) for frame in range(2)]
    copies.append(pltpu.make_async_copy(gain, held_gain, sems.at[2]))
    for copy in copies:
        copy.start()
    odd = place[1] % 2
    for frame in range(2):
        copies[frame].wait()
        far[frame] = held[frame, pl.ds((rows - HALO) * odd, HALO)]
        near[frame] = held[frame, pl.ds((rows - HALO) * (1 - odd), HALO)]
    copies[2].wait()


def inner_kernel(place, held, gain, weights, active, packed, squares, scale, sums):
    frames, rows, width, channels = held.shape
    for frame in range(frames):
        activate_rows(held.at[frame], gain, squares, scale, active.at[frame])
    count = rows - 2
    for out, taps in ((1, ((1, 0),)), (0, ((0, 0), (1, 1)))):
        terms = [(windows(active.at[frame], count), a) for frame, a in taps]
        convolve(sums.at[out], dot_t, weights, terms, count, width)
        pack_rows(packed.at[out], count, lambda row: sums[out, row * width : (row + 1) * width])


def late_inner_own_kernel(place, active, weights, own):
    count, width = active.shape[1] - 2, active.shape[2]
    terms = [(windows(active.at[frame], count), a) for frame, a in OWN[1]]
    convolve(own, dot_t, weights, terms, count, width)


def fill_edges(place, near, far, frame, gain, active, edges, raw, squares, scale):
    odd = place[1] % 2 == 1
    inner = jnp.logical_and(place[1] > 0, place[1] < place[3] - 1)
    rows = active.shape[1]
    for row in range(HALO):
        chip = near[frame, row]
        next_chip = jnp.where(inner, far[frame, row], jnp.zeros_like(chip))
        raw[row] = jnp.where(odd, chip, next_chip)
        raw[HALO + row] = jnp.where(odd, next_chip, chip)
    activate_rows(raw.at[0:HALO], gain, squares, scale, edges.at[0, 0:HALO])
    activate_rows(raw.at[HALO : 2 * HALO], gain, squares, scale, edges.at[1, 2 : 2 + HALO])
    edges[0, HALO : HALO + 2] = active[frame, 0:2]
    edges[1, 0:2] = active[frame, rows - 2 : rows]


def edge_windows(edges):
    width, channels = edges.shape[2], edges.shape[3]
    return lambda b: edges[:, b : b + HALO].reshape(2 * HALO * width, channels)


def pack_edges(partial, acc, width):
    pack_rows(partial, 2 * HALO, lambda row: acc[row * width : (row + 1) * width])


def late_edge_kernel(place, near, far, gain, active, weights, partial, edges, acc, raw, squares, scale):
    fill_edges(place, near, far, 1, gain, active, edges, raw, squares, scale)
    width = active.shape[2]
    convolve(acc, dot_t, weights, [(edge_windows(edges), 0)], 2 * HALO, width)
    pack_edges(partial, acc, width)


def early_edge_kernel(
    place, near, far, gain, active, weights, late, partial, edges, acc, raw, squares, scale
):
    fill_edges(place, near, far, 0, gain, active, edges, raw, squares, scale)
    width = active.shape[2]
    convolve(acc, dot_t, weights, [(edge_windows(edges), 0), (edge_windows(late), 1)], 2 * HALO, width)
    pack_edges(partial, acc, width)


def late_edge_own_kernel(place, early, late, weights, own):
    terms = [(edge_windows((early, late)[frame]), a) for frame, a in OWN[1]]
    convolve(own, dot_t, weights, terms, 2 * HALO, early.shape[2])


def early_own_kernel(place, active, early, weights, inner, edges):
    count, width = active.shape[1] - 2, active.shape[2]
    (frame, a), = OWN[0]
    convolve(inner, dot_t, weights, [(windows(active.at[frame], count), a)], count, width)
    convolve(edges, dot_t, weights, [(edge_windows(early), a)], 2 * HALO, width)


def finish(place, own, before, gain, raw, squares, scale, keep):
    before, tall, width = before
    start = place[1] * 8 - (tall - 8) // 2
    follows = place[0] > 0
    for row in range(tall):
        part = slice(row * width, (row + 1) * width)
        earlier = jnp.where(follows, before(row), 0.0)
        total = (own(row) + earlier).astype(BF16)
        raw[part] = total
        keep(row, total)
        total = total.astype(F32)
        squares[part] = (total * total).astype(BF16)
    scale[...] = scales(squares[...], 192)

    def get(row):
        part = slice(row * width, (row + 1) * width)
        inside = jnp.logical_and(start + row >= 0, start + row < place[3] * 8)
        lanes = []
        for at, count in spans(192):
            v = activated(
                raw[part, at : at + count].astype(F32), scale[part, 0:count], gain[at : at + count].reshape(1, count)
            )
            if not (tall - 8) // 2 <= row < (tall + 8) // 2:
                v = jnp.where(inside, v, 0.0)
            lanes.append(v)
        return jnp.concatenate(lanes, axis=1)

    return get


def second(place, own, before, gain, kernel, terms, partial, field, raw, squares, scale):
    rows = field.shape[1]
    width, wide = field.shape[2], rows - 2
    get = finish(place, own, before, gain, raw, squares, scale, lambda row, total: None)
    fill_field(field, *row_parts(rows, get))
    total = convolve_field(kernel, terms, wide)
    pack_rows(partial, wide, lambda row: total[row * width : (row + 1) * width])


def joined(inner, edges):
    count = inner.shape[0] * 2 // 3

    def get(row):
        if HALO <= row < HALO + count:
            return unpack_row(inner, row - HALO)
        return unpack_row(edges, row if row < HALO else row - count)

    return get, count + 2 * HALO, inner.shape[1]


def whole(packed):
    return lambda row: unpack_row(packed, row), packed.shape[0] * 2 // 3, packed.shape[1]


def joined_own(inner, edges, width):
    count = inner.shape[0] // width

    def get(row):
        ref, at = (inner, row - HALO) if HALO <= row < HALO + count else (edges, row if row < HALO else row - count)
        return ref[at * width : (at + 1) * width]

    return get


def rows_of(own, width):
    return lambda row: own[row * width : (row + 1) * width]


def late_second_kernel(
    place, own_inner, own_edges, inner, edges, gain, kernel, partial, field, raw, squares, scale
):
    before = joined(inner.at[1], edges)
    own = joined_own(own_inner, own_edges, field.shape[2])
    second(place, own, before, gain, kernel, [(field, 0)], partial, field, raw, squares, scale)


def early_second_kernel(
    place, own_inner, own_edges, inner, edges, gain, kernel, late, partial, field, raw, squares, scale
):
    before = joined(inner.at[0], edges)
    own = joined_own(own_inner, own_edges, field.shape[2])
    second(place, own, before, gain, kernel, [(field, 0), (late, 1)], partial, field, raw, squares, scale)


def second_own_kernel(place, early, late, kernel, latents, near, far, shortcut, own):
    wide, width = early.shape[1] - 2, early.shape[2]
    pixels = wide * width
    rows, channels = latents.shape[1], latents.shape[3]
    odd = place[1] % 2
    inner = wide - 1
    fields = (early, late)
    for out in (1, 0):
        own[out] = convolve_field(kernel, [(fields[frame], a) for frame, a in OWN[out]], wide)
        body = latents[out].reshape(rows * width, channels)
        own[out, width : pixels - width] += dot_t(body, shortcut[...])
        other = dot_t(near[out, jnp.where(odd == 1, HALO - 1, 0)], shortcut[...])
        own[out, pl.ds(jnp.where(odd == 1, 0, inner * width), width)] += other
        other = dot_t(far[out, jnp.where(odd == 1, 0, HALO - 1)], shortcut[...])
        own[out, pl.ds(jnp.where(odd == 1, inner * width, 0), width)] += other


def third(place, own, before, gain, block, packed, raw, squares, scale):
    tall = packed.shape[0] * 2 // 3

    def keep(row, total):
        if 0 < row < tall - 1:
            block[row - 1] = total

    own = rows_of(own, packed.shape[1])
    pack_rows(packed, tall, finish(place, own, whole(before), gain, raw, squares, scale, keep))


def late_third_kernel(place, own, before, gain, block, packed, raw, squares, scale):
    third(place, own.at[1], before, gain, block, packed, raw, squares, scale)


def early_third_kernel(place, own, before, gain, block, packed, raw, squares, scale):
    third(place, own.at[0], before, gain, block, packed, raw, squares, scale)


def weights_kernel(place, kernel, out):
    def halves(taps, parity):
        if parity == 0:
            return taps[0], taps[1] + taps[2]
        return taps[0] + taps[1], taps[2]

    for a in range(3):
        for i in range(2):
            rows = [halves([kernel[a, b, e].astype(F32) for b in range(3)], i) for e in range(3)]
            for j in range(2):
                upper = halves([rows[e][0] for e in range(3)], j)
                lower = halves([rows[e][1] for e in range(3)], j)
                for column in range(2):
                    at = 384 * column
                    for part in two_rows_weights(upper[column].astype(BF16), lower[column].astype(BF16)):
                        out[a, 2 * i + j, at : at + part.shape[0]] = part
                        at += part.shape[0]


def phase(terms, kernel, i, j, rows):
    lanes, weights = [], []
    for field, a in terms:
        for shift in (j, j + 1):
            lanes += two_rows(field, shift, i, rows)
        weights.append(kernel[a, 2 * i + j])
    return dot(jnp.concatenate(lanes, axis=1), jnp.concatenate(weights, axis=0))


def third_own_kernel(place, early, late, kernel, early_out, late_out, own, block_out, fields, sems):
    copies = [
        pltpu.make_async_copy(block, block_out.at[frame], sems.at[frame])
        for frame, block in enumerate((early_out, late_out))
    ]
    for copy in copies:
        copy.start()
    for frame, packed in enumerate((early, late)):
        fill_field(fields.at[frame], *packed_parts(packed))
    rows = early_out.shape[0]
    for out in (1, 0):
        terms = [(fields.at[frame], a) for frame, a in OWN[out]]
        for i in range(2):
            for j in range(2):
                own[out, 2 * i + j] = phase(terms, kernel, i, j, rows)
    for copy in copies:
        copy.wait()


def weave(total, j, rows, width, woven):
    for row in range(rows):
        value = total[row * width : (row + 1) * width]
        woven[row, 0, pl.ds(j, width, stride=2)] = value[:, 0:128]
        woven[row, 1, pl.ds(j, width, stride=2), 0:64] = value[:, 128:192]


def write_out(own, field, kernel, a, rows, width, woven, fine, out, sems):
    copies = []
    for i in range(2):
        for j in range(2):
            total = own[2 * i + j] + phase([(field, a)], kernel, i, j, rows)
            weave(total, j, rows, width, woven.at[i])
        for row in range(rows):
            fine[i, row, :, 0:128] = woven[i, row, 0].astype(BF16)
            fine[i, row, :, 128:192] = woven[i, row, 1, :, 0:64].astype(BF16)
        copies.append(pltpu.make_async_copy(fine.at[i], out.at[:, i], sems.at[i]))
        copies[-1].start()
    return copies


def late_last_kernel(place, packed, kernel, own, decoded, rest, field, woven, fine, sems):
    rows, width = packed.shape[0] * 2 // 3 - 2, packed.shape[1]
    fill_field(field, *packed_parts(packed, place[0] > 0))
    copies = write_out(own.at[1], field, kernel, 0, rows, width, woven, fine, decoded.at[1], sems)
    for i in range(2):
        for j in range(2):
            rest[2 * i + j] = own[0, 2 * i + j] + phase([(field, 1)], kernel, i, j, rows)
    for copy in copies:
        copy.wait()


def early_last_kernel(place, packed, kernel, rest, late, decoded, field, woven, fine, sems):
    rows, width = packed.shape[0] * 2 // 3 - 2, packed.shape[1]
    fill_field(field, *packed_parts(packed, place[0] > 0))
    for copy in write_out(rest, field, kernel, 0, rows, width, woven, fine, decoded.at[0], sems):
        copy.wait()


def onward(value):
    count = lax.axis_size("tm")
    return lax.ppermute(value, "tm", [(i, (i + 1) % count) for i in range(count)])


def swap(value, offset):
    count = lax.axis_size("rows")
    pairs = [(i, i + 1) for i in range(offset, count - 1, 2)]
    alone = set(range(count)) - {i for pair in pairs for i in pair}
    return lax.ppermute(
        value, "rows", pairs + [(b, a) for a, b in pairs] + [(i, i) for i in sorted(alone)]
    )


def body(
    latents,
    gain_first,
    kernel_first,
    gain_second,
    kernel_second,
    shortcut,
    gain_third,
    kernel_third,
):
    frames, rows, width, channels = latents.shape
    shape = jax.ShapeDtypeStruct
    shape = jax.ShapeDtypeStruct
    odd = lax.axis_index("rows") % 2
    near = lax.dynamic_slice_in_dim(latents, (rows - HALO) * (1 - odd), HALO, 1)
    far = lax.dynamic_slice_in_dim(latents, (rows - HALO) * odd, HALO, 1)
    near, far = swap(near, 0), swap(far, 1)

    wide1, wide2 = rows + 4, rows + 2
    pixels, pixels1, pixels2 = rows * width, wide1 * width, wide2 * width
    flops1, flops2, flops3 = (18 * n * 192 for n in (pixels1 * channels, pixels2 * 192, pixels * 192))
    dma = pltpu.SemaphoreType.DMA

    def work(tall, channels):
        return [pltpu.VMEM((tall * width, channels), BF16), pltpu.VMEM((tall * width, 128), F32)]

    rim = shape((frames, HALO, width, channels), BF16)
    held, gain_first, near, far = call(
        rim_kernel,
        (shape(latents.shape, BF16), shape((channels,), F32), rim, rim),
        [dma((3,))],
        1 << 34,
        (latents, gain_first),
        hbm=(0, 1),
    )
    far, near = swap(far, 1), swap(near, 0)
    inner_rows = rows - 2
    inner_pixels = inner_rows * width
    across = jnp.swapaxes(kernel_first, 3, 4)
    active, inner = call(
        inner_kernel,
        (
            shape(latents.shape, BF16),
            shape((2, inner_rows * 3 // 2, width, 128), BF16),
        ),
        work(rows, channels) + [pltpu.VMEM((2, inner_pixels, 192), F32)],
        2 * flops1,
        (held, gain_first, across),
    )
    inner = onward(inner)
    (late_inner,) = call(
        late_inner_own_kernel, (shape((inner_pixels, 192), F32),), [], flops1, (active, across)
    )
    edge_sums = shape((2 * HALO * width, 192), F32)
    edge_work = [pltpu.VMEM(edge_sums.shape, F32), pltpu.VMEM((2 * HALO, width, channels), BF16)]
    edge_work += work(HALO, channels)
    ends = shape((2, HALO + 2, width, channels), BF16)
    packed1 = shape((HALO * 3, width, 128), BF16)
    partial, late = call(
        late_edge_kernel,
        (packed1, ends),
        edge_work,
        flops1 // 2,
        (near, far, gain_first, active, across),
        after=(late_inner,),
    )
    late_edges = onward(partial)
    partial, early = call(
        early_edge_kernel,
        (packed1, ends),
        edge_work,
        flops1,
        (near, far, gain_first, active, across, late),
        after=(partial,),
    )
    early_edges = onward(partial)
    (late_rest,) = call(late_edge_own_kernel, (edge_sums,), [], flops1, (early, late, across))
    second_work = [pltpu.VMEM((pixels1, 192), BF16)] + work(wide1, 192)
    packed2 = shape((wide2 * 3 // 2, width, 128), BF16)
    field = shape((3, wide1, width, 256), BF16)
    partial, late = call(
        late_second_kernel,
        (packed2, field),
        second_work,
        flops2,
        (late_inner, late_rest, inner, late_edges, gain_second, kernel_second),
    )
    before_late = onward(partial)
    early_inner, early_rest = call(
        early_own_kernel,
        (shape((inner_pixels, 192), F32), edge_sums),
        [],
        flops1,
        (active, early, across),
        after=(partial,),
    )
    partial, early = call(
        early_second_kernel,
        (packed2, field),
        second_work,
        2 * flops2,
        (early_inner, early_rest, inner, early_edges, gain_second, kernel_second, late),
    )
    before_early = onward(partial)
    (own,) = call(
        second_own_kernel,
        (shape((2, pixels2, 192), F32),),
        [],
        3 * flops2,
        (early, late, kernel_second, held, near, far, shortcut.T),
    )
    (mixed,) = call(
        weights_kernel, (shape((3, 4, 768, 192), BF16),), [], 1 << 24, (kernel_third,), after=(own,)
    )
    third_work = [pltpu.VMEM((pixels2, 192), BF16)] + work(wide2, 192)
    block = shape((rows, width, 192), BF16)
    late_out, late = call(
        late_third_kernel,
        (block, packed2),
        third_work,
        1 << 24,
        (own, before_late, gain_third),
    )
    before_late = onward(late)
    early_out, early = call(
        early_third_kernel,
        (block, packed2),
        third_work,
        1 << 24,
        (own, before_early, gain_third),
    )
    before_early = onward(early)
    own, block_out = call(
        third_own_kernel,
        (shape((2, 4, pixels, 192), F32), shape((2, rows, width, 192), BF16)),
        [pltpu.VMEM((2, 3, wide2, width, 256), BF16), dma((2,))],
        3 * flops3,
        (early, late, mixed, early_out, late_out),
        out_hbm=(1,),
    )
    last_work = [
        pltpu.VMEM((3, wide2, width, 256), BF16),
        pltpu.VMEM((2, rows, 2, 2 * width, 128), F32),
        pltpu.VMEM((2, rows, 2 * width, 192), BF16),
        dma((2,)),
    ]
    fine = shape((2, rows, 2, 2 * width, 192), BF16)
    decoded, rest = call(
        late_last_kernel,
        (fine, shape((4, pixels, 192), F32)),
        last_work,
        2 * flops3,
        (before_late, mixed, own),
        out_hbm=(0,),
    )
    (decoded,) = call(
        early_last_kernel,
        (fine,),
        last_work,
        flops3,
        (before_early, mixed, rest, decoded),
        hbm=(3,),
        out_hbm=(0,),
        aliases={3: 0},
    )
    decoded = decoded.reshape(2, 2 * rows, 2 * width, 192)
    return (block_out, decoded)


def solution(mesh):
    return jax.shard_map(
        body,
        mesh=mesh,
        in_specs=(P("tm", "rows", None, None), P(), P(), P(), P(), P(), P(), P()),
        out_specs=(P("tm", "rows", None, None), P("tm", "rows", None, None)),
        check_vma=False,
    )
```

```python
import jax
import jax.numpy as jnp
from jax import lax
from jax.experimental import pallas as pl
from jax.experimental.pallas import tpu as pltpu
from jax.sharding import PartitionSpec as P

F32 = jnp.float32
BF16 = jnp.bfloat16
HALO = 3
LIMIT = 24


def dot(a, b):
    return jnp.dot(a, b, preferred_element_type=F32)


def dot_t(a, b):
    return lax.dot_general(a, b, (((1,), (1,)), ((), ())), preferred_element_type=F32)


def spans(channels):
    return [(at, min(128, channels - at)) for at in range(0, channels, 128)]


def scales(squares, channels):
    total = dot(squares, jnp.ones((channels, 128), BF16))
    return lax.rsqrt(total * (1.0 / channels) + 1e-06)


def activated(v, scale, gain):
    u = v * scale * gain
    return u * (0.5 + 0.5 * jnp.tanh(0.5 * u))


def column_masks(width, channels):
    column = lax.broadcasted_iota(jnp.int32, (width, channels), 0)
    return column == 0, column == width - 1


def beside(v, masks):
    width = v.shape[0]
    left = jnp.where(masks[0], 0.0, pltpu.roll(v, 1, 0))
    right = jnp.where(masks[1], 0.0, pltpu.roll(v, width - 1, 0))
    return left, right


def call(kernel, out_shape, scratch, flops, args, hbm=(), out_hbm=(), aliases=None, after=()):
    vmem = pl.BlockSpec(memory_space=pltpu.VMEM)
    far = pl.BlockSpec(memory_space=pltpu.HBM)
    args = [pltpu.with_memory_space_constraint(x, pltpu.HBM) if i in hbm else x for i, x in enumerate(args)]

    count = len(args)

    def placed(*refs):
        place = [f(axis) for f in (lax.axis_index, lax.axis_size) for axis in ("tm", "rows")]
        kernel(place, *refs[:count], *refs[count + len(after) :])

    return pl.pallas_call(
        placed,
        out_shape=out_shape,
        in_specs=[far if i in hbm else vmem for i in range(count)] + [pl.BlockSpec(memory_space=pl.ANY)] * len(after),
        out_specs=tuple(far if i in out_hbm else vmem for i in range(len(out_shape))),
        scratch_shapes=scratch,
        input_output_aliases=aliases or {},
        compiler_params=pltpu.CompilerParams(vmem_limit_bytes=LIMIT << 20),
        cost_estimate=pl.CostEstimate(flops=flops, bytes_accessed=4 << 20, transcendentals=0),
    )(*args, *after)


def pack_rows(ref, rows, get):
    for row in range(0, rows, 2):
        upper, lower = get(row), get(row + 1)
        ref[row] = upper[:, 0:128].astype(BF16)
        ref[row + 1] = lower[:, 0:128].astype(BF16)
        ref[rows + row // 2] = jnp.concatenate([upper[:, 128:192], lower[:, 128:192]], axis=1).astype(BF16)


def unpack_row(ref, row):
    rows = ref.shape[0] * 2 // 3
    rest = ref[rows + row // 2].astype(F32)
    side = 64 * (row % 2)
    return jnp.concatenate([ref[row].astype(F32), rest[:, side : side + 64]], axis=1)


def fill_field(field, rows, first, rest):
    width = field.shape[2]
    masks = column_masks(width, 128)
    for row in range(rows):
        for at, part in ((0, first(row)), (128, rest(row))):
            left, right = beside(part, masks)
            for shift, value in enumerate((left, part, right)):
                field[shift, row, :, at : at + 128] = value.astype(BF16)


def packed_parts(ref, follows=None):
    rows = ref.shape[0] * 2 // 3

    def guard(value):
        value = value.astype(F32)
        return value if follows is None else jnp.where(follows, value, 0.0)

    def first(row):
        return guard(ref[row])

    def rest(row):
        at = rows + row // 2
        if row % 2 == 0:
            return guard(ref[at])
        upper = ref[at].astype(F32)[:, 64:128]
        lower = jnp.zeros_like(upper) if row == rows - 1 else ref[at + 1].astype(F32)[:, 0:64]
        return guard(jnp.concatenate([upper, lower], axis=1))

    return rows, first, rest


def row_parts(rows, get):
    made = {}

    def row_of(row):
        if row not in made:
            made[row] = get(row)
        return made[row]

    def rest(row):
        upper = row_of(row)[:, 128:192]
        lower = row_of(row + 1)[:, 128:192] if row < rows - 1 else jnp.zeros_like(upper)
        return jnp.concatenate([upper, lower], axis=1)

    return rows, lambda row: row_of(row)[:, 0:128], rest


def two_rows(field, shift, row, rows):
    pixels = rows * field.shape[2]
    return [
        field[shift, row : row + rows].reshape(pixels, 256),
        field[shift, row + 1 : row + 1 + rows, :, 0:128].reshape(pixels, 128),
    ]


def two_rows_weights(upper, lower):
    return [upper, lower[128:192], lower[0:128]]


def convolve_field(kernel, terms, rows):
    lanes, weights = [], []
    for field, a in terms:
        for e in range(3):
            lanes += two_rows(field, e, 0, rows)
            weights += two_rows_weights(kernel[a, 0, e], kernel[a, 1, e])
            lanes.append(field[e, 2 : 2 + rows].reshape(rows * field.shape[2], 256))
            weights += [kernel[a, 2, e], jnp.zeros((64, 192), BF16)]
    return dot(jnp.concatenate(lanes, axis=1), jnp.concatenate(weights, axis=0))


def convolve(acc, product, kernel, terms, rows, width):
    masks = column_masks(width, 192)
    fields = [window(b) for window, a in terms for b in range(3)]
    if product is dot_t:
        fields = [jnp.concatenate(fields, axis=1)]
    for e in range(3):
        taps = [kernel[a, b, e] for window, a in terms for b in range(3)]
        if product is dot_t:
            taps = [jnp.concatenate(taps, axis=1)]
        total = None
        for field, tap in zip(fields, taps):
            term = product(field, tap)
            total = term if total is None else total + term
        for row in range(rows):
            part = slice(row * width, (row + 1) * width)
            moved = total[part]
            if e == 0:
                acc[part] = jnp.where(masks[0], 0.0, pltpu.roll(moved, 1, 0))
            elif e == 1:
                acc[part] += moved
            else:
                acc[part] += jnp.where(masks[1], 0.0, pltpu.roll(moved, width - 1, 0))


def windows(ref, rows):
    return lambda b: ref[b : b + rows].reshape(rows * ref.shape[1], ref.shape[2])


OWN = (((0, 2),), ((0, 1), (1, 2)))


def activate_rows(ref, gain, squares, scale, out):
    rows, width, channels = ref.shape
    pixels = rows * width
    v = ref[...].astype(F32)
    squares[0:pixels] = (v * v).astype(BF16).reshape(pixels, channels)
    scale[0:pixels] = scales(squares[0:pixels], channels)
    for row in range(rows):
        part = slice(row * width, (row + 1) * width)
        for at, lanes in spans(channels):
            out[row, :, at : at + lanes] = activated(
                ref[row, :, at : at + lanes].astype(F32), scale[part], gain[at : at + lanes].reshape(1, lanes)
            ).astype(BF16)


def rim_kernel(place, latents, gain, held, held_gain, near, far, sems):
    rows = held.shape[1]
    copies = [pltpu.make_async_copy(latents.at[frame], held.at[frame], sems.at[frame]) for frame in range(2)]
    copies.append(pltpu.make_async_copy(gain, held_gain, sems.at[2]))
    for copy in copies:
        copy.start()
    odd = place[1] % 2
    for frame in range(2):
        copies[frame].wait()
        far[frame] = held[frame, pl.ds((rows - HALO) * odd, HALO)]
        near[frame] = held[frame, pl.ds((rows - HALO) * (1 - odd), HALO)]
    copies[2].wait()


def inner_kernel(place, held, gain, weights, active, packed, squares, scale, sums):
    frames, rows, width, channels = held.shape
    for frame in range(frames):
        activate_rows(held.at[frame], gain, squares, scale, active.at[frame])
    count = rows - 2
    for out, taps in ((1, ((1, 0),)), (0, ((0, 0), (1, 1)))):
        terms = [(windows(active.at[frame], count), a) for frame, a in taps]
        convolve(sums.at[out], dot_t, weights, terms, count, width)
        pack_rows(packed.at[out], count, lambda row: sums[out, row * width : (row + 1) * width])


def late_inner_own_kernel(place, active, weights, own):
    count, width = active.shape[1] - 2, active.shape[2]
    terms = [(windows(active.at[frame], count), a) for frame, a in OWN[1]]
    convolve(own, dot_t, weights, terms, count, width)


def fill_edges(place, near, far, frame, gain, active, edges, raw, squares, scale):
    odd = place[1] % 2 == 1
    inner = jnp.logical_and(place[1] > 0, place[1] < place[3] - 1)
    rows = active.shape[1]
    for row in range(HALO):
        chip = near[frame, row]
        next_chip = jnp.where(inner, far[frame, row], jnp.zeros_like(chip))
        raw[row] = jnp.where(odd, chip, next_chip)
        raw[HALO + row] = jnp.where(odd, next_chip, chip)
    activate_rows(raw.at[0:HALO], gain, squares, scale, edges.at[0, 0:HALO])
    activate_rows(raw.at[HALO : 2 * HALO], gain, squares, scale, edges.at[1, 2 : 2 + HALO])
    edges[0, HALO : HALO + 2] = active[frame, 0:2]
    edges[1, 0:2] = active[frame, rows - 2 : rows]


def edge_windows(edges):
    width, channels = edges.shape[2], edges.shape[3]
    return lambda b: edges[:, b : b + HALO].reshape(2 * HALO * width, channels)


def pack_edges(partial, acc, width):
    pack_rows(partial, 2 * HALO, lambda row: acc[row * width : (row + 1) * width])


def late_edge_kernel(place, near, far, gain, active, weights, partial, edges, acc, raw, squares, scale):
    fill_edges(place, near, far, 1, gain, active, edges, raw, squares, scale)
    width = active.shape[2]
    convolve(acc, dot_t, weights, [(edge_windows(edges), 0)], 2 * HALO, width)
    pack_edges(partial, acc, width)


def early_edge_kernel(
    place, near, far, gain, active, weights, late, partial, edges, acc, raw, squares, scale
):
    fill_edges(place, near, far, 0, gain, active, edges, raw, squares, scale)
    width = active.shape[2]
    convolve(acc, dot_t, weights, [(edge_windows(edges), 0), (edge_windows(late), 1)], 2 * HALO, width)
    pack_edges(partial, acc, width)


def late_edge_own_kernel(place, early, late, weights, own):
    terms = [(edge_windows((early, late)[frame]), a) for frame, a in OWN[1]]
    convolve(own, dot_t, weights, terms, 2 * HALO, early.shape[2])


def early_own_kernel(place, active, early, weights, inner, edges):
    count, width = active.shape[1] - 2, active.shape[2]
    (frame, a), = OWN[0]
    convolve(inner, dot_t, weights, [(windows(active.at[frame], count), a)], count, width)
    convolve(edges, dot_t, weights, [(edge_windows(early), a)], 2 * HALO, width)


def finish(place, own, before, gain, raw, squares, scale, keep):
    before, tall, width = before
    start = place[1] * 8 - (tall - 8) // 2
    follows = place[0] > 0
    for row in range(tall):
        part = slice(row * width, (row + 1) * width)
        earlier = jnp.where(follows, before(row), 0.0)
        total = (own(row) + earlier).astype(BF16)
        raw[part] = total
        keep(row, total)
        total = total.astype(F32)
        squares[part] = (total * total).astype(BF16)
    scale[...] = scales(squares[...], 192)

    def get(row):
        part = slice(row * width, (row + 1) * width)
        inside = jnp.logical_and(start + row >= 0, start + row < place[3] * 8)
        lanes = []
        for at, count in spans(192):
            v = activated(
                raw[part, at : at + count].astype(F32), scale[part, 0:count], gain[at : at + count].reshape(1, count)
            )
            if not (tall - 8) // 2 <= row < (tall + 8) // 2:
                v = jnp.where(inside, v, 0.0)
            lanes.append(v)
        return jnp.concatenate(lanes, axis=1)

    return get


def second(place, own, before, gain, kernel, terms, partial, field, raw, squares, scale):
    rows = field.shape[1]
    width, wide = field.shape[2], rows - 2
    get = finish(place, own, before, gain, raw, squares, scale, lambda row, total: None)
    fill_field(field, *row_parts(rows, get))
    total = convolve_field(kernel, terms, wide)
    pack_rows(partial, wide, lambda row: total[row * width : (row + 1) * width])


def joined(inner, edges):
    count = inner.shape[0] * 2 // 3

    def get(row):
        if HALO <= row < HALO + count:
            return unpack_row(inner, row - HALO)
        return unpack_row(edges, row if row < HALO else row - count)

    return get, count + 2 * HALO, inner.shape[1]


def whole(packed):
    return lambda row: unpack_row(packed, row), packed.shape[0] * 2 // 3, packed.shape[1]


def joined_own(inner, edges, width):
    count = inner.shape[0] // width

    def get(row):
        ref, at = (inner, row - HALO) if HALO <= row < HALO + count else (edges, row if row < HALO else row - count)
        return ref[at * width : (at + 1) * width]

    return get


def rows_of(own, width):
    return lambda row: own[row * width : (row + 1) * width]


def late_second_kernel(
    place, own_inner, own_edges, inner, edges, gain, kernel, partial, field, raw, squares, scale
):
    before = joined(inner.at[1], edges)
    own = joined_own(own_inner, own_edges, field.shape[2])
    second(place, own, before, gain, kernel, [(field, 0)], partial, field, raw, squares, scale)


def early_second_kernel(
    place, own_inner, own_edges, inner, edges, gain, kernel, late, partial, field, raw, squares, scale
):
    before = joined(inner.at[0], edges)
    own = joined_own(own_inner, own_edges, field.shape[2])
    second(place, own, before, gain, kernel, [(field, 0), (late, 1)], partial, field, raw, squares, scale)


def second_own_kernel(place, early, late, kernel, latents, near, far, shortcut, own):
    wide, width = early.shape[1] - 2, early.shape[2]
    pixels = wide * width
    rows, channels = latents.shape[1], latents.shape[3]
    odd = place[1] % 2
    inner = wide - 1
    fields = (early, late)
    for out in (1, 0):
        own[out] = convolve_field(kernel, [(fields[frame], a) for frame, a in OWN[out]], wide)
        body = latents[out].reshape(rows * width, channels)
        own[out, width : pixels - width] += dot_t(body, shortcut[...])
        other = dot_t(near[out, jnp.where(odd == 1, HALO - 1, 0)], shortcut[...])
        own[out, pl.ds(jnp.where(odd == 1, 0, inner * width), width)] += other
        other = dot_t(far[out, jnp.where(odd == 1, 0, HALO - 1)], shortcut[...])
        own[out, pl.ds(jnp.where(odd == 1, inner * width, 0), width)] += other


def third(place, own, before, gain, block, packed, raw, squares, scale):
    tall = packed.shape[0] * 2 // 3

    def keep(row, total):
        if 0 < row < tall - 1:
            block[row - 1] = total

    own = rows_of(own, packed.shape[1])
    pack_rows(packed, tall, finish(place, own, whole(before), gain, raw, squares, scale, keep))


def late_third_kernel(place, own, before, gain, block, packed, raw, squares, scale):
    third(place, own.at[1], before, gain, block, packed, raw, squares, scale)


def early_third_kernel(place, own, before, gain, block, packed, raw, squares, scale):
    third(place, own.at[0], before, gain, block, packed, raw, squares, scale)


def weights_kernel(place, kernel, out):
    def halves(taps, parity):
        if parity == 0:
            return taps[0], taps[1] + taps[2]
        return taps[0] + taps[1], taps[2]

    for a in range(3):
        for i in range(2):
            rows = [halves([kernel[a, b, e].astype(F32) for b in range(3)], i) for e in range(3)]
            for j in range(2):
                upper = halves([rows[e][0] for e in range(3)], j)
                lower = halves([rows[e][1] for e in range(3)], j)
                for column in range(2):
                    at = 384 * column
                    for part in two_rows_weights(upper[column].astype(BF16), lower[column].astype(BF16)):
                        out[a, 2 * i + j, at : at + part.shape[0]] = part
                        at += part.shape[0]


def phase(terms, kernel, i, j, rows):
    lanes, weights = [], []
    for field, a in terms:
        for shift in (j, j + 1):
            lanes += two_rows(field, shift, i, rows)
        weights.append(kernel[a, 2 * i + j])
    return dot(jnp.concatenate(lanes, axis=1), jnp.concatenate(weights, axis=0))


def third_own_kernel(place, early, late, kernel, early_out, late_out, own, block_out, fields, sems):
    copies = [
        pltpu.make_async_copy(block, block_out.at[frame], sems.at[frame])
        for frame, block in enumerate((early_out, late_out))
    ]
    for copy in copies:
        copy.start()
    for frame, packed in enumerate((early, late)):
        fill_field(fields.at[frame], *packed_parts(packed))
    rows = early_out.shape[0]
    for out in (1, 0):
        terms = [(fields.at[frame], a) for frame, a in OWN[out]]
        for i in range(2):
            for j in range(2):
                own[out, 2 * i + j] = phase(terms, kernel, i, j, rows)
    for copy in copies:
        copy.wait()


def weave(total, j, rows, width, woven):
    for row in range(rows):
        value = total[row * width : (row + 1) * width]
        woven[row, 0, pl.ds(j, width, stride=2)] = value[:, 0:128]
        woven[row, 1, pl.ds(j, width, stride=2), 0:64] = value[:, 128:192]


def write_out(own, field, kernel, a, rows, width, woven, fine, out, sems):
    copies = []
    for i in range(2):
        for j in range(2):
            total = own[2 * i + j] + phase([(field, a)], kernel, i, j, rows)
            weave(total, j, rows, width, woven.at[i])
        for row in range(rows):
            fine[i, row, :, 0:128] = woven[i, row, 0].astype(BF16)
            fine[i, row, :, 128:192] = woven[i, row, 1, :, 0:64].astype(BF16)
        copies.append(pltpu.make_async_copy(fine.at[i], out.at[:, i], sems.at[i]))
        copies[-1].start()
    return copies


def late_last_kernel(place, packed, kernel, own, decoded, rest, field, woven, fine, sems):
    rows, width = packed.shape[0] * 2 // 3 - 2, packed.shape[1]
    fill_field(field, *packed_parts(packed, place[0] > 0))
    copies = write_out(own.at[1], field, kernel, 0, rows, width, woven, fine, decoded.at[1], sems)
    for i in range(2):
        for j in range(2):
            rest[2 * i + j] = own[0, 2 * i + j] + phase([(field, 1)], kernel, i, j, rows)
    for copy in copies:
        copy.wait()


def early_last_kernel(place, packed, kernel, rest, late, decoded, field, woven, fine, sems):
    rows, width = packed.shape[0] * 2 // 3 - 2, packed.shape[1]
    fill_field(field, *packed_parts(packed, place[0] > 0))
    for copy in write_out(rest, field, kernel, 0, rows, width, woven, fine, decoded.at[0], sems):
        copy.wait()


def onward(value):
    count = lax.axis_size("tm")
    return lax.ppermute(value, "tm", [(i, (i + 1) % count) for i in range(count)])


def swap(value, offset):
    groups, slabs = lax.axis_size("tm"), lax.axis_size("rows")
    pairs = [(g * slabs + i, g * slabs + i + 1) for g in range(groups) for i in range(offset, slabs - 1, 2)]
    if offset:
        pairs += [(g * slabs + i, (g + 1) * slabs + i) for g in range(0, groups - 1, 2) for i in (0, slabs - 1)]
    alone = set(range(groups * slabs)) - {i for pair in pairs for i in pair}
    return lax.ppermute(
        value, ("tm", "rows"), pairs + [(b, a) for a, b in pairs] + [(i, i) for i in sorted(alone)]
    )


def body(
    latents,
    gain_first,
    kernel_first,
    gain_second,
    kernel_second,
    shortcut,
    gain_third,
    kernel_third,
):
    frames, rows, width, channels = latents.shape
    shape = jax.ShapeDtypeStruct
    shape = jax.ShapeDtypeStruct
    odd = lax.axis_index("rows") % 2
    near = lax.dynamic_slice_in_dim(latents, (rows - HALO) * (1 - odd), HALO, 1)
    far = lax.dynamic_slice_in_dim(latents, (rows - HALO) * odd, HALO, 1)
    near, far = swap(near, 0), swap(far, 1)

    wide1, wide2 = rows + 4, rows + 2
    pixels, pixels1, pixels2 = rows * width, wide1 * width, wide2 * width
    flops1, flops2, flops3 = (18 * n * 192 for n in (pixels1 * channels, pixels2 * 192, pixels * 192))
    dma = pltpu.SemaphoreType.DMA

    def work(tall, channels):
        return [pltpu.VMEM((tall * width, channels), BF16), pltpu.VMEM((tall * width, 128), F32)]

    rim = shape((frames, HALO, width, channels), BF16)
    held, gain_first, near, far = call(
        rim_kernel,
        (shape(latents.shape, BF16), shape((channels,), F32), rim, rim),
        [dma((3,))],
        1 << 34,
        (latents, gain_first),
        hbm=(0, 1),
    )
    far, near = swap(far, 1), swap(near, 0)
    inner_rows = rows - 2
    inner_pixels = inner_rows * width
    across = jnp.swapaxes(kernel_first, 3, 4)
    active, inner = call(
        inner_kernel,
        (
            shape(latents.shape, BF16),
            shape((2, inner_rows * 3 // 2, width, 128), BF16),
        ),
        work(rows, channels) + [pltpu.VMEM((2, inner_pixels, 192), F32)],
        2 * flops1,
        (held, gain_first, across),
    )
    inner = onward(inner)
    (late_inner,) = call(
        late_inner_own_kernel, (shape((inner_pixels, 192), F32),), [], flops1, (active, across)
    )
    edge_sums = shape((2 * HALO * width, 192), F32)
    edge_work = [pltpu.VMEM(edge_sums.shape, F32), pltpu.VMEM((2 * HALO, width, channels), BF16)]
    edge_work += work(HALO, channels)
    ends = shape((2, HALO + 2, width, channels), BF16)
    packed1 = shape((HALO * 3, width, 128), BF16)
    partial, late = call(
        late_edge_kernel,
        (packed1, ends),
        edge_work,
        flops1 // 2,
        (near, far, gain_first, active, across),
        after=(late_inner,),
    )
    late_edges = onward(partial)
    partial, early = call(
        early_edge_kernel,
        (packed1, ends),
        edge_work,
        flops1,
        (near, far, gain_first, active, across, late),
        after=(partial,),
    )
    early_edges = onward(partial)
    (late_rest,) = call(late_edge_own_kernel, (edge_sums,), [], flops1, (early, late, across))
    second_work = [pltpu.VMEM((pixels1, 192), BF16)] + work(wide1, 192)
    packed2 = shape((wide2 * 3 // 2, width, 128), BF16)
    field = shape((3, wide1, width, 256), BF16)
    early_inner, early_rest = call(
        early_own_kernel,
        (shape((inner_pixels, 192), F32), edge_sums),
        [],
        flops1,
        (active, early, across),
        after=(late_rest,),
    )
    partial, late = call(
        late_second_kernel,
        (packed2, field),
        second_work,
        flops2,
        (late_inner, late_rest, inner, late_edges, gain_second, kernel_second),
        after=(early_rest,),
    )
    before_late = onward(partial)
    partial, early = call(
        early_second_kernel,
        (packed2, field),
        second_work,
        2 * flops2,
        (early_inner, early_rest, inner, early_edges, gain_second, kernel_second, late),
    )
    before_early = onward(partial)
    (own,) = call(
        second_own_kernel,
        (shape((2, pixels2, 192), F32),),
        [],
        3 * flops2,
        (early, late, kernel_second, held, near, far, shortcut.T),
    )
    (mixed,) = call(
        weights_kernel, (shape((3, 4, 768, 192), BF16),), [], 1 << 24, (kernel_third,), after=(own,)
    )
    third_work = [pltpu.VMEM((pixels2, 192), BF16)] + work(wide2, 192)
    block = shape((rows, width, 192), BF16)
    late_out, late = call(
        late_third_kernel,
        (block, packed2),
        third_work,
        1 << 24,
        (own, before_late, gain_third),
    )
    before_late = onward(late)
    early_out, early = call(
        early_third_kernel,
        (block, packed2),
        third_work,
        1 << 24,
        (own, before_early, gain_third),
        after=(mixed,),
    )
    before_early = onward(early)
    own, block_out = call(
        third_own_kernel,
        (shape((2, 4, pixels, 192), F32), shape((2, rows, width, 192), BF16)),
        [pltpu.VMEM((2, 3, wide2, width, 256), BF16), dma((2,))],
        3 * flops3,
        (early, late, mixed, early_out, late_out),
        out_hbm=(1,),
    )
    last_work = [
        pltpu.VMEM((3, wide2, width, 256), BF16),
        pltpu.VMEM((2, rows, 2, 2 * width, 128), F32),
        pltpu.VMEM((2, rows, 2 * width, 192), BF16),
        dma((2,)),
    ]
    fine = shape((2, rows, 2, 2 * width, 192), BF16)
    decoded, rest = call(
        late_last_kernel,
        (fine, shape((4, pixels, 192), F32)),
        last_work,
        2 * flops3,
        (before_late, mixed, own),
        out_hbm=(0,),
    )
    (decoded,) = call(
        early_last_kernel,
        (fine,),
        last_work,
        flops3,
        (before_early, mixed, rest, decoded),
        hbm=(3,),
        out_hbm=(0,),
        aliases={3: 0},
    )
    decoded = decoded.reshape(2, 2 * rows, 2 * width, 192)
    return (block_out, decoded)


def solution(mesh):
    return jax.shard_map(
        body,
        mesh=mesh,
        in_specs=(P("tm", "rows", None, None), P(), P(), P(), P(), P(), P(), P()),
        out_specs=(P("tm", "rows", None, None), P("tm", "rows", None, None)),
        check_vma=False,
    )
```

```python
import jax
import jax.numpy as jnp
from jax import lax
from jax.experimental import pallas as pl
from jax.experimental.pallas import tpu as pltpu
from jax.sharding import PartitionSpec as P

F32 = jnp.float32
BF16 = jnp.bfloat16
HALO = 3
LIMIT = 24


def dot(a, b):
    return jnp.dot(a, b, preferred_element_type=F32)


def dot_t(a, b):
    return lax.dot_general(a, b, (((1,), (1,)), ((), ())), preferred_element_type=F32)


def spans(channels):
    return [(at, min(128, channels - at)) for at in range(0, channels, 128)]


def scales(squares, channels):
    total = dot(squares, jnp.ones((channels, 128), BF16))
    return lax.rsqrt(total * (1.0 / channels) + 1e-06)


def activated(v, scale, gain):
    u = v * scale * gain
    return u * (0.5 + 0.5 * jnp.tanh(0.5 * u))


def column_masks(width, channels):
    column = lax.broadcasted_iota(jnp.int32, (width, channels), 0)
    return column == 0, column == width - 1


def beside(v, masks):
    width = v.shape[0]
    left = jnp.where(masks[0], 0.0, pltpu.roll(v, 1, 0))
    right = jnp.where(masks[1], 0.0, pltpu.roll(v, width - 1, 0))
    return left, right


def call(kernel, out_shape, scratch, flops, args, hbm=(), out_hbm=(), aliases=None, after=()):
    vmem = pl.BlockSpec(memory_space=pltpu.VMEM)
    far = pl.BlockSpec(memory_space=pltpu.HBM)
    args = [pltpu.with_memory_space_constraint(x, pltpu.HBM) if i in hbm else x for i, x in enumerate(args)]

    count = len(args)

    def placed(*refs):
        place = [f(axis) for f in (lax.axis_index, lax.axis_size) for axis in ("tm", "rows")]
        kernel(place, *refs[:count], *refs[count + len(after) :])

    return pl.pallas_call(
        placed,
        out_shape=out_shape,
        in_specs=[far if i in hbm else vmem for i in range(count)] + [pl.BlockSpec(memory_space=pl.ANY)] * len(after),
        out_specs=tuple(far if i in out_hbm else vmem for i in range(len(out_shape))),
        scratch_shapes=scratch,
        input_output_aliases=aliases or {},
        compiler_params=pltpu.CompilerParams(vmem_limit_bytes=LIMIT << 20),
        cost_estimate=pl.CostEstimate(flops=flops, bytes_accessed=4 << 20, transcendentals=0),
    )(*args, *after)


def pack_rows(ref, rows, get):
    for row in range(0, rows, 2):
        upper, lower = get(row), get(row + 1)
        ref[row] = upper[:, 0:128].astype(BF16)
        ref[row + 1] = lower[:, 0:128].astype(BF16)
        ref[rows + row // 2] = jnp.concatenate([upper[:, 128:192], lower[:, 128:192]], axis=1).astype(BF16)


def unpack_row(ref, row):
    rows = ref.shape[0] * 2 // 3
    rest = ref[rows + row // 2].astype(F32)
    side = 64 * (row % 2)
    return jnp.concatenate([ref[row].astype(F32), rest[:, side : side + 64]], axis=1)


def fill_field(field, rows, first, rest):
    width = field.shape[2]
    masks = column_masks(width, 128)
    for row in range(rows):
        for at, part in ((0, first(row)), (128, rest(row))):
            left, right = beside(part, masks)
            for shift, value in enumerate((left, part, right)):
                field[shift, row, :, at : at + 128] = value.astype(BF16)


def packed_parts(ref, follows=None):
    rows = ref.shape[0] * 2 // 3

    def guard(value):
        value = value.astype(F32)
        return value if follows is None else jnp.where(follows, value, 0.0)

    def first(row):
        return guard(ref[row])

    def rest(row):
        at = rows + row // 2
        if row % 2 == 0:
            return guard(ref[at])
        upper = ref[at].astype(F32)[:, 64:128]
        lower = jnp.zeros_like(upper) if row == rows - 1 else ref[at + 1].astype(F32)[:, 0:64]
        return guard(jnp.concatenate([upper, lower], axis=1))

    return rows, first, rest


def row_parts(rows, get):
    made = {}

    def row_of(row):
        if row not in made:
            made[row] = get(row)
        return made[row]

    def rest(row):
        upper = row_of(row)[:, 128:192]
        lower = row_of(row + 1)[:, 128:192] if row < rows - 1 else jnp.zeros_like(upper)
        return jnp.concatenate([upper, lower], axis=1)

    return rows, lambda row: row_of(row)[:, 0:128], rest


def two_rows(field, shift, row, rows):
    pixels = rows * field.shape[2]
    return [
        field[shift, row : row + rows].reshape(pixels, 256),
        field[shift, row + 1 : row + 1 + rows, :, 0:128].reshape(pixels, 128),
    ]


def two_rows_weights(upper, lower):
    return [upper, lower[128:192], lower[0:128]]


def convolve_field(kernel, terms, rows):
    lanes, weights = [], []
    for field, a in terms:
        for e in range(3):
            lanes += two_rows(field, e, 0, rows)
            weights += two_rows_weights(kernel[a, 0, e], kernel[a, 1, e])
            lanes.append(field[e, 2 : 2 + rows].reshape(rows * field.shape[2], 256))
            weights += [kernel[a, 2, e], jnp.zeros((64, 192), BF16)]
    return dot(jnp.concatenate(lanes, axis=1), jnp.concatenate(weights, axis=0))


def convolve(acc, product, kernel, terms, rows, width):
    masks = column_masks(width, 192)
    fields = [window(b) for window, a in terms for b in range(3)]
    if product is dot_t:
        fields = [jnp.concatenate(fields, axis=1)]
    for e in range(3):
        taps = [kernel[a, b, e] for window, a in terms for b in range(3)]
        if product is dot_t:
            taps = [jnp.concatenate(taps, axis=1)]
        total = None
        for field, tap in zip(fields, taps):
            term = product(field, tap)
            total = term if total is None else total + term
        for row in range(rows):
            part = slice(row * width, (row + 1) * width)
            moved = total[part]
            if e == 0:
                acc[part] = jnp.where(masks[0], 0.0, pltpu.roll(moved, 1, 0))
            elif e == 1:
                acc[part] += moved
            else:
                acc[part] += jnp.where(masks[1], 0.0, pltpu.roll(moved, width - 1, 0))


def windows(ref, rows):
    return lambda b: ref[b : b + rows].reshape(rows * ref.shape[1], ref.shape[2])


OWN = (((0, 2),), ((0, 1), (1, 2)))


def activate_rows(fields, gain, squares, scale, put):
    rows, width, channels = fields[0].shape
    pixels = rows * width
    for i, ref in enumerate(fields):
        v = ref[...].astype(F32)
        squares[i * pixels : (i + 1) * pixels] = (v * v).astype(BF16).reshape(pixels, channels)
    every = len(fields) * pixels
    scale[0:every] = scales(squares[0:every], channels)
    for i, ref in enumerate(fields):
        for row in range(rows):
            part = slice(i * pixels + row * width, i * pixels + (row + 1) * width)
            for at, lanes in spans(channels):
                v = activated(
                    ref[row, :, at : at + lanes].astype(F32),
                    scale[part],
                    gain[at : at + lanes].reshape(1, lanes),
                )
                put(i, row, slice(at, at + lanes), v.astype(BF16))


def rim_kernel(place, latents, gain, held, held_gain, near, far, sems):
    rows = held.shape[1]
    copies = [pltpu.make_async_copy(latents.at[frame], held.at[frame], sems.at[frame]) for frame in range(2)]
    copies.append(pltpu.make_async_copy(gain, held_gain, sems.at[2]))
    for copy in copies:
        copy.start()
    odd = place[1] % 2
    for frame in range(2):
        copies[frame].wait()
        far[frame] = held[frame, pl.ds((rows - HALO) * odd, HALO)]
        near[frame] = held[frame, pl.ds((rows - HALO) * (1 - odd), HALO)]
    copies[2].wait()


def inner_kernel(place, held, gain, weights, active, packed, squares, scale, sums):
    frames, rows, width, channels = held.shape

    def put(frame, row, lanes, value):
        active[frame, row, :, lanes] = value

    for frame in range(frames):
        activate_rows(
            [held.at[frame]], gain, squares, scale, lambda _, *args, frame=frame: put(frame, *args)
        )
    count = rows - 2
    for out, taps in ((1, ((1, 0),)), (0, ((0, 0), (1, 1)))):
        terms = [(windows(active.at[frame], count), a) for frame, a in taps]
        convolve(sums.at[out], dot_t, weights, terms, count, width)
        pack_rows(packed.at[out], count, lambda row: sums[out, row * width : (row + 1) * width])


def late_inner_own_kernel(place, active, weights, own):
    count, width = active.shape[1] - 2, active.shape[2]
    terms = [(windows(active.at[frame], count), a) for frame, a in OWN[1]]
    convolve(own, dot_t, weights, terms, count, width)


def fill_edges(place, near, far, frame, gain, active, edges, raw, squares, scale):
    odd = place[1] % 2 == 1
    inner = jnp.logical_and(place[1] > 0, place[1] < place[3] - 1)
    rows = active.shape[1]
    for row in range(HALO):
        chip = near[frame, row]
        next_chip = jnp.where(inner, far[frame, row], jnp.zeros_like(chip))
        raw[row] = jnp.where(odd, chip, next_chip)
        raw[HALO + row] = jnp.where(odd, next_chip, chip)

    def put(_, row, lanes, value):
        side, at = divmod(row, HALO)
        edges[side, at + 2 * side, :, lanes] = value

    activate_rows([raw], gain, squares, scale, put)
    edges[0, HALO : HALO + 2] = active[frame, 0:2]
    edges[1, 0:2] = active[frame, rows - 2 : rows]


def edge_windows(edges):
    width, channels = edges.shape[2], edges.shape[3]
    return lambda b: edges[:, b : b + HALO].reshape(2 * HALO * width, channels)


def pack_edges(partial, acc, width):
    pack_rows(partial, 2 * HALO, lambda row: acc[row * width : (row + 1) * width])


def late_edge_kernel(place, near, far, gain, active, weights, partial, edges, acc, raw, squares, scale):
    fill_edges(place, near, far, 1, gain, active, edges, raw, squares, scale)
    width = active.shape[2]
    convolve(acc, dot_t, weights, [(edge_windows(edges), 0)], 2 * HALO, width)
    pack_edges(partial, acc, width)


def early_edge_kernel(
    place, near, far, gain, active, weights, late, partial, edges, acc, raw, squares, scale
):
    fill_edges(place, near, far, 0, gain, active, edges, raw, squares, scale)
    width = active.shape[2]
    convolve(acc, dot_t, weights, [(edge_windows(edges), 0), (edge_windows(late), 1)], 2 * HALO, width)
    pack_edges(partial, acc, width)


def late_edge_own_kernel(place, early, late, weights, own):
    terms = [(edge_windows((early, late)[frame]), a) for frame, a in OWN[1]]
    convolve(own, dot_t, weights, terms, 2 * HALO, early.shape[2])


def early_own_kernel(place, active, early, weights, own, tall):
    rows, width = active.shape[1], active.shape[2]
    tall[0:HALO] = early[0, 0:HALO]
    tall[HALO : HALO + rows] = active[0]
    tall[HALO + rows :] = early[1, 2:]
    (frame, a), = OWN[0]
    convolve(own, dot_t, weights, [(windows(tall, rows + 4), a)], rows + 4, width)


def finish(place, own, before, gain, raw, squares, scale, keep):
    before, tall, width = before
    start = place[1] * 8 - (tall - 8) // 2
    follows = place[0] > 0
    for row in range(tall):
        part = slice(row * width, (row + 1) * width)
        earlier = jnp.where(follows, before(row), 0.0)
        total = (own(row) + earlier).astype(BF16)
        raw[part] = total
        keep(row, total)
        total = total.astype(F32)
        squares[part] = (total * total).astype(BF16)
    scale[...] = scales(squares[...], 192)

    def get(row):
        part = slice(row * width, (row + 1) * width)
        inside = jnp.logical_and(start + row >= 0, start + row < place[3] * 8)
        lanes = []
        for at, count in spans(192):
            v = activated(
                raw[part, at : at + count].astype(F32), scale[part, 0:count], gain[at : at + count].reshape(1, count)
            )
            if not (tall - 8) // 2 <= row < (tall + 8) // 2:
                v = jnp.where(inside, v, 0.0)
            lanes.append(v)
        return jnp.concatenate(lanes, axis=1)

    return get


def second(place, own, before, gain, kernel, terms, partial, field, raw, squares, scale):
    rows = field.shape[1]
    width, wide = field.shape[2], rows - 2
    get = finish(place, own, before, gain, raw, squares, scale, lambda row, total: None)
    fill_field(field, *row_parts(rows, get))
    total = convolve_field(kernel, terms, wide)
    pack_rows(partial, wide, lambda row: total[row * width : (row + 1) * width])


def joined(inner, edges):
    count = inner.shape[0] * 2 // 3

    def get(row):
        if HALO <= row < HALO + count:
            return unpack_row(inner, row - HALO)
        return unpack_row(edges, row if row < HALO else row - count)

    return get, count + 2 * HALO, inner.shape[1]


def whole(packed):
    return lambda row: unpack_row(packed, row), packed.shape[0] * 2 // 3, packed.shape[1]


def joined_own(inner, edges, width):
    count = inner.shape[0] // width

    def get(row):
        ref, at = (inner, row - HALO) if HALO <= row < HALO + count else (edges, row if row < HALO else row - count)
        return ref[at * width : (at + 1) * width]

    return get


def rows_of(own, width):
    return lambda row: own[row * width : (row + 1) * width]


def late_second_kernel(
    place, own_inner, own_edges, inner, edges, gain, kernel, partial, field, raw, squares, scale
):
    before = joined(inner.at[1], edges)
    own = joined_own(own_inner, own_edges, field.shape[2])
    second(place, own, before, gain, kernel, [(field, 0)], partial, field, raw, squares, scale)


def early_second_kernel(
    place, own, inner, edges, gain, kernel, late, partial, field, raw, squares, scale
):
    before = joined(inner.at[0], edges)
    own = rows_of(own, field.shape[2])
    second(place, own, before, gain, kernel, [(field, 0), (late, 1)], partial, field, raw, squares, scale)


def second_own_kernel(place, early, late, kernel, latents, near, far, shortcut, own):
    wide, width = early.shape[1] - 2, early.shape[2]
    pixels = wide * width
    rows, channels = latents.shape[1], latents.shape[3]
    odd = place[1] % 2
    inner = wide - 1
    fields = (early, late)
    for out in (1, 0):
        own[out] = convolve_field(kernel, [(fields[frame], a) for frame, a in OWN[out]], wide)
        body = latents[out].reshape(rows * width, channels)
        own[out, width : pixels - width] += dot_t(body, shortcut[...])
        other = dot_t(near[out, jnp.where(odd == 1, HALO - 1, 0)], shortcut[...])
        own[out, pl.ds(jnp.where(odd == 1, 0, inner * width), width)] += other
        other = dot_t(far[out, jnp.where(odd == 1, 0, HALO - 1)], shortcut[...])
        own[out, pl.ds(jnp.where(odd == 1, inner * width, 0), width)] += other


def third(place, own, before, gain, block, packed, raw, squares, scale):
    tall = packed.shape[0] * 2 // 3

    def keep(row, total):
        if 0 < row < tall - 1:
            block[row - 1] = total

    own = rows_of(own, packed.shape[1])
    pack_rows(packed, tall, finish(place, own, whole(before), gain, raw, squares, scale, keep))


def late_third_kernel(place, own, before, gain, block, packed, raw, squares, scale):
    third(place, own.at[1], before, gain, block, packed, raw, squares, scale)


def early_third_kernel(place, own, before, gain, block, packed, raw, squares, scale):
    third(place, own.at[0], before, gain, block, packed, raw, squares, scale)


def weights_kernel(place, kernel, out):
    def halves(taps, parity):
        if parity == 0:
            return taps[0], taps[1] + taps[2]
        return taps[0] + taps[1], taps[2]

    for a in range(3):
        for i in range(2):
            rows = [halves([kernel[a, b, e] for b in range(3)], i) for e in range(3)]
            for j in range(2):
                upper = halves([rows[e][0] for e in range(3)], j)
                lower = halves([rows[e][1] for e in range(3)], j)
                for column in range(2):
                    at = 384 * column
                    for part in two_rows_weights(upper[column], lower[column]):
                        out[a, 2 * i + j, at : at + part.shape[0]] = part
                        at += part.shape[0]


def phase(terms, kernel, i, j, rows):
    lanes, weights = [], []
    for field, a in terms:
        for shift in (j, j + 1):
            lanes += two_rows(field, shift, i, rows)
        weights.append(kernel[a, 2 * i + j])
    return dot(jnp.concatenate(lanes, axis=1), jnp.concatenate(weights, axis=0))


def third_own_kernel(place, early, late, kernel, early_out, late_out, own, block_out, fields, sems):
    copies = [
        pltpu.make_async_copy(block, block_out.at[frame], sems.at[frame])
        for frame, block in enumerate((early_out, late_out))
    ]
    for copy in copies:
        copy.start()
    for frame, packed in enumerate((early, late)):
        fill_field(fields.at[frame], *packed_parts(packed))
    rows = early_out.shape[0]
    for out in (1, 0):
        terms = [(fields.at[frame], a) for frame, a in OWN[out]]
        for i in range(2):
            for j in range(2):
                own[out, 2 * i + j] = phase(terms, kernel, i, j, rows)
    for copy in copies:
        copy.wait()


def weave(total, j, rows, width, woven):
    for row in range(rows):
        value = total[row * width : (row + 1) * width]
        woven[row, 0, pl.ds(j, width, stride=2)] = value[:, 0:128]
        woven[row, 1, pl.ds(j, width, stride=2), 0:64] = value[:, 128:192]


def write_out(own, field, kernel, a, rows, width, woven, fine, out, sems):
    copies = []
    for i in range(2):
        for j in range(2):
            total = own[2 * i + j] + phase([(field, a)], kernel, i, j, rows)
            weave(total, j, rows, width, woven.at[i])
        for row in range(rows):
            fine[i, row, :, 0:128] = woven[i, row, 0].astype(BF16)
            fine[i, row, :, 128:192] = woven[i, row, 1, :, 0:64].astype(BF16)
            if row % 2:
                part = slice(row - 1, row + 1)
                copies.append(pltpu.make_async_copy(fine.at[i, part], out.at[part, i], sems.at[i, row // 2]))
                copies[-1].start()
    return copies


def late_last_kernel(place, packed, kernel, own, decoded, rest, field, woven, fine, sems):
    rows, width = packed.shape[0] * 2 // 3 - 2, packed.shape[1]
    fill_field(field, *packed_parts(packed, place[0] > 0))
    copies = write_out(own.at[1], field, kernel, 0, rows, width, woven, fine, decoded.at[1], sems)
    for i in range(2):
        for j in range(2):
            rest[2 * i + j] = own[0, 2 * i + j] + phase([(field, 1)], kernel, i, j, rows)
    for copy in copies:
        copy.wait()


def early_last_kernel(place, packed, kernel, rest, late, decoded, field, woven, fine, sems):
    rows, width = packed.shape[0] * 2 // 3 - 2, packed.shape[1]
    fill_field(field, *packed_parts(packed, place[0] > 0))
    for copy in write_out(rest, field, kernel, 0, rows, width, woven, fine, decoded.at[0], sems):
        copy.wait()


def onward_open(value):
    count = lax.axis_size("tm")
    return lax.ppermute(value, "tm", [(i, i + 1) for i in range(count - 1)])


def onward(value):
    count = lax.axis_size("tm")
    return lax.ppermute(value, "tm", [(i, (i + 1) % count) for i in range(count)])


def swap(value, offset):
    groups, slabs = lax.axis_size("tm"), lax.axis_size("rows")
    pairs = [(g * slabs + i, g * slabs + i + 1) for g in range(groups) for i in range(offset, slabs - 1, 2)]
    if offset:
        pairs += [(g * slabs + i, (g + 1) * slabs + i) for g in range(0, groups - 1, 2) for i in (0, slabs - 1)]
    alone = set(range(groups * slabs)) - {i for pair in pairs for i in pair}
    return lax.ppermute(
        value, ("tm", "rows"), pairs + [(b, a) for a, b in pairs] + [(i, i) for i in sorted(alone)]
    )


def body(
    latents,
    gain_first,
    kernel_first,
    gain_second,
    kernel_second,
    shortcut,
    gain_third,
    kernel_third,
):
    frames, rows, width, channels = latents.shape
    shape = jax.ShapeDtypeStruct
    shape = jax.ShapeDtypeStruct
    odd = lax.axis_index("rows") % 2
    near = lax.dynamic_slice_in_dim(latents, (rows - HALO) * (1 - odd), HALO, 1)
    far = lax.dynamic_slice_in_dim(latents, (rows - HALO) * odd, HALO, 1)
    near, far = swap(near, 0), swap(far, 1)

    wide1, wide2 = rows + 4, rows + 2
    pixels, pixels1, pixels2 = rows * width, wide1 * width, wide2 * width
    flops1, flops2, flops3 = (18 * n * 192 for n in (pixels1 * channels, pixels2 * 192, pixels * 192))
    dma = pltpu.SemaphoreType.DMA

    def work(tall, channels):
        return [pltpu.VMEM((tall * width, channels), BF16), pltpu.VMEM((tall * width, 128), F32)]

    rim = shape((frames, HALO, width, channels), BF16)
    held, gain_first, near, far = call(
        rim_kernel,
        (shape(latents.shape, BF16), shape((channels,), F32), rim, rim),
        [dma((3,))],
        1 << 34,
        (latents, gain_first),
        hbm=(0, 1),
    )
    far, near = swap(far, 1), swap(near, 0)
    inner_rows = rows - 2
    inner_pixels = inner_rows * width
    across = jnp.swapaxes(kernel_first, 3, 4)
    active, inner = call(
        inner_kernel,
        (
            shape(latents.shape, BF16),
            shape((2, inner_rows * 3 // 2, width, 128), BF16),
        ),
        work(rows, channels) + [pltpu.VMEM((2, inner_pixels, 192), F32)],
        2 * flops1,
        (held, gain_first, across),
    )
    inner = onward(inner)
    (late_inner,) = call(
        late_inner_own_kernel, (shape((inner_pixels, 192), F32),), [], flops1, (active, across)
    )
    edge_sums = shape((2 * HALO * width, 192), F32)
    edge_work = [pltpu.VMEM(edge_sums.shape, F32), pltpu.VMEM((2 * HALO, width, channels), BF16)]
    edge_work += work(2 * HALO, channels)
    ends = shape((2, HALO + 2, width, channels), BF16)
    packed1 = shape((HALO * 3, width, 128), BF16)
    partial, late = call(
        late_edge_kernel,
        (packed1, ends),
        edge_work,
        flops1 // 2,
        (near, far, gain_first, active, across),
        after=(late_inner,),
    )
    late_edges = onward(partial)
    partial, early = call(
        early_edge_kernel,
        (packed1, ends),
        edge_work,
        flops1,
        (near, far, gain_first, active, across, late),
        after=(partial,),
    )
    early_edges = onward(partial)
    (late_rest,) = call(late_edge_own_kernel, (edge_sums,), [], 1 << 20, (early, late, across))
    second_work = [pltpu.VMEM((pixels1, 192), BF16)] + work(wide1, 192)
    packed2 = shape((wide2 * 3 // 2, width, 128), BF16)
    field = shape((3, wide1, width, 256), BF16)
    (early_own,) = call(
        early_own_kernel,
        (shape((pixels1, 192), F32),),
        [pltpu.VMEM((wide1 + 2, width, channels), BF16)],
        1 << 20,
        (active, early, across),
        after=(late_rest,),
    )
    partial, late = call(
        late_second_kernel,
        (packed2, field),
        second_work,
        flops2,
        (late_inner, late_rest, inner, late_edges, gain_second, kernel_second),
        after=(early_own,),
    )
    before_late = onward(partial)
    partial, early = call(
        early_second_kernel,
        (packed2, field),
        second_work,
        2 * flops2,
        (early_own, inner, early_edges, gain_second, kernel_second, late),
    )
    before_early = onward(partial)
    (own,) = call(
        second_own_kernel,
        (shape((2, pixels2, 192), F32),),
        [],
        3 * flops2,
        (early, late, kernel_second, held, near, far, shortcut.T),
    )
    (mixed,) = call(
        weights_kernel, (shape((3, 4, 768, 192), BF16),), [], 1 << 24, (kernel_third,), after=(own,)
    )
    third_work = [pltpu.VMEM((pixels2, 192), BF16)] + work(wide2, 192)
    block = shape((rows, width, 192), BF16)
    late_out, late = call(
        late_third_kernel,
        (block, packed2),
        third_work,
        1 << 24,
        (own, before_late, gain_third),
    )
    before_late = onward(late)
    early_out, early = call(
        early_third_kernel,
        (block, packed2),
        third_work,
        1 << 24,
        (own, before_early, gain_third),
        after=(mixed,),
    )
    before_early = onward_open(early)
    own, block_out = call(
        third_own_kernel,
        (shape((2, 4, pixels, 192), F32), shape((2, rows, width, 192), BF16)),
        [pltpu.VMEM((2, 3, wide2, width, 256), BF16), dma((2,))],
        3 * flops3,
        (early, late, mixed, early_out, late_out),
        out_hbm=(1,),
    )
    last_work = [
        pltpu.VMEM((3, wide2, width, 256), BF16),
        pltpu.VMEM((2, rows, 2, 2 * width, 128), F32),
        pltpu.VMEM((2, rows, 2 * width, 192), BF16),
        dma((2, rows // 2)),
    ]
    fine = shape((2, rows, 2, 2 * width, 192), BF16)
    decoded, rest = call(
        late_last_kernel,
        (fine, shape((4, pixels, 192), F32)),
        last_work,
        2 * flops3,
        (before_late, mixed, own),
        out_hbm=(0,),
    )
    (decoded,) = call(
        early_last_kernel,
        (fine,),
        last_work,
        flops3,
        (before_early, mixed, rest, decoded),
        hbm=(3,),
        out_hbm=(0,),
        aliases={3: 0},
    )
    decoded = decoded.reshape(2, 2 * rows, 2 * width, 192)
    return (block_out, decoded)


def solution(mesh):
    return jax.shard_map(
        body,
        mesh=mesh,
        in_specs=(P("tm", "rows", None, None), P(), P(), P(), P(), P(), P(), P()),
        out_specs=(P("tm", "rows", None, None), P("tm", "rows", None, None)),
        check_vma=False,
    )
```

```python
import jax
import jax.numpy as jnp
from jax import lax
from jax.experimental import pallas as pl
from jax.experimental.pallas import tpu as pltpu
from jax.sharding import PartitionSpec as P

F32 = jnp.float32
BF16 = jnp.bfloat16
HALO = 3
LIMIT = 24


def dot(a, b):
    return jnp.dot(a, b, preferred_element_type=F32)


def dot_t(a, b):
    return lax.dot_general(a, b, (((1,), (1,)), ((), ())), preferred_element_type=F32)


def spans(channels):
    return [(at, min(128, channels - at)) for at in range(0, channels, 128)]


def scales(squares, channels):
    total = dot(squares, jnp.ones((channels, 128), BF16))
    return lax.rsqrt(total * (1.0 / channels) + 1e-06)


def activated(v, scale, gain):
    u = v * scale * gain
    return u * (0.5 + 0.5 * jnp.tanh(0.5 * u))


def column_masks(width, channels):
    column = lax.broadcasted_iota(jnp.int32, (width, channels), 0)
    return column == 0, column == width - 1


def beside(v, masks):
    width = v.shape[0]
    left = jnp.where(masks[0], 0.0, pltpu.roll(v, 1, 0))
    right = jnp.where(masks[1], 0.0, pltpu.roll(v, width - 1, 0))
    return left, right


def call(kernel, out_shape, scratch, flops, args, hbm=(), out_hbm=(), aliases=None, after=()):
    vmem = pl.BlockSpec(memory_space=pltpu.VMEM)
    far = pl.BlockSpec(memory_space=pltpu.HBM)
    args = [pltpu.with_memory_space_constraint(x, pltpu.HBM) if i in hbm else x for i, x in enumerate(args)]

    count = len(args)

    def placed(*refs):
        place = [f(axis) for f in (lax.axis_index, lax.axis_size) for axis in ("tm", "rows")]
        kernel(place, *refs[:count], *refs[count + len(after) :])

    return pl.pallas_call(
        placed,
        out_shape=out_shape,
        in_specs=[far if i in hbm else vmem for i in range(count)] + [pl.BlockSpec(memory_space=pl.ANY)] * len(after),
        out_specs=tuple(far if i in out_hbm else vmem for i in range(len(out_shape))),
        scratch_shapes=scratch,
        input_output_aliases=aliases or {},
        compiler_params=pltpu.CompilerParams(vmem_limit_bytes=LIMIT << 20),
        cost_estimate=pl.CostEstimate(flops=flops, bytes_accessed=4 << 20, transcendentals=0),
    )(*args, *after)


def pack_rows(ref, rows, get):
    for row in range(0, rows, 2):
        upper, lower = get(row), get(row + 1)
        ref[row] = upper[:, 0:128].astype(BF16)
        ref[row + 1] = lower[:, 0:128].astype(BF16)
        ref[rows + row // 2] = jnp.concatenate([upper[:, 128:192], lower[:, 128:192]], axis=1).astype(BF16)


def unpack_row(ref, row):
    rows = ref.shape[0] * 2 // 3
    rest = ref[rows + row // 2].astype(F32)
    side = 64 * (row % 2)
    return jnp.concatenate([ref[row].astype(F32), rest[:, side : side + 64]], axis=1)


def fill_field(field, rows, first, rest):
    width = field.shape[2]
    masks = column_masks(width, 128)
    for row in range(rows):
        for at, part in ((0, first(row)), (128, rest(row))):
            left, right = beside(part, masks)
            for shift, value in enumerate((left, part, right)):
                field[shift, row, :, at : at + 128] = value.astype(BF16)


def packed_parts(ref, follows=None):
    rows = ref.shape[0] * 2 // 3

    def guard(value):
        value = value.astype(F32)
        return value if follows is None else jnp.where(follows, value, 0.0)

    def first(row):
        return guard(ref[row])

    def rest(row):
        at = rows + row // 2
        if row % 2 == 0:
            return guard(ref[at])
        upper = ref[at].astype(F32)[:, 64:128]
        lower = jnp.zeros_like(upper) if row == rows - 1 else ref[at + 1].astype(F32)[:, 0:64]
        return guard(jnp.concatenate([upper, lower], axis=1))

    return rows, first, rest


def row_parts(rows, get):
    made = {}

    def row_of(row):
        if row not in made:
            made[row] = get(row)
        return made[row]

    def rest(row):
        upper = row_of(row)[:, 128:192]
        lower = row_of(row + 1)[:, 128:192] if row < rows - 1 else jnp.zeros_like(upper)
        return jnp.concatenate([upper, lower], axis=1)

    return rows, lambda row: row_of(row)[:, 0:128], rest


def two_rows(field, shift, row, rows):
    pixels = rows * field.shape[2]
    return [
        field[shift, row : row + rows].reshape(pixels, 256),
        field[shift, row + 1 : row + 1 + rows, :, 0:128].reshape(pixels, 128),
    ]


def two_rows_weights(upper, lower):
    return [upper, lower[128:192], lower[0:128]]


def convolve_field(kernel, terms, rows):
    lanes, weights = [], []
    for field, a in terms:
        for e in range(3):
            lanes += two_rows(field, e, 0, rows)
            weights += two_rows_weights(kernel[a, 0, e], kernel[a, 1, e])
            lanes.append(field[e, 2 : 2 + rows].reshape(rows * field.shape[2], 256))
            weights += [kernel[a, 2, e], jnp.zeros((64, 192), BF16)]
    return dot(jnp.concatenate(lanes, axis=1), jnp.concatenate(weights, axis=0))


def convolve(acc, product, kernel, terms, rows, width):
    masks = column_masks(width, 192)
    fields = [window(b) for window, a in terms for b in range(3)]
    if product is dot_t:
        fields = [jnp.concatenate(fields, axis=1)]
    for e in range(3):
        taps = [kernel[a, b, e] for window, a in terms for b in range(3)]
        if product is dot_t:
            taps = [jnp.concatenate(taps, axis=1)]
        total = None
        for field, tap in zip(fields, taps):
            term = product(field, tap)
            total = term if total is None else total + term
        for row in range(rows):
            part = slice(row * width, (row + 1) * width)
            moved = total[part]
            if e == 0:
                acc[part] = jnp.where(masks[0], 0.0, pltpu.roll(moved, 1, 0))
            elif e == 1:
                acc[part] += moved
            else:
                acc[part] += jnp.where(masks[1], 0.0, pltpu.roll(moved, width - 1, 0))


def windows(ref, rows):
    return lambda b: ref[b : b + rows].reshape(rows * ref.shape[1], ref.shape[2])


OWN = (((0, 2),), ((0, 1), (1, 2)))


def activate_rows(fields, gain, squares, scale, put):
    rows, width, channels = fields[0].shape
    pixels = rows * width
    for i, ref in enumerate(fields):
        v = ref[...].astype(F32)
        squares[i * pixels : (i + 1) * pixels] = (v * v).astype(BF16).reshape(pixels, channels)
    every = len(fields) * pixels
    scale[0:every] = scales(squares[0:every], channels)
    for i, ref in enumerate(fields):
        for row in range(rows):
            part = slice(i * pixels + row * width, i * pixels + (row + 1) * width)
            for at, lanes in spans(channels):
                v = activated(
                    ref[row, :, at : at + lanes].astype(F32),
                    scale[part],
                    gain[at : at + lanes].reshape(1, lanes),
                )
                put(i, row, slice(at, at + lanes), v.astype(BF16))


def rim_kernel(place, latents, gain, held, held_gain, near, far, sems):
    rows = held.shape[1]
    copies = [pltpu.make_async_copy(latents.at[frame], held.at[frame], sems.at[frame]) for frame in range(2)]
    copies.append(pltpu.make_async_copy(gain, held_gain, sems.at[2]))
    for copy in copies:
        copy.start()
    odd = place[1] % 2
    for frame in range(2):
        copies[frame].wait()
        far[frame] = held[frame, pl.ds((rows - HALO) * odd, HALO)]
        near[frame] = held[frame, pl.ds((rows - HALO) * (1 - odd), HALO)]
    copies[2].wait()


def inner_kernel(place, held, gain, weights, active, packed, squares, scale, sums):
    frames, rows, width, channels = held.shape

    def put(frame, row, lanes, value):
        active[frame, row, :, lanes] = value

    for frame in range(frames):
        activate_rows(
            [held.at[frame]], gain, squares, scale, lambda _, *args, frame=frame: put(frame, *args)
        )
    count = rows - 2
    for out, taps in ((1, ((1, 0),)), (0, ((0, 0), (1, 1)))):
        terms = [(windows(active.at[frame], count), a) for frame, a in taps]
        convolve(sums.at[out], dot_t, weights, terms, count, width)
        pack_rows(packed.at[out], count, lambda row: sums[out, row * width : (row + 1) * width])


def late_inner_own_kernel(place, active, weights, own):
    count, width = active.shape[1] - 2, active.shape[2]
    terms = [(windows(active.at[frame], count), a) for frame, a in OWN[1]]
    convolve(own, dot_t, weights, terms, count, width)


def fill_edges(place, near, far, frame, gain, active, edges, raw, squares, scale):
    odd = place[1] % 2 == 1
    inner = jnp.logical_and(place[1] > 0, place[1] < place[3] - 1)
    rows = active.shape[1]
    for row in range(HALO):
        chip = near[frame, row]
        next_chip = jnp.where(inner, far[frame, row], jnp.zeros_like(chip))
        raw[row] = jnp.where(odd, chip, next_chip)
        raw[HALO + row] = jnp.where(odd, next_chip, chip)

    def put(_, row, lanes, value):
        side, at = divmod(row, HALO)
        edges[side, at + 2 * side, :, lanes] = value

    activate_rows([raw], gain, squares, scale, put)
    edges[0, HALO : HALO + 2] = active[frame, 0:2]
    edges[1, 0:2] = active[frame, rows - 2 : rows]


def edge_windows(edges):
    width, channels = edges.shape[2], edges.shape[3]
    return lambda b: edges[:, b : b + HALO].reshape(2 * HALO * width, channels)


def pack_edges(partial, acc, width):
    pack_rows(partial, 2 * HALO, lambda row: acc[row * width : (row + 1) * width])


def late_edge_kernel(place, near, far, gain, active, weights, partial, edges, acc, raw, squares, scale):
    fill_edges(place, near, far, 1, gain, active, edges, raw, squares, scale)
    width = active.shape[2]
    convolve(acc, dot_t, weights, [(edge_windows(edges), 0)], 2 * HALO, width)
    pack_edges(partial, acc, width)


def early_edge_kernel(
    place, near, far, gain, active, weights, late, partial, edges, acc, raw, squares, scale
):
    fill_edges(place, near, far, 0, gain, active, edges, raw, squares, scale)
    width = active.shape[2]
    convolve(acc, dot_t, weights, [(edge_windows(edges), 0), (edge_windows(late), 1)], 2 * HALO, width)
    pack_edges(partial, acc, width)


def late_edge_own_kernel(place, early, late, weights, own):
    terms = [(edge_windows((early, late)[frame]), a) for frame, a in OWN[1]]
    convolve(own, dot_t, weights, terms, 2 * HALO, early.shape[2])


def early_own_kernel(place, active, early, weights, own, tall):
    rows, width = active.shape[1], active.shape[2]
    tall[0:HALO] = early[0, 0:HALO]
    tall[HALO : HALO + rows] = active[0]
    tall[HALO + rows :] = early[1, 2:]
    (frame, a), = OWN[0]
    convolve(own, dot_t, weights, [(windows(tall, rows + 4), a)], rows + 4, width)


def finish(place, own, before, gain, raw, squares, scale, keep):
    before, tall, width = before
    start = place[1] * 8 - (tall - 8) // 2
    follows = place[0] > 0
    for row in range(tall):
        part = slice(row * width, (row + 1) * width)
        earlier = jnp.where(follows, before(row), 0.0)
        total = (own(row) + earlier).astype(BF16)
        raw[part] = total
        keep(row, total)
        total = total.astype(F32)
        squares[part] = (total * total).astype(BF16)
    scale[...] = scales(squares[...], 192)

    def get(row):
        part = slice(row * width, (row + 1) * width)
        inside = jnp.logical_and(start + row >= 0, start + row < place[3] * 8)
        lanes = []
        for at, count in spans(192):
            v = activated(
                raw[part, at : at + count].astype(F32), scale[part, 0:count], gain[at : at + count].reshape(1, count)
            )
            if not (tall - 8) // 2 <= row < (tall + 8) // 2:
                v = jnp.where(inside, v, 0.0)
            lanes.append(v)
        return jnp.concatenate(lanes, axis=1)

    return get


def second(place, own, before, gain, kernel, terms, partial, field, raw, squares, scale):
    rows = field.shape[1]
    width, wide = field.shape[2], rows - 2
    get = finish(place, own, before, gain, raw, squares, scale, lambda row, total: None)
    fill_field(field, *row_parts(rows, get))
    total = convolve_field(kernel, terms, wide)
    pack_rows(partial, wide, lambda row: total[row * width : (row + 1) * width])


def joined(inner, edges):
    count = inner.shape[0] * 2 // 3

    def get(row):
        if HALO <= row < HALO + count:
            return unpack_row(inner, row - HALO)
        return unpack_row(edges, row if row < HALO else row - count)

    return get, count + 2 * HALO, inner.shape[1]


def whole(packed):
    return lambda row: unpack_row(packed, row), packed.shape[0] * 2 // 3, packed.shape[1]


def joined_own(inner, edges, width):
    count = inner.shape[0] // width

    def get(row):
        ref, at = (inner, row - HALO) if HALO <= row < HALO + count else (edges, row if row < HALO else row - count)
        return ref[at * width : (at + 1) * width]

    return get


def rows_of(own, width):
    return lambda row: own[row * width : (row + 1) * width]


def late_second_kernel(
    place, own_inner, own_edges, inner, edges, gain, kernel, partial, field, raw, squares, scale
):
    before = joined(inner.at[1], edges)
    own = joined_own(own_inner, own_edges, field.shape[2])
    second(place, own, before, gain, kernel, [(field, 0)], partial, field, raw, squares, scale)


def early_second_kernel(
    place, own, inner, edges, gain, kernel, late, partial, field, raw, squares, scale
):
    before = joined(inner.at[0], edges)
    own = rows_of(own, field.shape[2])
    second(place, own, before, gain, kernel, [(field, 0), (late, 1)], partial, field, raw, squares, scale)


def second_own_kernel(place, early, late, kernel, latents, near, far, shortcut, own):
    wide, width = early.shape[1] - 2, early.shape[2]
    pixels = wide * width
    rows, channels = latents.shape[1], latents.shape[3]
    odd = place[1] % 2
    inner = wide - 1
    fields = (early, late)
    for out in (1, 0):
        own[out] = convolve_field(kernel, [(fields[frame], a) for frame, a in OWN[out]], wide)
        body = latents[out].reshape(rows * width, channels)
        own[out, width : pixels - width] += dot_t(body, shortcut[...])
        other = dot_t(near[out, jnp.where(odd == 1, HALO - 1, 0)], shortcut[...])
        own[out, pl.ds(jnp.where(odd == 1, 0, inner * width), width)] += other
        other = dot_t(far[out, jnp.where(odd == 1, 0, HALO - 1)], shortcut[...])
        own[out, pl.ds(jnp.where(odd == 1, inner * width, 0), width)] += other


def third(place, own, before, gain, block, packed, raw, squares, scale):
    tall = packed.shape[0] * 2 // 3

    def keep(row, total):
        if 0 < row < tall - 1:
            block[row - 1] = total

    own = rows_of(own, packed.shape[1])
    pack_rows(packed, tall, finish(place, own, whole(before), gain, raw, squares, scale, keep))


def late_third_kernel(place, own, before, gain, block, packed, raw, squares, scale):
    third(place, own.at[1], before, gain, block, packed, raw, squares, scale)


def early_third_kernel(place, own, before, gain, block, packed, raw, squares, scale):
    third(place, own.at[0], before, gain, block, packed, raw, squares, scale)


def weights_kernel(place, kernel, out):
    def halves(taps, parity):
        if parity == 0:
            return taps[0], taps[1] + taps[2]
        return taps[0] + taps[1], taps[2]

    for a in range(3):
        for i in range(2):
            rows = [halves([kernel[a, b, e] for b in range(3)], i) for e in range(3)]
            for j in range(2):
                upper = halves([rows[e][0] for e in range(3)], j)
                lower = halves([rows[e][1] for e in range(3)], j)
                for column in range(2):
                    at = 384 * column
                    for part in two_rows_weights(upper[column], lower[column]):
                        out[a, 2 * i + j, at : at + part.shape[0]] = part
                        at += part.shape[0]


def phase(terms, kernel, i, j, rows):
    lanes, weights = [], []
    for field, a in terms:
        for shift in (j, j + 1):
            lanes += two_rows(field, shift, i, rows)
        weights.append(kernel[a, 2 * i + j])
    return dot(jnp.concatenate(lanes, axis=1), jnp.concatenate(weights, axis=0))


def third_late_own_kernel(place, packed, kernel, own, field):
    rows = packed.shape[0] * 2 // 3 - 2
    fill_field(field, *packed_parts(packed))
    for i in range(2):
        for j in range(2):
            own[2 * i + j] = phase([(field, 2)], kernel, i, j, rows)


def third_own_kernel(place, packed, late, kernel, early_out, late_out, own, block_out, field, sems):
    copies = [
        pltpu.make_async_copy(block, block_out.at[frame], sems.at[frame])
        for frame, block in enumerate((early_out, late_out))
    ]
    for copy in copies:
        copy.start()
    fill_field(field, *packed_parts(packed))
    rows = early_out.shape[0]
    for i in range(2):
        for j in range(2):
            own[1, 2 * i + j] = late[2 * i + j] + phase([(field, 1)], kernel, i, j, rows)
            own[0, 2 * i + j] = phase([(field, 2)], kernel, i, j, rows)
    for copy in copies:
        copy.wait()


def weave(total, j, rows, width, woven):
    for row in range(rows):
        value = total[row * width : (row + 1) * width]
        woven[row, 0, pl.ds(j, width, stride=2)] = value[:, 0:128]
        woven[row, 1, pl.ds(j, width, stride=2), 0:64] = value[:, 128:192]


def write_out(own, field, kernel, a, rows, width, woven, fine, out, sems):
    copies = []
    for i in range(2):
        for j in range(2):
            total = own[2 * i + j] + phase([(field, a)], kernel, i, j, rows)
            weave(total, j, rows, width, woven.at[i])
        for row in range(rows):
            fine[i, row, :, 0:128] = woven[i, row, 0].astype(BF16)
            fine[i, row, :, 128:192] = woven[i, row, 1, :, 0:64].astype(BF16)
            if row % 2:
                part = slice(row - 1, row + 1)
                copies.append(pltpu.make_async_copy(fine.at[i, part], out.at[part, i], sems.at[i, row // 2]))
                copies[-1].start()
    return copies


def late_last_kernel(place, packed, kernel, own, decoded, rest, field, woven, fine, sems):
    rows, width = packed.shape[0] * 2 // 3 - 2, packed.shape[1]
    fill_field(field, *packed_parts(packed, place[0] > 0))
    copies = write_out(own.at[1], field, kernel, 0, rows, width, woven, fine, decoded.at[1], sems)
    for i in range(2):
        for j in range(2):
            rest[2 * i + j] = own[0, 2 * i + j] + phase([(field, 1)], kernel, i, j, rows)
    for copy in copies:
        copy.wait()


def early_last_kernel(place, packed, kernel, rest, late, decoded, field, woven, fine, sems):
    rows, width = packed.shape[0] * 2 // 3 - 2, packed.shape[1]
    fill_field(field, *packed_parts(packed, place[0] > 0))
    for copy in write_out(rest, field, kernel, 0, rows, width, woven, fine, decoded.at[0], sems):
        copy.wait()


def onward_open(value):
    count = lax.axis_size("tm")
    return lax.ppermute(value, "tm", [(i, i + 1) for i in range(count - 1)])


def onward(value):
    count = lax.axis_size("tm")
    return lax.ppermute(value, "tm", [(i, (i + 1) % count) for i in range(count)])


def swap(value, offset):
    groups, slabs = lax.axis_size("tm"), lax.axis_size("rows")
    pairs = [(g * slabs + i, g * slabs + i + 1) for g in range(groups) for i in range(offset, slabs - 1, 2)]
    if offset:
        pairs += [(g * slabs + i, (g + 1) * slabs + i) for g in range(0, groups - 1, 2) for i in (0, slabs - 1)]
    alone = set(range(groups * slabs)) - {i for pair in pairs for i in pair}
    return lax.ppermute(
        value, ("tm", "rows"), pairs + [(b, a) for a, b in pairs] + [(i, i) for i in sorted(alone)]
    )


def body(
    latents,
    gain_first,
    kernel_first,
    gain_second,
    kernel_second,
    shortcut,
    gain_third,
    kernel_third,
):
    frames, rows, width, channels = latents.shape
    shape = jax.ShapeDtypeStruct
    shape = jax.ShapeDtypeStruct
    odd = lax.axis_index("rows") % 2
    near = lax.dynamic_slice_in_dim(latents, (rows - HALO) * (1 - odd), HALO, 1)
    far = lax.dynamic_slice_in_dim(latents, (rows - HALO) * odd, HALO, 1)
    near, far = swap(near, 0), swap(far, 1)

    wide1, wide2 = rows + 4, rows + 2
    pixels, pixels1, pixels2 = rows * width, wide1 * width, wide2 * width
    flops1, flops2, flops3 = (18 * n * 192 for n in (pixels1 * channels, pixels2 * 192, pixels * 192))
    dma = pltpu.SemaphoreType.DMA

    def work(tall, channels):
        return [pltpu.VMEM((tall * width, channels), BF16), pltpu.VMEM((tall * width, 128), F32)]

    rim = shape((frames, HALO, width, channels), BF16)
    held, gain_first, near, far = call(
        rim_kernel,
        (shape(latents.shape, BF16), shape((channels,), F32), rim, rim),
        [dma((3,))],
        1 << 34,
        (latents, gain_first),
        hbm=(0, 1),
    )
    far, near = swap(far, 1), swap(near, 0)
    inner_rows = rows - 2
    inner_pixels = inner_rows * width
    across = jnp.swapaxes(kernel_first, 3, 4)
    active, inner = call(
        inner_kernel,
        (
            shape(latents.shape, BF16),
            shape((2, inner_rows * 3 // 2, width, 128), BF16),
        ),
        work(rows, channels) + [pltpu.VMEM((2, inner_pixels, 192), F32)],
        2 * flops1,
        (held, gain_first, across),
    )
    inner = onward(inner)
    (late_inner,) = call(
        late_inner_own_kernel, (shape((inner_pixels, 192), F32),), [], flops1, (active, across)
    )
    edge_sums = shape((2 * HALO * width, 192), F32)
    edge_work = [pltpu.VMEM(edge_sums.shape, F32), pltpu.VMEM((2 * HALO, width, channels), BF16)]
    edge_work += work(2 * HALO, channels)
    ends = shape((2, HALO + 2, width, channels), BF16)
    packed1 = shape((HALO * 3, width, 128), BF16)
    partial, late = call(
        late_edge_kernel,
        (packed1, ends),
        edge_work,
        flops1 // 2,
        (near, far, gain_first, active, across),
        after=(late_inner,),
    )
    late_edges = onward(partial)
    partial, early = call(
        early_edge_kernel,
        (packed1, ends),
        edge_work,
        flops1,
        (near, far, gain_first, active, across, late),
        after=(partial,),
    )
    early_edges = onward(partial)
    (late_rest,) = call(
        late_edge_own_kernel, (edge_sums,), [], flops1, (early, late, across), after=(kernel_second,)
    )
    second_work = [pltpu.VMEM((pixels1, 192), BF16)] + work(wide1, 192)
    packed2 = shape((wide2 * 3 // 2, width, 128), BF16)
    field = shape((3, wide1, width, 256), BF16)
    (early_own,) = call(
        early_own_kernel,
        (shape((pixels1, 192), F32),),
        [pltpu.VMEM((wide1 + 2, width, channels), BF16)],
        1 << 20,
        (active, early, across),
        after=(late_rest,),
    )
    partial, late = call(
        late_second_kernel,
        (packed2, field),
        second_work,
        flops2,
        (late_inner, late_rest, inner, late_edges, gain_second, kernel_second),
        after=(early_own,),
    )
    before_late = onward(partial)
    partial, early = call(
        early_second_kernel,
        (packed2, field),
        second_work,
        2 * flops2,
        (early_own, inner, early_edges, gain_second, kernel_second, late),
    )
    before_early = onward(partial)
    (own,) = call(
        second_own_kernel,
        (shape((2, pixels2, 192), F32),),
        [],
        3 * flops2,
        (early, late, kernel_second, held, near, far, shortcut.T),
    )
    (mixed,) = call(
        weights_kernel, (shape((3, 4, 768, 192), BF16),), [], 1 << 24, (kernel_third,), after=(own,)
    )
    third_work = [pltpu.VMEM((pixels2, 192), BF16)] + work(wide2, 192)
    block = shape((rows, width, 192), BF16)
    late_out, late = call(
        late_third_kernel,
        (block, packed2),
        third_work,
        1 << 24,
        (own, before_late, gain_third),
    )
    before_late = onward(late)
    (late_own,) = call(
        third_late_own_kernel,
        (shape((4, pixels, 192), F32),),
        [pltpu.VMEM((3, wide2, width, 256), BF16)],
        flops3,
        (late, mixed),
    )
    early_out, early = call(
        early_third_kernel,
        (block, packed2),
        third_work,
        1 << 24,
        (own, before_early, gain_third),
        after=(late_own,),
    )
    before_early = onward_open(early)
    own, block_out = call(
        third_own_kernel,
        (shape((2, 4, pixels, 192), F32), shape((2, rows, width, 192), BF16)),
        [pltpu.VMEM((3, wide2, width, 256), BF16), dma((2,))],
        2 * flops3,
        (early, late_own, mixed, early_out, late_out),
        out_hbm=(1,),
    )
    last_work = [
        pltpu.VMEM((3, wide2, width, 256), BF16),
        pltpu.VMEM((2, rows, 2, 2 * width, 128), F32),
        pltpu.VMEM((2, rows, 2 * width, 192), BF16),
        dma((2, rows // 2)),
    ]
    fine = shape((2, rows, 2, 2 * width, 192), BF16)
    decoded, rest = call(
        late_last_kernel,
        (fine, shape((4, pixels, 192), F32)),
        last_work,
        2 * flops3,
        (before_late, mixed, own),
        out_hbm=(0,),
    )
    (decoded,) = call(
        early_last_kernel,
        (fine,),
        last_work,
        flops3,
        (before_early, mixed, rest, decoded),
        hbm=(3,),
        out_hbm=(0,),
        aliases={3: 0},
    )
    decoded = decoded.reshape(2, 2 * rows, 2 * width, 192)
    return (block_out, decoded)


def solution(mesh):
    return jax.shard_map(
        body,
        mesh=mesh,
        in_specs=(P("tm", "rows", None, None), P(), P(), P(), P(), P(), P(), P()),
        out_specs=(P("tm", "rows", None, None), P("tm", "rows", None, None)),
        check_vma=False,
    )
```

```python
import jax
import jax.numpy as jnp
from jax import lax
from jax.experimental import pallas as pl
from jax.experimental.pallas import tpu as pltpu
from jax.sharding import PartitionSpec as P

F32 = jnp.float32
BF16 = jnp.bfloat16
HALO = 3
LIMIT = 24


def dot(a, b):
    return jnp.dot(a, b, preferred_element_type=F32)


def dot_t(a, b):
    return lax.dot_general(a, b, (((1,), (1,)), ((), ())), preferred_element_type=F32)


def spans(channels):
    return [(at, min(128, channels - at)) for at in range(0, channels, 128)]


def scales(squares, channels):
    total = dot(squares, jnp.ones((channels, 128), BF16))
    return lax.rsqrt(total * (1.0 / channels) + 1e-06)


def activated(v, scale, gain):
    u = v * scale * gain
    return u * (0.5 + 0.5 * jnp.tanh(0.5 * u))


def column_masks(width, channels):
    column = lax.broadcasted_iota(jnp.int32, (width, channels), 0)
    return column == 0, column == width - 1


def beside(v, masks):
    width = v.shape[0]
    left = jnp.where(masks[0], 0.0, pltpu.roll(v, 1, 0))
    right = jnp.where(masks[1], 0.0, pltpu.roll(v, width - 1, 0))
    return left, right


def call(kernel, out_shape, scratch, flops, args, hbm=(), out_hbm=(), aliases=None, after=()):
    vmem = pl.BlockSpec(memory_space=pltpu.VMEM)
    far = pl.BlockSpec(memory_space=pltpu.HBM)
    args = [pltpu.with_memory_space_constraint(x, pltpu.HBM) if i in hbm else x for i, x in enumerate(args)]

    count = len(args)

    def placed(*refs):
        place = [f(axis) for f in (lax.axis_index, lax.axis_size) for axis in ("tm", "rows")]
        kernel(place, *refs[:count], *refs[count + len(after) :])

    return pl.pallas_call(
        placed,
        out_shape=out_shape,
        in_specs=[far if i in hbm else vmem for i in range(count)] + [pl.BlockSpec(memory_space=pl.ANY)] * len(after),
        out_specs=tuple(far if i in out_hbm else vmem for i in range(len(out_shape))),
        scratch_shapes=scratch,
        input_output_aliases=aliases or {},
        compiler_params=pltpu.CompilerParams(vmem_limit_bytes=LIMIT << 20),
        cost_estimate=pl.CostEstimate(flops=flops, bytes_accessed=4 << 20, transcendentals=0),
    )(*args, *after)


def pack_rows(ref, rows, get):
    for row in range(0, rows, 2):
        upper, lower = get(row), get(row + 1)
        ref[row] = upper[:, 0:128].astype(BF16)
        ref[row + 1] = lower[:, 0:128].astype(BF16)
        ref[rows + row // 2] = jnp.concatenate([upper[:, 128:192], lower[:, 128:192]], axis=1).astype(BF16)


def unpack_row(ref, row):
    rows = ref.shape[0] * 2 // 3
    rest = ref[rows + row // 2].astype(F32)
    side = 64 * (row % 2)
    return jnp.concatenate([ref[row].astype(F32), rest[:, side : side + 64]], axis=1)


def fill_field(field, rows, first, rest):
    width = field.shape[2]
    masks = column_masks(width, 128)
    for row in range(rows):
        for at, part in ((0, first(row)), (128, rest(row))):
            left, right = beside(part, masks)
            for shift, value in enumerate((left, part, right)):
                field[shift, row, :, at : at + 128] = value.astype(BF16)


def packed_parts(ref, follows=None):
    rows = ref.shape[0] * 2 // 3

    def guard(value):
        value = value.astype(F32)
        return value if follows is None else jnp.where(follows, value, 0.0)

    def first(row):
        return guard(ref[row])

    def rest(row):
        at = rows + row // 2
        if row % 2 == 0:
            return guard(ref[at])
        upper = ref[at].astype(F32)[:, 64:128]
        lower = jnp.zeros_like(upper) if row == rows - 1 else ref[at + 1].astype(F32)[:, 0:64]
        return guard(jnp.concatenate([upper, lower], axis=1))

    return rows, first, rest


def row_parts(rows, get):
    made = {}

    def row_of(row):
        if row not in made:
            made[row] = get(row)
        return made[row]

    def rest(row):
        upper = row_of(row)[:, 128:192]
        lower = row_of(row + 1)[:, 128:192] if row < rows - 1 else jnp.zeros_like(upper)
        return jnp.concatenate([upper, lower], axis=1)

    return rows, lambda row: row_of(row)[:, 0:128], rest


def two_rows(field, shift, row, rows):
    pixels = rows * field.shape[2]
    return [
        field[shift, row : row + rows].reshape(pixels, 256),
        field[shift, row + 1 : row + 1 + rows, :, 0:128].reshape(pixels, 128),
    ]


def two_rows_weights(upper, lower):
    return [upper, lower[128:192], lower[0:128]]


def convolve_field(kernel, terms, rows):
    lanes, weights = [], []
    for field, a in terms:
        for e in range(3):
            lanes += two_rows(field, e, 0, rows)
            weights += two_rows_weights(kernel[a, 0, e], kernel[a, 1, e])
            lanes.append(field[e, 2 : 2 + rows].reshape(rows * field.shape[2], 256))
            weights += [kernel[a, 2, e], jnp.zeros((64, 192), BF16)]
    return dot(jnp.concatenate(lanes, axis=1), jnp.concatenate(weights, axis=0))


def convolve(acc, product, kernel, terms, rows, width):
    masks = column_masks(width, 192)
    fields = [window(b) for window, a in terms for b in range(3)]
    if product is dot_t:
        fields = [jnp.concatenate(fields, axis=1)]
    for e in range(3):
        taps = [kernel[a, b, e] for window, a in terms for b in range(3)]
        if product is dot_t:
            taps = [jnp.concatenate(taps, axis=1)]
        total = None
        for field, tap in zip(fields, taps):
            term = product(field, tap)
            total = term if total is None else total + term
        for row in range(rows):
            part = slice(row * width, (row + 1) * width)
            moved = total[part]
            if e == 0:
                acc[part] = jnp.where(masks[0], 0.0, pltpu.roll(moved, 1, 0))
            elif e == 1:
                acc[part] += moved
            else:
                acc[part] += jnp.where(masks[1], 0.0, pltpu.roll(moved, width - 1, 0))


def windows(ref, rows):
    return lambda b: ref[b : b + rows].reshape(rows * ref.shape[1], ref.shape[2])


OWN = (((0, 2),), ((0, 1), (1, 2)))


def activate_rows(fields, gain, squares, scale, put):
    rows, width, channels = fields[0].shape
    pixels = rows * width
    for i, ref in enumerate(fields):
        v = ref[...].astype(F32)
        squares[i * pixels : (i + 1) * pixels] = (v * v).astype(BF16).reshape(pixels, channels)
    every = len(fields) * pixels
    scale[0:every] = scales(squares[0:every], channels)
    for i, ref in enumerate(fields):
        for row in range(rows):
            part = slice(i * pixels + row * width, i * pixels + (row + 1) * width)
            for at, lanes in spans(channels):
                v = activated(
                    ref[row, :, at : at + lanes].astype(F32),
                    scale[part],
                    gain[at : at + lanes].reshape(1, lanes),
                )
                put(i, row, slice(at, at + lanes), v.astype(BF16))


def rim_kernel(place, latents, gain, held, held_gain, near, far, sems):
    rows = held.shape[1]
    copies = [pltpu.make_async_copy(latents.at[frame], held.at[frame], sems.at[frame]) for frame in range(2)]
    copies.append(pltpu.make_async_copy(gain, held_gain, sems.at[2]))
    for copy in copies:
        copy.start()
    odd = place[1] % 2
    for frame in range(2):
        copies[frame].wait()
        far[frame] = held[frame, pl.ds((rows - HALO) * odd, HALO)]
        near[frame] = held[frame, pl.ds((rows - HALO) * (1 - odd), HALO)]
    copies[2].wait()


def active_kernel(place, held, gain, active, squares, scale):
    def put(frame, row, lanes, value):
        active[frame, row, :, lanes] = value

    for frame in range(held.shape[0]):
        activate_rows(
            [held.at[frame]], gain, squares, scale, lambda _, *args, frame=frame: put(frame, *args)
        )


def inner_kernel(place, active, weights, packed, sums):
    frames, rows, width, channels = active.shape
    count = rows - 2
    for out, taps in ((1, ((1, 0),)), (0, ((0, 0), (1, 1)))):
        terms = [(windows(active.at[frame], count), a) for frame, a in taps]
        convolve(sums.at[out], dot_t, weights, terms, count, width)
        pack_rows(packed.at[out], count, lambda row: sums[out, row * width : (row + 1) * width])


def late_inner_own_kernel(place, active, weights, own):
    count, width = active.shape[1] - 2, active.shape[2]
    terms = [(windows(active.at[frame], count), a) for frame, a in OWN[1]]
    convolve(own, dot_t, weights, terms, count, width)


def fill_edges(place, near, far, frame, gain, active, edges, raw, squares, scale):
    odd = place[1] % 2 == 1
    inner = jnp.logical_and(place[1] > 0, place[1] < place[3] - 1)
    rows = active.shape[1]
    for row in range(HALO):
        chip = near[frame, row]
        next_chip = jnp.where(inner, far[frame, row], jnp.zeros_like(chip))
        raw[row] = jnp.where(odd, chip, next_chip)
        raw[HALO + row] = jnp.where(odd, next_chip, chip)

    def put(_, row, lanes, value):
        side, at = divmod(row, HALO)
        edges[side, at + 2 * side, :, lanes] = value

    activate_rows([raw], gain, squares, scale, put)
    edges[0, HALO : HALO + 2] = active[frame, 0:2]
    edges[1, 0:2] = active[frame, rows - 2 : rows]


def edge_windows(edges):
    width, channels = edges.shape[2], edges.shape[3]
    return lambda b: edges[:, b : b + HALO].reshape(2 * HALO * width, channels)


def pack_edges(partial, acc, width):
    pack_rows(partial, 2 * HALO, lambda row: acc[row * width : (row + 1) * width])


def late_edge_kernel(place, near, far, gain, active, weights, partial, edges, acc, raw, squares, scale):
    fill_edges(place, near, far, 1, gain, active, edges, raw, squares, scale)
    width = active.shape[2]
    convolve(acc, dot_t, weights, [(edge_windows(edges), 0)], 2 * HALO, width)
    pack_edges(partial, acc, width)


def early_edge_kernel(
    place, near, far, gain, active, weights, late, partial, edges, acc, raw, squares, scale
):
    fill_edges(place, near, far, 0, gain, active, edges, raw, squares, scale)
    width = active.shape[2]
    convolve(acc, dot_t, weights, [(edge_windows(edges), 0), (edge_windows(late), 1)], 2 * HALO, width)
    pack_edges(partial, acc, width)


def late_edge_own_kernel(place, early, late, weights, own):
    terms = [(edge_windows((early, late)[frame]), a) for frame, a in OWN[1]]
    convolve(own, dot_t, weights, terms, 2 * HALO, early.shape[2])


def early_own_kernel(place, active, early, weights, own, tall):
    rows, width = active.shape[1], active.shape[2]
    tall[0:HALO] = early[0, 0:HALO]
    tall[HALO : HALO + rows] = active[0]
    tall[HALO + rows :] = early[1, 2:]
    (frame, a), = OWN[0]
    convolve(own, dot_t, weights, [(windows(tall, rows + 4), a)], rows + 4, width)


def finish(place, own, before, gain, raw, squares, scale, keep):
    before, tall, width = before
    start = place[1] * 8 - (tall - 8) // 2
    follows = place[0] > 0
    for row in range(tall):
        part = slice(row * width, (row + 1) * width)
        earlier = jnp.where(follows, before(row), 0.0)
        total = (own(row) + earlier).astype(BF16)
        raw[part] = total
        keep(row, total)
        total = total.astype(F32)
        squares[part] = (total * total).astype(BF16)
    scale[...] = scales(squares[...], 192)

    def get(row):
        part = slice(row * width, (row + 1) * width)
        inside = jnp.logical_and(start + row >= 0, start + row < place[3] * 8)
        lanes = []
        for at, count in spans(192):
            v = activated(
                raw[part, at : at + count].astype(F32), scale[part, 0:count], gain[at : at + count].reshape(1, count)
            )
            if not (tall - 8) // 2 <= row < (tall + 8) // 2:
                v = jnp.where(inside, v, 0.0)
            lanes.append(v)
        return jnp.concatenate(lanes, axis=1)

    return get


def second(place, own, before, gain, kernel, terms, partial, field, raw, squares, scale):
    rows = field.shape[1]
    width, wide = field.shape[2], rows - 2
    get = finish(place, own, before, gain, raw, squares, scale, lambda row, total: None)
    fill_field(field, *row_parts(rows, get))
    total = convolve_field(kernel, terms, wide)
    pack_rows(partial, wide, lambda row: total[row * width : (row + 1) * width])


def joined(inner, edges):
    count = inner.shape[0] * 2 // 3

    def get(row):
        if HALO <= row < HALO + count:
            return unpack_row(inner, row - HALO)
        return unpack_row(edges, row if row < HALO else row - count)

    return get, count + 2 * HALO, inner.shape[1]


def whole(packed):
    return lambda row: unpack_row(packed, row), packed.shape[0] * 2 // 3, packed.shape[1]


def joined_own(inner, edges, width):
    count = inner.shape[0] // width

    def get(row):
        ref, at = (inner, row - HALO) if HALO <= row < HALO + count else (edges, row if row < HALO else row - count)
        return ref[at * width : (at + 1) * width]

    return get


def rows_of(own, width):
    return lambda row: own[row * width : (row + 1) * width]


def late_second_kernel(
    place, own_inner, own_edges, inner, edges, gain, kernel, partial, field, raw, squares, scale
):
    before = joined(inner.at[1], edges)
    own = joined_own(own_inner, own_edges, field.shape[2])
    second(place, own, before, gain, kernel, [(field, 0)], partial, field, raw, squares, scale)


def early_second_kernel(
    place, own, inner, edges, gain, kernel, late, partial, field, raw, squares, scale
):
    before = joined(inner.at[0], edges)
    own = rows_of(own, field.shape[2])
    second(place, own, before, gain, kernel, [(field, 0), (late, 1)], partial, field, raw, squares, scale)


def second_own_kernel(place, early, late, kernel, latents, near, far, shortcut, own):
    wide, width = early.shape[1] - 2, early.shape[2]
    pixels = wide * width
    rows, channels = latents.shape[1], latents.shape[3]
    odd = place[1] % 2
    inner = wide - 1
    fields = (early, late)
    for out in (1, 0):
        own[out] = convolve_field(kernel, [(fields[frame], a) for frame, a in OWN[out]], wide)
        body = latents[out].reshape(rows * width, channels)
        own[out, width : pixels - width] += dot_t(body, shortcut[...])
        other = dot_t(near[out, jnp.where(odd == 1, HALO - 1, 0)], shortcut[...])
        own[out, pl.ds(jnp.where(odd == 1, 0, inner * width), width)] += other
        other = dot_t(far[out, jnp.where(odd == 1, 0, HALO - 1)], shortcut[...])
        own[out, pl.ds(jnp.where(odd == 1, inner * width, 0), width)] += other


def third(place, own, before, gain, block, packed, raw, squares, scale):
    tall = packed.shape[0] * 2 // 3

    def keep(row, total):
        if 0 < row < tall - 1:
            block[row - 1] = total

    own = rows_of(own, packed.shape[1])
    pack_rows(packed, tall, finish(place, own, whole(before), gain, raw, squares, scale, keep))


def late_third_kernel(place, own, before, gain, block, packed, raw, squares, scale):
    third(place, own.at[1], before, gain, block, packed, raw, squares, scale)


def early_third_kernel(place, own, before, gain, block, packed, raw, squares, scale):
    third(place, own.at[0], before, gain, block, packed, raw, squares, scale)


def weights_kernel(place, kernel, out):
    def halves(taps, parity):
        if parity == 0:
            return taps[0], taps[1] + taps[2]
        return taps[0] + taps[1], taps[2]

    for a in range(3):
        for i in range(2):
            rows = [halves([kernel[a, b, e] for b in range(3)], i) for e in range(3)]
            for j in range(2):
                upper = halves([rows[e][0] for e in range(3)], j)
                lower = halves([rows[e][1] for e in range(3)], j)
                for column in range(2):
                    at = 384 * column
                    for part in two_rows_weights(upper[column], lower[column]):
                        out[a, 2 * i + j, at : at + part.shape[0]] = part
                        at += part.shape[0]


def phase(terms, kernel, i, j, rows):
    lanes, weights = [], []
    for field, a in terms:
        for shift in (j, j + 1):
            lanes += two_rows(field, shift, i, rows)
        weights.append(kernel[a, 2 * i + j])
    return dot(jnp.concatenate(lanes, axis=1), jnp.concatenate(weights, axis=0))


def third_late_own_kernel(place, packed, kernel, own, field):
    rows = packed.shape[0] * 2 // 3 - 2
    fill_field(field, *packed_parts(packed))
    for i in range(2):
        for j in range(2):
            own[2 * i + j] = phase([(field, 2)], kernel, i, j, rows)


def third_own_kernel(place, packed, late, kernel, early_out, late_out, own, block_out, field, sems):
    copies = [
        pltpu.make_async_copy(block, block_out.at[frame], sems.at[frame])
        for frame, block in enumerate((early_out, late_out))
    ]
    for copy in copies:
        copy.start()
    fill_field(field, *packed_parts(packed))
    rows = early_out.shape[0]
    for i in range(2):
        for j in range(2):
            own[1, 2 * i + j] = late[2 * i + j] + phase([(field, 1)], kernel, i, j, rows)
            own[0, 2 * i + j] = phase([(field, 2)], kernel, i, j, rows)
    for copy in copies:
        copy.wait()


def weave(total, j, rows, width, woven):
    for row in range(rows):
        value = total[row * width : (row + 1) * width]
        woven[row, 0, pl.ds(j, width, stride=2)] = value[:, 0:128]
        woven[row, 1, pl.ds(j, width, stride=2), 0:64] = value[:, 128:192]


def write_out(own, field, kernel, a, rows, width, woven, fine, out, sems):
    copies = []
    for i in range(2):
        for j in range(2):
            total = own[2 * i + j] + phase([(field, a)], kernel, i, j, rows)
            weave(total, j, rows, width, woven.at[i])
        for row in range(rows):
            fine[i, row, :, 0:128] = woven[i, row, 0].astype(BF16)
            fine[i, row, :, 128:192] = woven[i, row, 1, :, 0:64].astype(BF16)
            if row % 2:
                part = slice(row - 1, row + 1)
                copies.append(pltpu.make_async_copy(fine.at[i, part], out.at[part, i], sems.at[i, row // 2]))
                copies[-1].start()
    return copies


def late_last_kernel(place, packed, kernel, own, decoded, rest, field, woven, fine, sems):
    rows, width = packed.shape[0] * 2 // 3 - 2, packed.shape[1]
    fill_field(field, *packed_parts(packed, place[0] > 0))
    copies = write_out(own.at[1], field, kernel, 0, rows, width, woven, fine, decoded.at[1], sems)
    for i in range(2):
        for j in range(2):
            rest[2 * i + j] = own[0, 2 * i + j] + phase([(field, 1)], kernel, i, j, rows)
    for copy in copies:
        copy.wait()


def early_last_kernel(place, packed, kernel, rest, late, decoded, field, woven, fine, sems):
    rows, width = packed.shape[0] * 2 // 3 - 2, packed.shape[1]
    fill_field(field, *packed_parts(packed, place[0] > 0))
    for copy in write_out(rest, field, kernel, 0, rows, width, woven, fine, decoded.at[0], sems):
        copy.wait()


def onward_open(value):
    count = lax.axis_size("tm")
    return lax.ppermute(value, "tm", [(i, i + 1) for i in range(count - 1)])


def onward(value):
    count = lax.axis_size("tm")
    return lax.ppermute(value, "tm", [(i, (i + 1) % count) for i in range(count)])


def swap(value, offset):
    groups, slabs = lax.axis_size("tm"), lax.axis_size("rows")
    pairs = [(g * slabs + i, g * slabs + i + 1) for g in range(groups) for i in range(offset, slabs - 1, 2)]
    if offset:
        pairs += [(g * slabs + i, (g + 1) * slabs + i) for g in range(0, groups - 1, 2) for i in (0, slabs - 1)]
    alone = set(range(groups * slabs)) - {i for pair in pairs for i in pair}
    return lax.ppermute(
        value, ("tm", "rows"), pairs + [(b, a) for a, b in pairs] + [(i, i) for i in sorted(alone)]
    )


def body(
    latents,
    gain_first,
    kernel_first,
    gain_second,
    kernel_second,
    shortcut,
    gain_third,
    kernel_third,
):
    frames, rows, width, channels = latents.shape
    shape = jax.ShapeDtypeStruct
    shape = jax.ShapeDtypeStruct
    odd = lax.axis_index("rows") % 2
    near = lax.dynamic_slice_in_dim(latents, (rows - HALO) * (1 - odd), HALO, 1)
    far = lax.dynamic_slice_in_dim(latents, (rows - HALO) * odd, HALO, 1)
    near, far = swap(near, 0), swap(far, 1)

    wide1, wide2 = rows + 4, rows + 2
    pixels, pixels1, pixels2 = rows * width, wide1 * width, wide2 * width
    flops1, flops2, flops3 = (18 * n * 192 for n in (pixels1 * channels, pixels2 * 192, pixels * 192))
    dma = pltpu.SemaphoreType.DMA

    def work(tall, channels):
        return [pltpu.VMEM((tall * width, channels), BF16), pltpu.VMEM((tall * width, 128), F32)]

    rim = shape((frames, HALO, width, channels), BF16)
    held, gain_first, near, far = call(
        rim_kernel,
        (shape(latents.shape, BF16), shape((channels,), F32), rim, rim),
        [dma((3,))],
        1 << 34,
        (latents, gain_first),
        hbm=(0, 1),
    )
    far, near = swap(far, 1), swap(near, 0)
    inner_rows = rows - 2
    inner_pixels = inner_rows * width
    across = jnp.swapaxes(kernel_first, 3, 4)
    (active,) = call(
        active_kernel, (shape(latents.shape, BF16),), work(rows, channels), 1 << 20, (held, gain_first)
    )
    (inner,) = call(
        inner_kernel,
        (shape((2, inner_rows * 3 // 2, width, 128), BF16),),
        [pltpu.VMEM((2, inner_pixels, 192), F32)],
        2 * flops1,
        (active, across),
    )
    inner = onward(inner)
    (late_inner,) = call(
        late_inner_own_kernel, (shape((inner_pixels, 192), F32),), [], flops1, (active, across)
    )
    edge_sums = shape((2 * HALO * width, 192), F32)
    edge_work = [pltpu.VMEM(edge_sums.shape, F32), pltpu.VMEM((2 * HALO, width, channels), BF16)]
    edge_work += work(2 * HALO, channels)
    ends = shape((2, HALO + 2, width, channels), BF16)
    packed1 = shape((HALO * 3, width, 128), BF16)
    partial, late = call(
        late_edge_kernel,
        (packed1, ends),
        edge_work,
        flops1 // 2,
        (near, far, gain_first, active, across),
        after=(late_inner,),
    )
    late_edges = onward(partial)
    partial, early = call(
        early_edge_kernel,
        (packed1, ends),
        edge_work,
        flops1,
        (near, far, gain_first, active, across, late),
        after=(partial,),
    )
    early_edges = onward(partial)
    (late_rest,) = call(
        late_edge_own_kernel, (edge_sums,), [], flops1, (early, late, across), after=(kernel_second,)
    )
    second_work = [pltpu.VMEM((pixels1, 192), BF16)] + work(wide1, 192)
    packed2 = shape((wide2 * 3 // 2, width, 128), BF16)
    field = shape((3, wide1, width, 256), BF16)
    (early_own,) = call(
        early_own_kernel,
        (shape((pixels1, 192), F32),),
        [pltpu.VMEM((wide1 + 2, width, channels), BF16)],
        1 << 20,
        (active, early, across),
        after=(late_rest,),
    )
    partial, late = call(
        late_second_kernel,
        (packed2, field),
        second_work,
        flops2,
        (late_inner, late_rest, inner, late_edges, gain_second, kernel_second),
        after=(early_own,),
    )
    before_late = onward(partial)
    partial, early = call(
        early_second_kernel,
        (packed2, field),
        second_work,
        2 * flops2,
        (early_own, inner, early_edges, gain_second, kernel_second, late),
    )
    before_early = onward(partial)
    (own,) = call(
        second_own_kernel,
        (shape((2, pixels2, 192), F32),),
        [],
        3 * flops2,
        (early, late, kernel_second, held, near, far, shortcut.T),
    )
    (mixed,) = call(
        weights_kernel, (shape((3, 4, 768, 192), BF16),), [], 1 << 24, (kernel_third,), after=(own,)
    )
    third_work = [pltpu.VMEM((pixels2, 192), BF16)] + work(wide2, 192)
    block = shape((rows, width, 192), BF16)
    late_out, late = call(
        late_third_kernel,
        (block, packed2),
        third_work,
        1 << 24,
        (own, before_late, gain_third),
    )
    before_late = onward(late)
    (late_own,) = call(
        third_late_own_kernel,
        (shape((4, pixels, 192), F32),),
        [pltpu.VMEM((3, wide2, width, 256), BF16)],
        flops3,
        (late, mixed),
    )
    early_out, early = call(
        early_third_kernel,
        (block, packed2),
        third_work,
        1 << 24,
        (own, before_early, gain_third),
        after=(late_own,),
    )
    before_early = onward_open(early)
    own, block_out = call(
        third_own_kernel,
        (shape((2, 4, pixels, 192), F32), shape((2, rows, width, 192), BF16)),
        [pltpu.VMEM((3, wide2, width, 256), BF16), dma((2,))],
        2 * flops3,
        (early, late_own, mixed, early_out, late_out),
        out_hbm=(1,),
    )
    last_work = [
        pltpu.VMEM((3, wide2, width, 256), BF16),
        pltpu.VMEM((2, rows, 2, 2 * width, 128), F32),
        pltpu.VMEM((2, rows, 2 * width, 192), BF16),
        dma((2, rows // 2)),
    ]
    fine = shape((2, rows, 2, 2 * width, 192), BF16)
    decoded, rest = call(
        late_last_kernel,
        (fine, shape((4, pixels, 192), F32)),
        last_work,
        2 * flops3,
        (before_late, mixed, own),
        out_hbm=(0,),
    )
    (decoded,) = call(
        early_last_kernel,
        (fine,),
        last_work,
        flops3,
        (before_early, mixed, rest, decoded),
        hbm=(3,),
        out_hbm=(0,),
        aliases={3: 0},
    )
    decoded = decoded.reshape(2, 2 * rows, 2 * width, 192)
    return (block_out, decoded)


def solution(mesh):
    return jax.shard_map(
        body,
        mesh=mesh,
        in_specs=(P("tm", "rows", None, None), P(), P(), P(), P(), P(), P(), P()),
        out_specs=(P("tm", "rows", None, None), P("tm", "rows", None, None)),
        check_vma=False,
    )
```

```python
import jax
import jax.numpy as jnp
from jax import lax
from jax.experimental import pallas as pl
from jax.experimental.pallas import tpu as pltpu
from jax.sharding import PartitionSpec as P

F32 = jnp.float32
BF16 = jnp.bfloat16
HALO = 3
LIMIT = 24


def dot(a, b):
    return jnp.dot(a, b, preferred_element_type=F32)


def dot_t(a, b):
    return lax.dot_general(a, b, (((1,), (1,)), ((), ())), preferred_element_type=F32)


def spans(channels):
    return [(at, min(128, channels - at)) for at in range(0, channels, 128)]


def scales(squares, channels):
    total = dot(squares, jnp.ones((channels, 128), BF16))
    return lax.rsqrt(total * (1.0 / channels) + 1e-06)


def activated(v, scale, gain):
    u = v * scale * gain
    return u * (0.5 + 0.5 * jnp.tanh(0.5 * u))


def column_masks(width, channels):
    column = lax.broadcasted_iota(jnp.int32, (width, channels), 0)
    return column == 0, column == width - 1


def beside(v, masks):
    width = v.shape[0]
    left = jnp.where(masks[0], 0.0, pltpu.roll(v, 1, 0))
    right = jnp.where(masks[1], 0.0, pltpu.roll(v, width - 1, 0))
    return left, right


def call(kernel, out_shape, scratch, flops, args, hbm=(), out_hbm=(), aliases=None, after=()):
    vmem = pl.BlockSpec(memory_space=pltpu.VMEM)
    far = pl.BlockSpec(memory_space=pltpu.HBM)
    args = [pltpu.with_memory_space_constraint(x, pltpu.HBM) if i in hbm else x for i, x in enumerate(args)]

    count = len(args)

    def placed(*refs):
        place = [f(axis) for f in (lax.axis_index, lax.axis_size) for axis in ("tm", "rows")]
        kernel(place, *refs[:count], *refs[count + len(after) :])

    return pl.pallas_call(
        placed,
        out_shape=out_shape,
        in_specs=[far if i in hbm else vmem for i in range(count)] + [pl.BlockSpec(memory_space=pl.ANY)] * len(after),
        out_specs=tuple(far if i in out_hbm else vmem for i in range(len(out_shape))),
        scratch_shapes=scratch,
        input_output_aliases=aliases or {},
        compiler_params=pltpu.CompilerParams(vmem_limit_bytes=LIMIT << 20),
        cost_estimate=pl.CostEstimate(flops=flops, bytes_accessed=4 << 20, transcendentals=0),
    )(*args, *after)


def pack_rows(ref, rows, get):
    for row in range(0, rows, 2):
        upper, lower = get(row), get(row + 1)
        ref[row] = upper[:, 0:128].astype(BF16)
        ref[row + 1] = lower[:, 0:128].astype(BF16)
        ref[rows + row // 2] = jnp.concatenate([upper[:, 128:192], lower[:, 128:192]], axis=1).astype(BF16)


def unpack_row(ref, row):
    rows = ref.shape[0] * 2 // 3
    rest = ref[rows + row // 2].astype(F32)
    side = 64 * (row % 2)
    return jnp.concatenate([ref[row].astype(F32), rest[:, side : side + 64]], axis=1)


def fill_field(field, rows, first, rest):
    width = field.shape[2]
    masks = column_masks(width, 128)
    for row in range(rows):
        for at, part in ((0, first(row)), (128, rest(row))):
            left, right = beside(part, masks)
            for shift, value in enumerate((left, part, right)):
                field[shift, row, :, at : at + 128] = value.astype(BF16)


def packed_parts(ref, follows=None):
    rows = ref.shape[0] * 2 // 3

    def guard(value):
        value = value.astype(F32)
        return value if follows is None else jnp.where(follows, value, 0.0)

    def first(row):
        return guard(ref[row])

    def rest(row):
        at = rows + row // 2
        if row % 2 == 0:
            return guard(ref[at])
        upper = ref[at].astype(F32)[:, 64:128]
        lower = jnp.zeros_like(upper) if row == rows - 1 else ref[at + 1].astype(F32)[:, 0:64]
        return guard(jnp.concatenate([upper, lower], axis=1))

    return rows, first, rest


def row_parts(rows, get):
    made = {}

    def row_of(row):
        if row not in made:
            made[row] = get(row)
        return made[row]

    def rest(row):
        upper = row_of(row)[:, 128:192]
        lower = row_of(row + 1)[:, 128:192] if row < rows - 1 else jnp.zeros_like(upper)
        return jnp.concatenate([upper, lower], axis=1)

    return rows, lambda row: row_of(row)[:, 0:128], rest


def two_rows(field, shift, row, rows):
    pixels = rows * field.shape[2]
    return [
        field[shift, row : row + rows].reshape(pixels, 256),
        field[shift, row + 1 : row + 1 + rows, :, 0:128].reshape(pixels, 128),
    ]


def two_rows_weights(upper, lower):
    return [upper, lower[128:192], lower[0:128]]


def convolve_field(kernel, terms, rows):
    lanes, weights = [], []
    for field, a in terms:
        for e in range(3):
            lanes += two_rows(field, e, 0, rows)
            weights += two_rows_weights(kernel[a, 0, e], kernel[a, 1, e])
            lanes.append(field[e, 2 : 2 + rows].reshape(rows * field.shape[2], 256))
            weights += [kernel[a, 2, e], jnp.zeros((64, 192), BF16)]
    return dot(jnp.concatenate(lanes, axis=1), jnp.concatenate(weights, axis=0))


def convolve(acc, product, kernel, terms, rows, width):
    masks = column_masks(width, 192)
    fields = [window(b) for window, a in terms for b in range(3)]
    if product is dot_t:
        fields = [jnp.concatenate(fields, axis=1)]
    for e in range(3):
        taps = [kernel[a, b, e] for window, a in terms for b in range(3)]
        if product is dot_t:
            taps = [jnp.concatenate(taps, axis=1)]
        total = None
        for field, tap in zip(fields, taps):
            term = product(field, tap)
            total = term if total is None else total + term
        for row in range(rows):
            part = slice(row * width, (row + 1) * width)
            moved = total[part]
            if e == 0:
                acc[part] = jnp.where(masks[0], 0.0, pltpu.roll(moved, 1, 0))
            elif e == 1:
                acc[part] += moved
            else:
                acc[part] += jnp.where(masks[1], 0.0, pltpu.roll(moved, width - 1, 0))


def windows(ref, rows):
    return lambda b: ref[b : b + rows].reshape(rows * ref.shape[1], ref.shape[2])


OWN = (((0, 2),), ((0, 1), (1, 2)))


def activate_rows(fields, gain, squares, scale, put):
    rows, width, channels = fields[0].shape
    pixels = rows * width
    for i, ref in enumerate(fields):
        v = ref[...].astype(F32)
        squares[i * pixels : (i + 1) * pixels] = (v * v).astype(BF16).reshape(pixels, channels)
    every = len(fields) * pixels
    scale[0:every] = scales(squares[0:every], channels)
    for i, ref in enumerate(fields):
        for row in range(rows):
            part = slice(i * pixels + row * width, i * pixels + (row + 1) * width)
            for at, lanes in spans(channels):
                v = activated(
                    ref[row, :, at : at + lanes].astype(F32),
                    scale[part],
                    gain[at : at + lanes].reshape(1, lanes),
                )
                put(i, row, slice(at, at + lanes), v.astype(BF16))


def rim_kernel(place, latents, gain, held, held_gain, near, far, sems):
    rows = held.shape[1]
    copies = [pltpu.make_async_copy(latents.at[frame], held.at[frame], sems.at[frame]) for frame in range(2)]
    copies.append(pltpu.make_async_copy(gain, held_gain, sems.at[2]))
    for copy in copies:
        copy.start()
    odd = place[1] % 2
    for frame in range(2):
        copies[frame].wait()
        far[frame] = held[frame, pl.ds((rows - HALO) * odd, HALO)]
        near[frame] = held[frame, pl.ds((rows - HALO) * (1 - odd), HALO)]
    copies[2].wait()


def active_kernel(place, held, gain, active, squares, scale):
    def put(frame, row, lanes, value):
        active[frame, row, :, lanes] = value

    for frame in range(held.shape[0]):
        activate_rows(
            [held.at[frame]], gain, squares, scale, lambda _, *args, frame=frame: put(frame, *args)
        )


def inner_kernel(place, active, weights, packed, sums):
    frames, rows, width, channels = active.shape
    count = rows - 2
    for out, taps in ((1, ((1, 0),)), (0, ((0, 0), (1, 1)))):
        terms = [(windows(active.at[frame], count), a) for frame, a in taps]
        convolve(sums.at[out], dot_t, weights, terms, count, width)
        pack_rows(packed.at[out], count, lambda row: sums[out, row * width : (row + 1) * width])


def late_inner_own_kernel(place, active, weights, own):
    count, width = active.shape[1] - 2, active.shape[2]
    terms = [(windows(active.at[frame], count), a) for frame, a in OWN[1]]
    convolve(own, dot_t, weights, terms, count, width)


def fill_edges(place, near, far, frame, gain, active, edges, raw, squares, scale):
    odd = place[1] % 2 == 1
    inner = jnp.logical_and(place[1] > 0, place[1] < place[3] - 1)
    rows = active.shape[1]
    for row in range(HALO):
        chip = near[frame, row]
        next_chip = jnp.where(inner, far[frame, row], jnp.zeros_like(chip))
        raw[row] = jnp.where(odd, chip, next_chip)
        raw[HALO + row] = jnp.where(odd, next_chip, chip)

    def put(_, row, lanes, value):
        side, at = divmod(row, HALO)
        edges[side, at + 2 * side, :, lanes] = value

    activate_rows([raw], gain, squares, scale, put)
    edges[0, HALO : HALO + 2] = active[frame, 0:2]
    edges[1, 0:2] = active[frame, rows - 2 : rows]


def edge_windows(edges):
    width, channels = edges.shape[2], edges.shape[3]
    return lambda b: edges[:, b : b + HALO].reshape(2 * HALO * width, channels)


def pack_edges(partial, acc, width):
    pack_rows(partial, 2 * HALO, lambda row: acc[row * width : (row + 1) * width])


def late_edge_kernel(place, near, far, gain, active, weights, partial, edges, acc, raw, squares, scale):
    fill_edges(place, near, far, 1, gain, active, edges, raw, squares, scale)
    width = active.shape[2]
    convolve(acc, dot_t, weights, [(edge_windows(edges), 0)], 2 * HALO, width)
    pack_edges(partial, acc, width)


def early_edge_kernel(
    place, near, far, gain, active, weights, late, partial, edges, acc, raw, squares, scale
):
    fill_edges(place, near, far, 0, gain, active, edges, raw, squares, scale)
    width = active.shape[2]
    convolve(acc, dot_t, weights, [(edge_windows(edges), 0), (edge_windows(late), 1)], 2 * HALO, width)
    pack_edges(partial, acc, width)


def late_edge_own_kernel(place, early, late, weights, own):
    terms = [(edge_windows((early, late)[frame]), a) for frame, a in OWN[1]]
    convolve(own, dot_t, weights, terms, 2 * HALO, early.shape[2])


def early_own_kernel(place, active, early, weights, own, tall):
    rows, width = active.shape[1], active.shape[2]
    tall[0:HALO] = early[0, 0:HALO]
    tall[HALO : HALO + rows] = active[0]
    tall[HALO + rows :] = early[1, 2:]
    (frame, a), = OWN[0]
    convolve(own, dot_t, weights, [(windows(tall, rows + 4), a)], rows + 4, width)


def finish(place, own, before, gain, raw, squares, scale, keep):
    before, tall, width = before
    start = place[1] * 8 - (tall - 8) // 2
    follows = place[0] > 0
    for row in range(tall):
        part = slice(row * width, (row + 1) * width)
        earlier = jnp.where(follows, before(row), 0.0)
        total = (own(row) + earlier).astype(BF16)
        raw[part] = total
        keep(row, total)
        total = total.astype(F32)
        squares[part] = (total * total).astype(BF16)
    scale[...] = scales(squares[...], 192)

    def get(row):
        part = slice(row * width, (row + 1) * width)
        inside = jnp.logical_and(start + row >= 0, start + row < place[3] * 8)
        lanes = []
        for at, count in spans(192):
            v = activated(
                raw[part, at : at + count].astype(F32), scale[part, 0:count], gain[at : at + count].reshape(1, count)
            )
            if not (tall - 8) // 2 <= row < (tall + 8) // 2:
                v = jnp.where(inside, v, 0.0)
            lanes.append(v)
        return jnp.concatenate(lanes, axis=1)

    return get


def second(place, own, before, gain, kernel, terms, partial, field, raw, squares, scale):
    rows = field.shape[1]
    width, wide = field.shape[2], rows - 2
    get = finish(place, own, before, gain, raw, squares, scale, lambda row, total: None)
    fill_field(field, *row_parts(rows, get))
    total = convolve_field(kernel, terms, wide)
    pack_rows(partial, wide, lambda row: total[row * width : (row + 1) * width])


def joined(inner, edges):
    count = inner.shape[0] * 2 // 3

    def get(row):
        if HALO <= row < HALO + count:
            return unpack_row(inner, row - HALO)
        return unpack_row(edges, row if row < HALO else row - count)

    return get, count + 2 * HALO, inner.shape[1]


def whole(packed):
    return lambda row: unpack_row(packed, row), packed.shape[0] * 2 // 3, packed.shape[1]


def joined_own(inner, edges, width):
    count = inner.shape[0] // width

    def get(row):
        ref, at = (inner, row - HALO) if HALO <= row < HALO + count else (edges, row if row < HALO else row - count)
        return ref[at * width : (at + 1) * width]

    return get


def rows_of(own, width):
    return lambda row: own[row * width : (row + 1) * width]


def late_second_kernel(
    place, own_inner, own_edges, inner, edges, gain, kernel, partial, field, raw, squares, scale
):
    before = joined(inner.at[1], edges)
    own = joined_own(own_inner, own_edges, field.shape[2])
    second(place, own, before, gain, kernel, [(field, 0)], partial, field, raw, squares, scale)


def early_second_kernel(
    place, own, inner, edges, gain, kernel, late, partial, field, raw, squares, scale
):
    before = joined(inner.at[0], edges)
    own = rows_of(own, field.shape[2])
    second(place, own, before, gain, kernel, [(field, 0), (late, 1)], partial, field, raw, squares, scale)


def second_own_kernel(place, early, late, kernel, latents, near, far, shortcut, own):
    wide, width = early.shape[1] - 2, early.shape[2]
    pixels = wide * width
    rows, channels = latents.shape[1], latents.shape[3]
    odd = place[1] % 2
    inner = wide - 1
    fields = (early, late)
    for out in (1, 0):
        own[out] = convolve_field(kernel, [(fields[frame], a) for frame, a in OWN[out]], wide)
        body = latents[out].reshape(rows * width, channels)
        own[out, width : pixels - width] += dot_t(body, shortcut[...])
        other = dot_t(near[out, jnp.where(odd == 1, HALO - 1, 0)], shortcut[...])
        own[out, pl.ds(jnp.where(odd == 1, 0, inner * width), width)] += other
        other = dot_t(far[out, jnp.where(odd == 1, 0, HALO - 1)], shortcut[...])
        own[out, pl.ds(jnp.where(odd == 1, inner * width, 0), width)] += other


def third(place, own, before, gain, block, packed, raw, squares, scale):
    tall = packed.shape[0] * 2 // 3

    def keep(row, total):
        if 0 < row < tall - 1:
            block[row - 1] = total

    own = rows_of(own, packed.shape[1])
    pack_rows(packed, tall, finish(place, own, whole(before), gain, raw, squares, scale, keep))


def late_third_kernel(place, own, before, gain, block, packed, raw, squares, scale):
    third(place, own.at[1], before, gain, block, packed, raw, squares, scale)


def early_third_kernel(place, own, before, gain, block, packed, raw, squares, scale):
    third(place, own.at[0], before, gain, block, packed, raw, squares, scale)


def weights_kernel(place, kernel, out):
    def halves(taps, parity):
        if parity == 0:
            return taps[0], taps[1] + taps[2]
        return taps[0] + taps[1], taps[2]

    for a in range(3):
        for i in range(2):
            rows = [halves([kernel[a, b, e] for b in range(3)], i) for e in range(3)]
            for j in range(2):
                upper = halves([rows[e][0] for e in range(3)], j)
                lower = halves([rows[e][1] for e in range(3)], j)
                for column in range(2):
                    at = 384 * column
                    for part in two_rows_weights(upper[column], lower[column]):
                        out[a, 2 * i + j, at : at + part.shape[0]] = part
                        at += part.shape[0]


def phase(terms, kernel, i, j, rows):
    lanes, weights = [], []
    for field, a in terms:
        for shift in (j, j + 1):
            lanes += two_rows(field, shift, i, rows)
        weights.append(kernel[a, 2 * i + j])
    return dot(jnp.concatenate(lanes, axis=1), jnp.concatenate(weights, axis=0))


def third_late_own_kernel(place, packed, kernel, own, field):
    rows = packed.shape[0] * 2 // 3 - 2
    fill_field(field, *packed_parts(packed))
    for i in range(2):
        for j in range(2):
            own[2 * i + j] = phase([(field, 2)], kernel, i, j, rows)


def third_own_kernel(place, packed, late, kernel, early_out, late_out, own, block_out, field, sems):
    copies = [
        pltpu.make_async_copy(block, block_out.at[frame], sems.at[frame])
        for frame, block in enumerate((early_out, late_out))
    ]
    for copy in copies:
        copy.start()
    fill_field(field, *packed_parts(packed))
    rows = early_out.shape[0]
    for i in range(2):
        for j in range(2):
            own[1, 2 * i + j] = late[2 * i + j] + phase([(field, 1)], kernel, i, j, rows)
            own[0, 2 * i + j] = phase([(field, 2)], kernel, i, j, rows)
    for copy in copies:
        copy.wait()


def weave(total, j, rows, width, woven):
    for row in range(rows):
        value = total[row * width : (row + 1) * width]
        woven[row, 0, pl.ds(j, width, stride=2)] = value[:, 0:128]
        woven[row, 1, pl.ds(j, width, stride=2), 0:64] = value[:, 128:192]


def write_out(own, field, kernel, a, rows, width, woven, fine, out, sems):
    copies = []
    for i in range(2):
        for j in range(2):
            total = own[2 * i + j] + phase([(field, a)], kernel, i, j, rows)
            weave(total, j, rows, width, woven.at[i])
        for row in range(rows):
            fine[i, row, :, 0:128] = woven[i, row, 0].astype(BF16)
            fine[i, row, :, 128:192] = woven[i, row, 1, :, 0:64].astype(BF16)
            if row % 2:
                part = slice(row - 1, row + 1)
                copies.append(pltpu.make_async_copy(fine.at[i, part], out.at[part, i], sems.at[i, row // 2]))
                copies[-1].start()
    return copies


def late_last_kernel(place, packed, kernel, own, decoded, rest, field, woven, fine, sems):
    rows, width = packed.shape[0] * 2 // 3 - 2, packed.shape[1]
    fill_field(field, *packed_parts(packed, place[0] > 0))
    copies = write_out(own.at[1], field, kernel, 0, rows, width, woven, fine, decoded.at[1], sems)
    for i in range(2):
        for j in range(2):
            rest[2 * i + j] = own[0, 2 * i + j] + phase([(field, 1)], kernel, i, j, rows)
    for copy in copies:
        copy.wait()


def early_last_kernel(place, packed, kernel, rest, late, decoded, field, woven, fine, sems):
    rows, width = packed.shape[0] * 2 // 3 - 2, packed.shape[1]
    fill_field(field, *packed_parts(packed, place[0] > 0))
    for copy in write_out(rest, field, kernel, 0, rows, width, woven, fine, decoded.at[0], sems):
        copy.wait()


def onward_open(value):
    count = lax.axis_size("tm")
    return lax.ppermute(value, "tm", [(i, i + 1) for i in range(count - 1)])


def onward(value):
    count = lax.axis_size("tm")
    return lax.ppermute(value, "tm", [(i, (i + 1) % count) for i in range(count)])


def swap(value, offset):
    groups, slabs = lax.axis_size("tm"), lax.axis_size("rows")
    pairs = [(g * slabs + i, g * slabs + i + 1) for g in range(groups) for i in range(offset, slabs - 1, 2)]
    if offset:
        pairs += [(g * slabs + i, (g + 1) * slabs + i) for g in range(0, groups - 1, 2) for i in (0, slabs - 1)]
    alone = set(range(groups * slabs)) - {i for pair in pairs for i in pair}
    return lax.ppermute(
        value, ("tm", "rows"), pairs + [(b, a) for a, b in pairs] + [(i, i) for i in sorted(alone)]
    )


def body(
    latents,
    gain_first,
    kernel_first,
    gain_second,
    kernel_second,
    shortcut,
    gain_third,
    kernel_third,
):
    frames, rows, width, channels = latents.shape
    shape = jax.ShapeDtypeStruct
    shape = jax.ShapeDtypeStruct
    odd = lax.axis_index("rows") % 2
    near = lax.dynamic_slice_in_dim(latents, (rows - HALO) * (1 - odd), HALO, 1)
    far = lax.dynamic_slice_in_dim(latents, (rows - HALO) * odd, HALO, 1)
    near, far = swap(near, 0), swap(far, 1)

    wide1, wide2 = rows + 4, rows + 2
    pixels, pixels1, pixels2 = rows * width, wide1 * width, wide2 * width
    flops1, flops2, flops3 = (18 * n * 192 for n in (pixels1 * channels, pixels2 * 192, pixels * 192))
    dma = pltpu.SemaphoreType.DMA

    def work(tall, channels):
        return [pltpu.VMEM((tall * width, channels), BF16), pltpu.VMEM((tall * width, 128), F32)]

    rim = shape((frames, HALO, width, channels), BF16)
    held, gain_first, near, far = call(
        rim_kernel,
        (shape(latents.shape, BF16), shape((channels,), F32), rim, rim),
        [dma((3,))],
        1 << 34,
        (latents, gain_first),
        hbm=(0, 1),
    )
    far, near = swap(far, 1), swap(near, 0)
    inner_rows = rows - 2
    inner_pixels = inner_rows * width
    across = jnp.swapaxes(kernel_first, 3, 4)
    (active,) = call(
        active_kernel, (shape(latents.shape, BF16),), work(rows, channels), 1 << 20, (held, gain_first)
    )
    (inner,) = call(
        inner_kernel,
        (shape((2, inner_rows * 3 // 2, width, 128), BF16),),
        [pltpu.VMEM((2, inner_pixels, 192), F32)],
        2 * flops1,
        (active, across),
    )
    inner = onward(inner)
    (late_inner,) = call(
        late_inner_own_kernel, (shape((inner_pixels, 192), F32),), [], flops1, (active, across)
    )
    edge_sums = shape((2 * HALO * width, 192), F32)
    edge_work = [pltpu.VMEM(edge_sums.shape, F32), pltpu.VMEM((2 * HALO, width, channels), BF16)]
    edge_work += work(2 * HALO, channels)
    ends = shape((2, HALO + 2, width, channels), BF16)
    packed1 = shape((HALO * 3, width, 128), BF16)
    partial, late = call(
        late_edge_kernel,
        (packed1, ends),
        edge_work,
        flops1 // 2,
        (near, far, gain_first, active, across),
        after=(late_inner,),
    )
    late_edges = onward(partial)
    partial, early = call(
        early_edge_kernel,
        (packed1, ends),
        edge_work,
        flops1,
        (near, far, gain_first, active, across, late),
        after=(partial,),
    )
    early_edges = onward(partial)
    (late_rest,) = call(
        late_edge_own_kernel, (edge_sums,), [], flops1, (early, late, across), after=(kernel_second,)
    )
    second_work = [pltpu.VMEM((pixels1, 192), BF16)] + work(wide1, 192)
    packed2 = shape((wide2 * 3 // 2, width, 128), BF16)
    field = shape((3, wide1, width, 256), BF16)
    (early_own,) = call(
        early_own_kernel,
        (shape((pixels1, 192), F32),),
        [pltpu.VMEM((wide1 + 2, width, channels), BF16)],
        1 << 20,
        (active, early, across),
        after=(late_rest,),
    )
    partial, late = call(
        late_second_kernel,
        (packed2, field),
        second_work,
        flops2,
        (late_inner, late_rest, inner, late_edges, gain_second, kernel_second),
        after=(early_own,),
    )
    before_late = onward(partial)
    partial, early = call(
        early_second_kernel,
        (packed2, field),
        second_work,
        2 * flops2,
        (early_own, inner, early_edges, gain_second, kernel_second, late),
    )
    before_early = onward(partial)
    (own,) = call(
        second_own_kernel,
        (shape((2, pixels2, 192), F32),),
        [],
        3 * flops2,
        (early, late, kernel_second, held, near, far, shortcut.T),
    )
    (mixed,) = call(
        weights_kernel, (shape((3, 4, 768, 192), BF16),), [], 1 << 24, (kernel_third,), after=(own,)
    )
    third_work = [pltpu.VMEM((pixels2, 192), BF16)] + work(wide2, 192)
    block = shape((rows, width, 192), BF16)
    late_out, late = call(
        late_third_kernel,
        (block, packed2),
        third_work,
        1 << 24,
        (own, before_late, gain_third),
    )
    before_late = onward_open(late)
    (late_own,) = call(
        third_late_own_kernel,
        (shape((4, pixels, 192), F32),),
        [pltpu.VMEM((3, wide2, width, 256), BF16)],
        flops3,
        (late, mixed),
    )
    early_out, early = call(
        early_third_kernel,
        (block, packed2),
        third_work,
        1 << 24,
        (own, before_early, gain_third),
        after=(late_own,),
    )
    before_early = onward_open(early)
    own, block_out = call(
        third_own_kernel,
        (shape((2, 4, pixels, 192), F32), shape((2, rows, width, 192), BF16)),
        [pltpu.VMEM((3, wide2, width, 256), BF16), dma((2,))],
        2 * flops3,
        (early, late_own, mixed, early_out, late_out),
        out_hbm=(1,),
    )
    last_work = [
        pltpu.VMEM((3, wide2, width, 256), BF16),
        pltpu.VMEM((2, rows, 2, 2 * width, 128), F32),
        pltpu.VMEM((2, rows, 2 * width, 192), BF16),
        dma((2, rows // 2)),
    ]
    fine = shape((2, rows, 2, 2 * width, 192), BF16)
    decoded, rest = call(
        late_last_kernel,
        (fine, shape((4, pixels, 192), F32)),
        last_work,
        2 * flops3,
        (before_late, mixed, own),
        out_hbm=(0,),
    )
    (decoded,) = call(
        early_last_kernel,
        (fine,),
        last_work,
        flops3,
        (before_early, mixed, rest, decoded),
        hbm=(3,),
        out_hbm=(0,),
        aliases={3: 0},
    )
    decoded = decoded.reshape(2, 2 * rows, 2 * width, 192)
    return (block_out, decoded)


def solution(mesh):
    return jax.shard_map(
        body,
        mesh=mesh,
        in_specs=(P("tm", "rows", None, None), P(), P(), P(), P(), P(), P(), P()),
        out_specs=(P("tm", "rows", None, None), P("tm", "rows", None, None)),
        check_vma=False,
    )
```
